32 devices in a mesh: blk: 8 (over z, y), head: 4 (over x, core).
Axes of the slice: x: 2, y: 2, z: 4, core: 2. Of those that a mesh axis runs over, the one named last changes fastest.
Arguments:
- layer_entry_vectors: bfloat16 [64, 16, 2048], P('blk', None, 'head'), may hold values from -6 to 6
- guessed_lookup_vectors: bfloat16 [64, 16, 2048], P('blk', None, 'head'), may hold values from -3 to 3
- guessed_content_vectors: bfloat16 [64, 16, 2048], P('blk', None, 'head'), may hold values from -6 to 6
- gating_query: bfloat16 [64, 16, 2048], P('blk', 'head'), may hold values from -6 to 6
- lane_memory_store: float32 [4, 1024, 2048], P('head', 'blk'), may hold values from -3 to 3
- prior_step_store: float32 [4, 1024, 32], P('head', 'blk'), may hold values from -6 to 6
- fading_blend_ratio: float32 [2048], P('head'), may hold values from 0 to 1
- learning_speed_blend: float32 [2048], P('head'), may hold values from 0 to 1
- fading_left_factor: bfloat16 [2048, 96], P('head'), may hold values from -0.125 to 0.125
- fading_right_factor: bfloat16 [96, 2048], P(None, 'head'), may hold values from -0.625 to 0.625
- fading_offset: float32 [2048], P('head'), may hold values from -6 to 1
- learning_speed_left: bfloat16 [2048, 96], P('head'), may hold values from -0.125 to 0.125
- learning_speed_right: bfloat16 [96, 2048], P(None, 'head'), may hold values from -0.625 to 0.625
- learning_speed_offset: float32 [2048], P('head'), may hold values from -2 to 2
- erasing_lookup_factor: float32 [2048], P('head'), may hold values from 0.1 to 1.9
- written_lookup_factor: float32 [2048], P('head'), may hold values from 0 to 1
- present_reward_factors: float32 [2048], P('head'), may hold values from -3 to 3
- lane_standard_factor: float32 [2048], P('head'), may hold values from 0.1 to 1.9
- lane_standard_offset: float32 [2048], P('head'), may hold values from -2 to 2
- caller_memory_directory: int32 [64, 32, 2], P(None, 'head'), may hold values from 0 to 1023, as said below
- kept_target_place: int32 [64, 32, 2], P(None, 'head'), may hold values from 0 to 1023, as said below
- caller_sequence: int32 [64], replicated, may hold values from 0 to 63, as said below
- approved_guesses: int32 [64], replicated, may hold values from 0 to 16
Outputs:
- temporal_blend_result: bfloat16 [64, 16, 2048], P('blk', None, 'head')
- new_states: float32 [4, 1024, 2048], P('head', 'blk')
- new_edges: float32 [4, 1024, 32], P('head', 'blk')
The draws below stay inside these ranges and needn't reach their ends.
Inputs may be any that keep to these rules, and one draw needn't show every extreme that they name: `caller_memory_directory`: every entry names a slot of the pool of head group h // 8; all entries of one head group are distinct and cover its 1024 slots. For the positions p of one blk index, taken through q = caller_sequence[p], exactly 16 of the slots of each head group lie on each blk index (slot // 128). `kept_target_place`: same rules as the page table: every slot of a head group is written exactly once, and one blk index's positions write exactly 16 slots of each head group on each blk index. `caller_sequence`: A permutation of the 64 requests.
All inputs are finite; a program needn't handle non-finite values.
Results may differ from the reference program's by a relative error of at most 0.006.
Values may be sent and summed in bfloat16 or wider, within the bound.
No kernel may reach another device: no remote copies, remote signals or barrier semaphores. Data moves between devices by JAX's collectives and lax.ppermute only.
A program may use at most 64 MiB of HBM per device.

```python
import jax
import jax.numpy as jnp
from jax import lax

EMBEDDING_SIZE = 2048
ATTENTION_LANES = 32
LANE_SIZE = 64
LR_W = 96
LR_A = 96
PROPOSED_STEPS = 16
SLOT_ROWS = 32
HEAD_DEV = 8
HALVES = 2
SLOT_DEV = 128
PEER_SLOTS = 16
CALLER_TOTAL = 64
SLOTS = 1024
GROUPS = 4
BLOCKS = 8
N_HEAD = 4


def shuffle_rows(row_key):
    return jax.random.permutation(row_key, SLOT_DEV).astype(jnp.int32)


def routed_slots(base_key, stream):
    stream_key = jax.random.fold_in(base_key, stream)
    source = jnp.arange(BLOCKS, dtype=jnp.int32)[:, None]
    columns = []
    for group_index in range(GROUPS):
        group_key = jax.random.fold_in(stream_key, group_index)
        spread = jax.vmap(shuffle_rows)(jax.random.split(jax.random.fold_in(group_key, 1), BLOCKS))
        within = jax.vmap(shuffle_rows)(jax.random.split(jax.random.fold_in(group_key, 2), BLOCKS))
        holder = (source + spread // PEER_SLOTS) % BLOCKS
        arrival = source * PEER_SLOTS + spread % PEER_SLOTS
        slot_ids = holder * SLOT_DEV + within[holder, arrival]
        columns.append(slot_ids.reshape(CALLER_TOTAL, HEAD_DEV, HALVES))
    return jnp.concatenate(columns, axis=1).astype(jnp.int32)


def serving(base_key):
    return jax.random.permutation(jax.random.fold_in(base_key, 5), CALLER_TOTAL).astype(jnp.int32)


def draw_caller_sequence(key, part):
    return serving(key)


def draw_caller_memory_directory(key, part):
    slot_table = routed_slots(key, 11)
    return jnp.zeros_like(slot_table).at[serving(key)].set(slot_table)


def draw_kept_target_place(key, part):
    slot_table = routed_slots(key, 13)
    return jnp.zeros_like(slot_table).at[serving(key)].set(slot_table)


def with_ends(entries, key, low, top_value):
    spot = [jax.random.randint(jax.random.fold_in(key, axis), (), 0, length) for axis, length in enumerate(entries.shape)]
    widest = entries.shape.index(max(entries.shape))
    neighbour = spot[:widest] + [(spot[widest] + 1) % entries.shape[widest]] + spot[widest + 1:]
    return entries.at[tuple(spot)].set(low).at[tuple(neighbour)].set(top_value)


def levels(key, dims, pieces, least, high):
    factor_of, own = 1.0, jax.random.fold_in(key, 6)
    for position, parts in pieces:
        draws = jnp.exp(jax.random.uniform(jax.random.fold_in(own, position), (parts,), jnp.float32, least / len(pieces), high / len(pieces)))
        factor_of = factor_of * jnp.repeat(draws, dims[position] // parts).reshape([-1 if axis == position else 1 for axis in range(len(dims))])
    return factor_of


def scatter_about(own_key, shape, scale, bound, cuts=(), held_as=jnp.bfloat16):
    entries = jax.random.normal(own_key, shape, jnp.float32) * scale
    if len(cuts) > 0:
        entries = levels(own_key, shape, cuts, -0.22, 0.18) * entries
    return jnp.clip(entries, min=-bound, max=bound).astype(held_as)


def setup_inputs(seed: int = 0) -> dict:
    splits = jax.random.split(jax.random.key(seed), 24)
    return {
        "layer_entry_vectors": scatter_about(splits[0], (CALLER_TOTAL, PROPOSED_STEPS, EMBEDDING_SIZE), 1.0, 6.0, ((0, 8), (2, 4))),
        "guessed_lookup_vectors": scatter_about(splits[1], (CALLER_TOTAL, PROPOSED_STEPS, EMBEDDING_SIZE), 0.5, 3.0, ((0, 8), (2, 4))),
        "guessed_content_vectors": scatter_about(splits[2], (CALLER_TOTAL, PROPOSED_STEPS, EMBEDDING_SIZE), 1.0, 6.0, ((0, 8), (2, 4))),
        "gating_query": scatter_about(splits[3], (CALLER_TOTAL, PROPOSED_STEPS, EMBEDDING_SIZE), 1.0, 6.0, ((0, 8), (1, 4))),
        "lane_memory_store": scatter_about(splits[4], (GROUPS, SLOTS, SLOT_ROWS * LANE_SIZE), 0.5, 3.0, ((0, 4), (1, 8)), jnp.float32),
        "prior_step_store": scatter_about(splits[5], (GROUPS, SLOTS, SLOT_ROWS), 1.0, 6.0, ((0, 4), (1, 8)), jnp.float32),
        "fading_blend_ratio": jnp.clip(1.0 * jax.random.uniform(splits[6], (EMBEDDING_SIZE,), jnp.float32) ** levels(splits[6], (EMBEDDING_SIZE,), ((0, 4),), -0.2, 0.2), 0.0, 1.0),
        "learning_speed_blend": jnp.clip(1.0 * jax.random.uniform(splits[7], (EMBEDDING_SIZE,), jnp.float32) ** levels(splits[7], (EMBEDDING_SIZE,), ((0, 4),), -0.2, 0.2), 0.0, 1.0),
        "fading_left_factor": scatter_about(splits[8], (EMBEDDING_SIZE, LR_W), EMBEDDING_SIZE ** -0.5, 0.125, ((0, 4),)),
        "fading_right_factor": scatter_about(splits[9], (LR_W, EMBEDDING_SIZE), LR_W ** -0.5, 0.625, ((1, 4),)),
        "fading_offset": jnp.clip(-6.0 + 7.0 * jax.random.uniform(splits[10], (EMBEDDING_SIZE,), jnp.float32) ** levels(splits[10], (EMBEDDING_SIZE,), ((0, 4),), -0.2, 0.2), -6.0, 1.0),
        "learning_speed_left": scatter_about(splits[11], (EMBEDDING_SIZE, LR_A), EMBEDDING_SIZE ** -0.5, 0.125, ((0, 4),)),
        "learning_speed_right": scatter_about(splits[12], (LR_A, EMBEDDING_SIZE), LR_A ** -0.5, 0.625, ((1, 4),)),
        "learning_speed_offset": jnp.clip(jax.random.uniform(splits[13], (EMBEDDING_SIZE,), jnp.float32, -2.0, 2.0) * levels(splits[13], (EMBEDDING_SIZE,), ((0, 4),), -0.4, 0.0), -2.0, 2.0),
        "erasing_lookup_factor": jnp.clip(1.0 + 0.18 * jax.random.normal(splits[14], (EMBEDDING_SIZE,), jnp.float32), 0.1, 1.9),
        "written_lookup_factor": jnp.clip(1.0 * jax.random.uniform(splits[15], (EMBEDDING_SIZE,), jnp.float32) ** levels(splits[15], (EMBEDDING_SIZE,), ((0, 4),), -0.2, 0.2), 0.0, 1.0),
        "present_reward_factors": scatter_about(splits[16], (EMBEDDING_SIZE,), 0.5, 3.0, ((0, 4),), jnp.float32),
        "lane_standard_factor": jnp.clip(1.0 + 0.18 * jax.random.normal(splits[17], (EMBEDDING_SIZE,), jnp.float32), 0.1, 1.9),
        "lane_standard_offset": scatter_about(splits[18], (EMBEDDING_SIZE,), 0.3, 2.0, ((0, 4),), jnp.float32),
        "caller_memory_directory": draw_caller_memory_directory(jax.random.fold_in(splits[23], 71), 0),
        "kept_target_place": draw_kept_target_place(jax.random.fold_in(splits[23], 71), 0),
        "caller_sequence": draw_caller_sequence(jax.random.fold_in(splits[23], 71), 0),
        "approved_guesses": with_ends(jax.random.randint(splits[22], (CALLER_TOTAL,), 0, PROPOSED_STEPS + 1), jax.random.fold_in(splits[22], 1), 0, PROPOSED_STEPS).astype(jnp.int32),
    }


EPSILON = 1e-05
NORM_EPSILON = 0.00064

def head_scan(packed, counts):
    start_state, forget, unit_key, in_rate, adjusted_lookup, content_lines, gating_query_lines = packed

    def advance(carried, per_step):
        carry_state, accepted_state = carried
        step_index, forget_t, unit_t, rate_t, key_t, value_t, recept_t = per_step
        projected = lax.optimization_barrier(jnp.sum(carry_state * unit_t[:, None, :], axis=-1))
        carry_state = carry_state * forget_t[:, None, :] - projected[:, :, None] * (rate_t * unit_t)[:, None, :] + value_t[:, :, None] * key_t[:, None, :]
        output = lax.optimization_barrier(jnp.sum(carry_state * recept_t[:, None, :], axis=-1))
        accepted_state = jnp.where((counts == step_index + 1)[:, None, None], carry_state, accepted_state)
        return ((carry_state, accepted_state), output)
    step_ids = jnp.arange(PROPOSED_STEPS, dtype=jnp.int32)
    carried, outputs = lax.scan(advance, (start_state, start_state), (step_ids, forget, unit_key, in_rate, adjusted_lookup, content_lines, gating_query_lines))
    return (outputs, carried[1])

def reference(layer_entry_vectors, guessed_lookup_vectors, guessed_content_vectors, gating_query, lane_memory_store, prior_step_store, fading_blend_ratio, learning_speed_blend, fading_left_factor, fading_right_factor, fading_offset, learning_speed_left, learning_speed_right, learning_speed_offset, erasing_lookup_factor, written_lookup_factor, present_reward_factors, lane_standard_factor, lane_standard_offset, caller_memory_directory, kept_target_place, caller_sequence, approved_guesses):
    heads_on_device = ATTENTION_LANES // N_HEAD
    halves = LANE_SIZE // SLOT_ROWS
    group_ids = (jnp.arange(ATTENTION_LANES, dtype=jnp.int32) // heads_on_device)[None, :, None]
    counts = approved_guesses[caller_sequence]
    wanted = caller_memory_directory[caller_sequence]
    targets = kept_target_place[caller_sequence]
    start_states = lane_memory_store[group_ids, wanted].reshape(CALLER_TOTAL, ATTENTION_LANES, LANE_SIZE, LANE_SIZE)
    edge_rows = prior_step_store[group_ids, wanted].reshape(CALLER_TOTAL, EMBEDDING_SIZE)
    current = layer_entry_vectors.astype(jnp.float32)
    previous = jnp.concatenate([edge_rows[:, None, :], current[:, :-1]], axis=1)
    shift_delta = previous - current
    row_count = CALLER_TOTAL * PROPOSED_STEPS
    mixed_decay = (current + shift_delta * fading_blend_ratio).astype(jnp.bfloat16).reshape(row_count, EMBEDDING_SIZE)
    mixed_rate = (current + shift_delta * learning_speed_blend).astype(jnp.bfloat16).reshape(row_count, EMBEDDING_SIZE)
    decay_inner = jnp.tanh(jnp.dot(mixed_decay, fading_left_factor, preferred_element_type=jnp.float32)).astype(jnp.bfloat16)
    rate_inner = jnp.dot(mixed_rate, learning_speed_left, preferred_element_type=jnp.float32).astype(jnp.bfloat16)
    decay_term = jnp.dot(decay_inner, fading_right_factor, preferred_element_type=jnp.float32).reshape(CALLER_TOTAL, PROPOSED_STEPS, EMBEDDING_SIZE)
    rate_term = jnp.dot(rate_inner, learning_speed_right, preferred_element_type=jnp.float32).reshape(CALLER_TOTAL, PROPOSED_STEPS, EMBEDDING_SIZE)
    log_forget = -jax.nn.softplus(-(fading_offset + decay_term)) - 0.5
    forget = jnp.exp(-jnp.exp(log_forget))
    in_rate = jax.nn.sigmoid(learning_speed_offset + rate_term)
    key_full = guessed_lookup_vectors.astype(jnp.float32)
    grouped = (key_full * erasing_lookup_factor).reshape(CALLER_TOTAL, PROPOSED_STEPS, ATTENTION_LANES, LANE_SIZE)
    unit_key = grouped * lax.rsqrt(lax.optimization_barrier(jnp.sum(grouped * grouped, axis=-1, keepdims=True)) + EPSILON)
    adjusted_lookup = key_full * (1.0 + (in_rate - 1.0) * written_lookup_factor)
    content_lines = guessed_content_vectors.astype(jnp.float32)
    gating_query_lines = gating_query.astype(jnp.float32)

    def by_head(array):
        return jnp.transpose(array.reshape(CALLER_TOTAL, PROPOSED_STEPS, ATTENTION_LANES, LANE_SIZE), (2, 1, 0, 3))

    def run_head(packed):
        return head_scan(packed, counts)
    outputs, accepted_states = lax.map(run_head, (jnp.transpose(start_states, (1, 0, 2, 3)), by_head(forget), by_head(unit_key), by_head(in_rate), by_head(adjusted_lookup), by_head(content_lines), by_head(gating_query_lines)))
    outputs = jnp.transpose(outputs, (2, 1, 0, 3))
    average = lax.optimization_barrier(jnp.mean(outputs, axis=-1, keepdims=True))
    centered = outputs - average
    variance = lax.optimization_barrier(jnp.mean(centered * centered, axis=-1, keepdims=True))
    standardized_lines = centered * lax.rsqrt(variance + NORM_EPSILON) * lane_standard_factor.reshape(ATTENTION_LANES, LANE_SIZE) + lane_standard_offset.reshape(ATTENTION_LANES, LANE_SIZE)
    present_reward_term = lax.optimization_barrier(jnp.sum((gating_query_lines * adjusted_lookup * present_reward_factors).reshape(CALLER_TOTAL, PROPOSED_STEPS, ATTENTION_LANES, LANE_SIZE), axis=-1, keepdims=True)) * content_lines.reshape(CALLER_TOTAL, PROPOSED_STEPS, ATTENTION_LANES, LANE_SIZE)
    temporal_blend_result = (standardized_lines + present_reward_term).astype(jnp.bfloat16).reshape(CALLER_TOTAL, PROPOSED_STEPS, EMBEDDING_SIZE)
    last_token = jnp.maximum(counts - 1, 0).astype(jnp.int32)
    picked = jnp.take_along_axis(current, last_token[:, None, None], axis=1)[:, 0]
    new_edge_rows = jnp.where((counts > 0)[:, None], picked, edge_rows)
    state_rows = jnp.transpose(accepted_states, (1, 0, 2, 3)).reshape(CALLER_TOTAL, ATTENTION_LANES, halves, SLOT_ROWS * LANE_SIZE)
    new_states = jnp.zeros((N_HEAD, SLOTS, SLOT_ROWS * LANE_SIZE), jnp.float32).at[group_ids, targets].set(state_rows)
    new_edges = jnp.zeros((N_HEAD, SLOTS, SLOT_ROWS), jnp.float32).at[group_ids, targets].set(new_edge_rows.reshape(CALLER_TOTAL, ATTENTION_LANES, halves, SLOT_ROWS))
    return (temporal_blend_result, new_states, new_edges)
```

```python
import functools

import jax
import jax.numpy as jnp
from jax import lax
from jax.experimental import pallas as pl
from jax.experimental.pallas import tpu as pltpu
from jax.sharding import PartitionSpec as P

EPSILON = 1e-05
NORM_EPSILON = 0.00064
DECAY_SCALE = 0.6065306597126334
F32 = jnp.float32
BF16 = jnp.bfloat16
I32 = jnp.int32
NT = (((1,), (1,)), ((), ()))
NN = (((1,), (0,)), ((), ()))

SMEM = functools.partial(pl.BlockSpec, memory_space=pltpu.SMEM)
VMEM = functools.partial(pl.BlockSpec, memory_space=pltpu.VMEM)


def call(kernel, out_shape, in_specs, scratch=(), flops=1 << 20, moved=1 << 20):
    return pl.pallas_call(
        kernel,
        out_shape=out_shape,
        in_specs=in_specs,
        out_specs=jax.tree.map(lambda _: VMEM(), out_shape),
        scratch_shapes=list(scratch),
        compiler_params=pltpu.CompilerParams(vmem_limit_bytes=48 * 1024 * 1024),
        cost_estimate=pl.CostEstimate(flops=flops, bytes_accessed=moved, transcendentals=0),
    )


def dot(a, b, dims=NN):
    return lax.dot_general(a, b, dims, preferred_element_type=F32)


def split(x):
    high = x.astype(BF16)
    return high, (x - high.astype(F32)).astype(BF16)


def group_sum(x, width):
    rows, lanes = x.shape
    block = max(width, 128)
    ones = (
        lax.broadcasted_iota(I32, (block, block), 0) // width
        == lax.broadcasted_iota(I32, (block, block), 1) // width
    ).astype(BF16)
    high, low = split(x)
    parts = []
    for start in range(0, lanes, block):
        cut = slice(start, start + block)
        parts.append(dot(high[:, cut], ones) + dot(low[:, cut], ones))
    return jnp.concatenate(parts, axis=1)


def positions(seq_ref, count):
    lane = lax.broadcasted_iota(I32, (1, count), 1)

    def block(b, acc):
        for k in range(8):
            acc = jnp.where(lane == seq_ref[b * 8 + k], b * 8 + k, acc)
        return acc

    return lax.fori_loop(0, count // 8, block, jnp.zeros((1, count), I32))


def place_of_slot(table_ref, position, base, blocks, per_peer, requests, slot_dev):
    heads, halves, count = table_ref.shape
    slot = lax.broadcasted_iota(I32, (slot_dev, count), 0) + base
    named = jnp.zeros((slot_dev, count), F32)
    for h in range(heads):
        for c in range(halves):
            named = jnp.where(table_ref[h, c : c + 1, :] == slot, 1.0, named)
    other_of = jnp.broadcast_to(position // requests, (16, count)).astype(F32).astype(BF16)
    other = dot(other_of, named.astype(BF16), NT)[0:1, :].astype(I32)
    rows = max(16, blocks)
    mask = other == lax.broadcasted_iota(I32, (rows, slot_dev), 0)
    before = (
        lax.broadcasted_iota(I32, (slot_dev, slot_dev), 0)
        < lax.broadcasted_iota(I32, (slot_dev, slot_dev), 1)
    ).astype(F32).astype(BF16)
    ahead = dot(mask.astype(F32).astype(BF16), before)
    rank = jnp.sum(jnp.where(mask, ahead, 0.0), axis=0, keepdims=True).astype(I32)
    return other * per_peer + rank


def place_of_item(table_ref, position, first, requests):
    heads, halves, count = table_ref.shape
    per_item = heads * halves
    items = requests * per_item
    mine = (
        jnp.broadcast_to(position, (16, count)) - first == lax.broadcasted_iota(I32, (16, count), 0)
    ).astype(F32).astype(BF16)
    lane = lax.broadcasted_iota(I32, (16, items), 1)
    owner = lax.broadcasted_iota(I32, (16, items), 0) == lane // per_item
    slots = jnp.zeros((16, items), F32)
    for h in range(heads):
        for c in range(halves):
            line = jnp.broadcast_to(table_ref[h, c : c + 1, :], (items, count))
            high = dot(mine, (line // 128).astype(F32).astype(BF16), NT)
            low = dot(mine, (line % 128).astype(F32).astype(BF16), NT)
            slots = jnp.where(lane % per_item == h * halves + c, high * 128.0 + low, slots)
    row = jnp.sum(jnp.where(owner, slots, 0.0), axis=0, keepdims=True)
    diagonal = lax.broadcasted_iota(I32, (items, items), 0) == lax.broadcasted_iota(I32, (items, items), 1)
    column = jnp.sum(jnp.where(diagonal, row, 0.0), axis=1, keepdims=True)
    return row.astype(I32), jnp.sum((column < row).astype(F32), axis=0, keepdims=True).astype(I32)


def send_kernel(
    blocks, requests, per_peer,
    seq_ref, read_ref, write_ref, state_ref,
    out_ref, index_ref, scratch,
):
    slot_dev = state_ref.shape[0]
    lanes = state_ref.shape[1] // 128
    me = lax.axis_index("blk")
    position = positions(seq_ref, read_ref.shape[2])
    place = place_of_slot(read_ref, position, me * slot_dev, blocks, per_peer, requests, slot_dev)
    pick = (place == lax.broadcasted_iota(I32, (slot_dev, slot_dev), 0)).astype(F32).astype(BF16)
    left = lax.broadcasted_iota(I32, (slot_dev, 128), 1) < 64
    half = lanes // 2
    for b in range(half):
        x = dot(pick, state_ref[:, b * 128 : (b + 1) * 128].astype(BF16))
        y = dot(pick, state_ref[:, (half + b) * 128 : (half + b + 1) * 128].astype(BF16))
        scratch[:, 2 * b, :] = jnp.where(left, x, pltpu.roll(y, 64, 1))
        scratch[:, 2 * b + 1, :] = jnp.where(left, pltpu.roll(x, 64, 1), y)
    out_ref[...] = scratch[...].astype(BF16)
    first = me * requests
    wanted, place = place_of_item(read_ref, position, first, requests)
    index_ref[0:1, :] = place
    index_ref[2:3, :] = wanted
    index_ref[1:2, :] = place_of_item(write_ref, position, first, requests)[1]
    index_ref[3:8, :] = jnp.zeros((5, slot_dev), I32)


def target_kernel(blocks, requests, per_peer, slot_dev, seq_ref, write_ref, out_ref):
    position = positions(seq_ref, write_ref.shape[2])
    base = lax.axis_index("blk") * slot_dev
    place = place_of_slot(write_ref, position, base, blocks, per_peer, requests, slot_dev)
    out_ref[...] = jnp.broadcast_to(place, out_ref.shape)


def shift_kernel(
    requests, heads, halves,
    index_ref, seq_ref, count_ref, edges_ref, layer_ref, mix_decay_ref, mix_rate_ref, left_decay_ref, left_rate_ref,
    out_ref, new_edge_ref, pool_scratch, edge_scratch, line_scratch,
):
    width = layer_ref.shape[1]
    steps = layer_ref.shape[0] // requests
    blocks, rows, slot_dev = edges_ref.shape
    first = lax.axis_index("blk") * requests

    @pl.loop(0, blocks)
    def _(b):
        pool = jnp.concatenate([edges_ref[b], jnp.zeros((slot_dev - rows, slot_dev), F32)], axis=0)
        pool_scratch[pl.ds(pl.multiple_of(b * slot_dev, slot_dev), slot_dev), :] = jnp.transpose(pool)

    for p in range(requests):
        for k in range(heads * halves):
            slot = index_ref[2, p * heads * halves + k]
            edge_scratch[p : p + 1, k * rows : (k + 1) * rows] = pool_scratch[pl.ds(slot, 1), :rows]
    edge = edge_scratch[...]
    line = layer_ref[...].astype(F32)
    line_scratch[...] = line
    step = lax.broadcasted_iota(I32, line.shape, 0) % steps
    edge_lines = jnp.broadcast_to(edge[:, None, :], (requests, steps, width)).reshape(line.shape)
    delta = jnp.where(step == 0, edge_lines, pltpu.roll(line, 1, 0)) - line
    rank = left_decay_ref.shape[0]
    mixed_decay = (line + delta * mix_decay_ref[...]).astype(BF16)
    mixed_rate = (line + delta * mix_rate_ref[...]).astype(BF16)
    partial_decay = dot(mixed_decay, left_decay_ref[...], NT).astype(BF16)
    partial_rate = dot(mixed_rate, left_rate_ref[...], NT).astype(BF16)
    out_ref[:, :rank] = partial_decay
    out_ref[:, rank:] = partial_rate
    for p in range(requests):
        n = count_ref[seq_ref[first + p]]
        picked = line_scratch[pl.ds(p * steps + jnp.maximum(n - 1, 0), 1), :]
        new_edge_ref[p : p + 1, :] = jnp.where(n > 0, picked, edge[p : p + 1, :])


def expand(x, head_width):
    steps, lanes = x.shape
    heads = lanes // head_width
    per_block = 128 // head_width
    lane = lax.broadcasted_iota(I32, (steps, 128), 1) // head_width
    zero = jnp.zeros((steps, 128), x.dtype)
    lines = []
    for h in range(heads):
        own = h // per_block
        block = jnp.where(lane == h % per_block, x[:, own * 128 : (own + 1) * 128], zero)
        lines.append(jnp.concatenate([block if b == own else zero for b in range(lanes // 128)], axis=1))
    return jnp.concatenate(lines, axis=0)


def prepare_kernel(
    requests, heads,
    seq_ref, count_ref, parts_ref, right_decay_ref, right_rate_ref, offset_decay_ref, offset_rate_ref,
    key_ref, value_ref, erase_ref, written_ref,
    a_ref, k_ref, b_ref, cum_ref, key_mod_ref, last_ref, value_t_ref, small_ref, solve_ref,
    cross, compact,
):
    rows, width = key_ref.shape
    steps = rows // requests
    head_width = width // heads
    rank = right_decay_ref.shape[0]
    first = lax.axis_index("blk") * requests
    total = parts_ref[0].astype(F32)
    for g in range(1, parts_ref.shape[0]):
        total = total + parts_ref[g].astype(F32)
    hidden = jnp.tanh(total[:, :rank]).astype(BF16)
    rate_hidden = total[:, rank:].astype(BF16)
    decay = offset_decay_ref[...] + dot(hidden, right_decay_ref[...])
    log_forget = -DECAY_SCALE * jax.nn.sigmoid(decay)
    rate = jax.nn.sigmoid(offset_rate_ref[...] + dot(rate_hidden, right_rate_ref[...]))
    key = key_ref[...].astype(F32)
    u = key * erase_ref[...]
    unit = u * lax.rsqrt(group_sum(u * u, head_width) + EPSILON)
    key_mod = key * (1.0 + (rate - 1.0) * written_ref[...])
    key_mod_ref[...] = key_mod
    step = lax.broadcasted_iota(I32, (rows, width), 0) % steps
    cum = log_forget
    shift = 1
    while shift < steps:
        cum = cum + jnp.where(step >= shift, pltpu.roll(cum, shift, 0), 0.0)
        shift *= 2
    grow = jnp.exp(-cum)
    cum_ref[...] = cum
    a_ref[...] = (unit * jnp.exp(cum - log_forget)).astype(BF16)
    k_ref[...] = (key_mod * grow).astype(BF16)
    b_ref[...] = (rate * unit * grow).astype(BF16)
    ident = (
        lax.broadcasted_iota(I32, (head_width, width), 0)
        == lax.broadcasted_iota(I32, (head_width, width), 1) % head_width
    ).astype(F32).astype(BF16)
    for p in range(requests):
        cut = slice(p * steps, (p + 1) * steps)
        n = count_ref[seq_ref[first + p]]
        at_n = cum_ref[pl.ds(p * steps + jnp.maximum(n - 1, 0), 1), :]
        last_ref[p : p + 1, :] = jnp.where(n > 0, jnp.exp(at_n), 1.0)
        right = jnp.concatenate([expand(k_ref[cut, :], head_width), expand(b_ref[cut, :], head_width)], axis=0)
        cross[p] = dot(a_ref[cut, :], right, NT)
        value_t_ref[p] = dot(ident, expand(value_ref[cut, :], head_width), NT).astype(BF16)
    lanes = heads * steps
    lane = lax.broadcasted_iota(I32, (requests, lanes), 1)
    source = lane % steps
    group = lane - source
    solve, carry = [], []
    for t in range(steps):
        weights = jnp.where(source < t, cross[:, t, lanes:], 0.0)
        solve_t = jnp.where(source == t, 1.0, 0.0)
        carry_t = jnp.where(source < t, cross[:, t, :lanes], 0.0)
        for s in range(t):
            weight = jnp.take_along_axis(weights, group + s, axis=1)
            solve_t = solve_t - weight * solve[s]
            carry_t = carry_t - weight * carry[s]
        solve.append(solve_t)
        carry.append(carry_t)
        compact[0, :, t, :] = solve_t
        compact[1, :, t, :] = carry_t
        solve_ref[0, t] = solve_t
        solve_ref[1, t] = carry_t
    small_ref[...] = compact[...].astype(BF16)


def spread(x, steps):
    lanes = x.shape[1]
    group = lax.broadcasted_iota(I32, x.shape, 1) // steps
    zero = jnp.zeros_like(x)
    return jnp.concatenate([jnp.where(group == h, x, zero) for h in range(lanes // steps)], axis=0)


def state_kernel(
    requests, heads, halves, per_peer,
    index_ref, seq_ref, count_ref, got_ref, a_ref, k_ref, b_ref, last_ref, value_t_ref, small_ref, new_edge_ref,
    send_ref, state_ref, both_ref, edge_scratch,
):
    rows, width = a_ref.shape
    steps = rows // requests
    head_width = width // heads
    pack = got_ref.shape[1]
    first = lax.axis_index("blk") * requests
    edge_rows = head_width // halves
    low = lax.broadcasted_iota(I32, (pack, 128), 1) < head_width

    def sent_at(item):
        place = index_ref[1, item]
        return place + place // per_peer

    for p in range(requests):
        cut = slice(p * steps, (p + 1) * steps)
        n = count_ref[seq_ref[first + p]]
        lines = []
        for c in range(halves):
            tops, bottoms = [], []
            for pair in range(heads // 2):
                at = (p * heads + 2 * pair) * halves + c
                even = got_ref[index_ref[0, at]].astype(F32)
                odd = got_ref[index_ref[0, at + halves]].astype(F32)
                tops.append(jnp.where(low, even, pltpu.roll(odd, head_width, 1)))
                bottoms.append(jnp.where(low, pltpu.roll(even, head_width, 1), odd))
            lines.append(jnp.concatenate(tops, axis=1))
            lines.append(jnp.concatenate(bottoms, axis=1))
        state = jnp.concatenate(lines, axis=0)
        state_b = state.astype(BF16)
        state_ref[p] = state_b
        along = dot(state_b, expand(a_ref[cut, :], head_width), NT).astype(BF16)
        value_t = value_t_ref[p]
        both = jnp.concatenate([along, value_t], axis=1)
        both_ref[p] = both
        weights = jnp.concatenate([spread(small_ref[0, p], steps), spread(small_ref[1, p], steps)], axis=1)
        removed = dot(both, weights, NT)
        update = jnp.concatenate([-removed, value_t.astype(F32)], axis=1)
        step = lax.broadcasted_iota(I32, update.shape, 1) % steps
        update = jnp.where(step < n, update, 0.0).astype(BF16)
        written = jnp.concatenate([expand(b_ref[cut, :], head_width), expand(k_ref[cut, :], head_width)], axis=0)
        kept = (state + dot(update, written)) * last_ref[p : p + 1, :]
        for c in range(halves):
            for pair in range(heads // 2):
                top = kept[(2 * c) * pack : (2 * c + 1) * pack, pair * 128 : (pair + 1) * 128]
                bottom = kept[(2 * c + 1) * pack : (2 * c + 2) * pack, pair * 128 : (pair + 1) * 128]
                at = (p * heads + 2 * pair) * halves + c
                send_ref[sent_at(at)] = jnp.where(low, top, pltpu.roll(bottom, head_width, 1)).astype(BF16)
                send_ref[sent_at(at + halves)] = jnp.where(low, pltpu.roll(top, head_width, 1), bottom).astype(BF16)
        for k in range(heads * halves):
            lane = k * edge_rows
            line = new_edge_ref[p : p + 1, lane // 128 * 128 : lane // 128 * 128 + 128]
            if lane % 128:
                line = pltpu.roll(line, 128 - lane % 128, 1)
            edge_scratch[pl.ds(index_ref[1, p * heads * halves + k], 1), :] = line
    blocks = rows_of(edge_scratch) // per_peer
    for b in range(blocks):
        block = edge_scratch[b * per_peer : (b + 1) * per_peer, :]
        if per_peer < pack:
            block = jnp.concatenate([block, jnp.zeros((pack - per_peer, 128), F32)], axis=0)
        send_ref[b * (per_peer + 1) + per_peer] = block.astype(BF16)


def rows_of(ref):
    return ref.shape[0]


def lines_kernel(gating_ref, *refs):
    *outs, scratch = refs
    requests, part = gating_ref.shape[:2]
    width = scratch.shape[1]
    me = lax.axis_index("head")
    for d, out in enumerate(outs):
        start = pl.multiple_of((me ^ d) * width, 128)
        for p in range(requests):
            scratch[p * part : (p + 1) * part, :] = gating_ref[p, :, pl.ds(start, width)].astype(F32)
        out[...] = scratch[...].astype(BF16)


def read_kernel(
    requests, heads, groups,
    *refs,
):
    return read_body(requests, heads, refs[:groups], *refs[groups:])


def read_body(
    requests, heads,
    recept_refs, cum_ref, key_mod_ref, k_ref, b_ref, solve_ref, state_ref, both_ref, value_ref, reward_ref, gain_ref, offset_ref,
    result_ref, line_scratch, cross, compact, out_scratch,
):
    rows, width = value_ref.shape
    steps = rows // requests
    head_width = width // heads
    lanes = heads * steps
    part = steps // len(recept_refs)
    row = lax.broadcasted_iota(I32, (rows, rows), 0)
    source = (row % steps // part) ^ lax.axis_index("head")
    source_row = source * (requests * part) + row // steps * part + row % part
    order = (source_row == lax.broadcasted_iota(I32, (rows, rows), 1)).astype(F32).astype(BF16)
    recept = dot(order, jnp.concatenate([ref[...] for ref in recept_refs], axis=0))
    bonus = group_sum(recept * key_mod_ref[...] * reward_ref[...], head_width)
    line_scratch[...] = (recept * jnp.exp(cum_ref[...])).astype(BF16)
    for p in range(requests):
        cut = slice(p * steps, (p + 1) * steps)
        right = jnp.concatenate([expand(k_ref[cut, :], head_width), expand(b_ref[cut, :], head_width)], axis=0)
        cross[p] = dot(line_scratch[cut, :], right, NT)
    lane = lax.broadcasted_iota(I32, (requests, lanes), 1)
    source = lane % steps
    group = lane - source
    for t in range(steps):
        weights = jnp.where(source <= t, cross[:, t, lanes:], 0.0)
        from_a = jnp.zeros((requests, lanes), F32)
        from_v = jnp.where(source <= t, cross[:, t, :lanes], 0.0)
        for s in range(t + 1):
            weight = jnp.take_along_axis(weights, group + s, axis=1)
            from_a = from_a - weight * solve_ref[0, s]
            from_v = from_v - weight * solve_ref[1, s]
        compact[0, :, t, :] = from_a
        compact[1, :, t, :] = from_v
    out_low = lax.broadcasted_iota(I32, (steps, 128), 1) < head_width
    for p in range(requests):
        cut = slice(p * steps, (p + 1) * steps)
        read = jnp.concatenate(
            [spread(compact[0, p].astype(BF16), steps), spread(compact[1, p].astype(BF16), steps)], axis=1
        )
        both = both_ref[p]
        state = state_ref[p]
        out = dot(read, jnp.concatenate([both, both], axis=0), NT)
        out = out + dot(expand(line_scratch[cut, :], head_width), jnp.concatenate([state, state], axis=0), NT)
        for pair in range(heads // 2):
            at = 2 * pair * steps
            out_scratch[cut, pair * 128 : (pair + 1) * 128] = jnp.where(
                out_low, out[at : at + steps, :], out[at + steps : at + 2 * steps, :]
            )
    out = out_scratch[...]
    centered = out - group_sum(out, head_width) * (1.0 / head_width)
    variance = group_sum(centered * centered, head_width) * (1.0 / head_width)
    line = centered * lax.rsqrt(variance + NORM_EPSILON) * gain_ref[...] + offset_ref[...]
    result_ref[...] = (line + bonus * value_ref[...].astype(F32)).astype(BF16)


def place_kernel(per_peer, index_ref, back_ref, out_ref, edge_ref, scratch, edge_scratch, edge_placed):
    slot_dev = out_ref.shape[0]
    pack = back_ref.shape[1]
    for b in range(slot_dev // per_peer):
        block = back_ref[b * (per_peer + 1) + per_peer].astype(F32)
        edge_scratch[b * per_peer : (b + 1) * per_peer, :] = block[:per_peer, :]
    for s in range(slot_dev):
        place = index_ref[0, s]
        scratch[s] = back_ref[place + place // per_peer].astype(F32)
        edge_placed[s : s + 1, :] = edge_scratch[pl.ds(place, 1), :]
    left = lax.broadcasted_iota(I32, (slot_dev, 128), 1) < 64
    half = pack // 2
    for b in range(half):
        even = scratch[:, 2 * b, :]
        odd = scratch[:, 2 * b + 1, :]
        out_ref[:, b * 128 : (b + 1) * 128] = jnp.where(left, even, pltpu.roll(odd, 64, 1))
        out_ref[:, (half + b) * 128 : (half + b + 1) * 128] = jnp.where(left, pltpu.roll(even, 64, 1), odd)
    edge_ref[...] = jnp.transpose(edge_placed[...])[: edge_ref.shape[0], :]


def local(
    layer_entry_vectors,
    guessed_lookup_vectors,
    guessed_content_vectors,
    gating_query,
    lane_memory_store,
    prior_step_store,
    fading_blend_ratio,
    learning_speed_blend,
    fading_left_factor,
    fading_right_factor,
    fading_offset,
    learning_speed_left,
    learning_speed_right,
    learning_speed_offset,
    erasing_lookup_factor,
    written_lookup_factor,
    present_reward_factors,
    lane_standard_factor,
    lane_standard_offset,
    caller_memory_directory,
    kept_target_place,
    caller_sequence,
    approved_guesses,
):
    blocks = lax.axis_size("blk")
    groups = lax.axis_size("head")
    requests, steps, width = layer_entry_vectors.shape
    heads, halves = caller_memory_directory.shape[1:]
    slot_dev = lane_memory_store.shape[1]
    slot_width = lane_memory_store.shape[2]
    pack = slot_width // 128
    per_peer = slot_dev // blocks
    edge_rows = prior_step_store.shape[2]
    rows = requests * steps
    rank = fading_left_factor.shape[1]
    sds = jax.ShapeDtypeStruct

    def line(x):
        return x.reshape(1, width)

    def exchange(x, axis):
        return lax.all_to_all(x, axis, split_axis=0, concat_axis=0, tiled=True)

    read_table = caller_memory_directory.transpose(1, 2, 0)
    write_table = kept_target_place.transpose(1, 2, 0)
    pool = jnp.broadcast_to(prior_step_store[0].T, (blocks, edge_rows, slot_dev))
    edges = exchange(pool, "blk")
    sent, index = call(
        functools.partial(send_kernel, blocks, requests, per_peer),
        (sds((slot_dev, pack, 128), BF16), sds((8, slot_dev), I32)),
        [SMEM()] + [VMEM()] * 3,
        [pltpu.VMEM((slot_dev, pack, 128), F32)],
    )(caller_sequence, read_table, write_table, lane_memory_store[0])
    got = exchange(sent.reshape(blocks, per_peer * pack, 128), "blk").reshape(slot_dev, pack, 128)

    layer = layer_entry_vectors.reshape(rows, width)
    key = guessed_lookup_vectors.reshape(rows, width)
    value = guessed_content_vectors.reshape(rows, width)
    partial_sums, new_edge = call(
        functools.partial(shift_kernel, requests, heads, halves),
        (sds((rows, 2 * rank), BF16), sds((requests, width), F32)),
        [SMEM(), SMEM(), SMEM()] + [VMEM()] * 6,
        [
            pltpu.VMEM((blocks * slot_dev, slot_dev), F32),
            pltpu.VMEM((requests, width), F32),
            pltpu.VMEM((rows, width), F32),
        ],
    )(
        index, caller_sequence, approved_guesses, edges, layer, line(fading_blend_ratio), line(learning_speed_blend),
        fading_left_factor.T, learning_speed_left.T,
    )
    parts = lax.all_gather(partial_sums, "head", axis=0)

    wide = sds((rows, width), BF16)
    full = sds((rows, width), F32)
    a_lines, k_lines, b_lines, cum, key_mod, last, value_t, small, solve = call(
        functools.partial(prepare_kernel, requests, heads),
        (
            wide, wide, wide, full, full,
            sds((requests, width), F32),
            sds((requests, width // heads, heads * steps), BF16),
            sds((2, requests, steps, heads * steps), BF16),
            sds((2, steps, requests, heads * steps), F32),
        ),
        [SMEM(), SMEM()] + [VMEM()] * 9,
        [
            pltpu.VMEM((requests, steps, 2 * heads * steps), F32),
            pltpu.VMEM((2, requests, steps, heads * steps), F32),
        ],
    )(
        caller_sequence, approved_guesses, parts, fading_right_factor, learning_speed_right,
        line(fading_offset), line(learning_speed_offset), key, value,
        line(erasing_lookup_factor), line(written_lookup_factor),
    )
    back, state, both = call(
        functools.partial(state_kernel, requests, heads, halves, per_peer),
        (
            sds((blocks * (per_peer + 1), pack, 128), BF16),
            sds((requests, width // heads, width), BF16),
            sds((requests, width // heads, 2 * heads * steps), BF16),
        ),
        [SMEM(), SMEM(), SMEM()] + [VMEM()] * 8,
        [pltpu.VMEM((slot_dev, 128), F32)],
    )(
        index, caller_sequence, approved_guesses, got, a_lines, k_lines, b_lines, last, value_t, small, new_edge,
    )
    back = exchange(back.reshape(blocks, (per_peer + 1) * pack, 128), "blk")
    back = back.reshape(blocks * (per_peer + 1), pack, 128)
    recept = call(
        lines_kernel,
        (sds((rows // groups, width), BF16),) * groups,
        [VMEM()],
        [pltpu.VMEM((rows // groups, width), F32)],
    )(gating_query)
    recept = [recept[0]] + [
        lax.ppermute(recept[d], "head", [(g, g ^ d) for g in range(groups)]) for d in range(1, groups)
    ]
    result = call(
        functools.partial(read_kernel, requests, heads, groups),
        wide,
        [VMEM()] * (11 + groups),
        [
            pltpu.VMEM((rows, width), BF16),
            pltpu.VMEM((requests, steps, 2 * heads * steps), F32),
            pltpu.VMEM((2, requests, steps, heads * steps), F32),
            pltpu.VMEM((rows, width), F32),
        ],
    )(
        *recept, cum, key_mod, k_lines, b_lines, solve, state, both, value,
        line(present_reward_factors), line(lane_standard_factor), line(lane_standard_offset),
    )
    target = call(
        functools.partial(target_kernel, blocks, requests, per_peer, slot_dev),
        sds((8, slot_dev), I32),
        [SMEM(), VMEM()],
    )(caller_sequence, write_table)
    new_states, new_edges = call(
        functools.partial(place_kernel, per_peer),
        (sds((slot_dev, slot_width), F32), sds((edge_rows, slot_dev), F32)),
        [SMEM(), VMEM()],
        [
            pltpu.VMEM((slot_dev, pack, 128), F32),
            pltpu.VMEM((slot_dev, 128), F32),
            pltpu.VMEM((slot_dev, 128), F32),
        ],
    )(target, back)
    return (result.reshape(requests, steps, width), new_states[None], new_edges.T[None])


def solution(mesh):
    return jax.shard_map(
        local,
        mesh=mesh,
        in_specs=(
            P("blk", None, "head"),
            P("blk", None, "head"),
            P("blk", None, "head"),
            P("blk", "head", None),
            P("head", "blk", None),
            P("head", "blk", None),
            P("head"),
            P("head"),
            P("head", None),
            P(None, "head"),
            P("head"),
            P("head", None),
            P(None, "head"),
            P("head"),
            P("head"),
            P("head"),
            P("head"),
            P("head"),
            P("head"),
            P(None, "head", None),
            P(None, "head", None),
            P(),
            P(),
        ),
        out_specs=(P("blk", None, "head"), P("head", "blk", None), P("head", "blk", None)),
        check_vma=False,
    )
```

```python
import functools

import jax
import jax.numpy as jnp
from jax import lax
from jax.experimental import pallas as pl
from jax.experimental.pallas import tpu as pltpu
from jax.sharding import PartitionSpec as P

EPSILON = 1e-05
NORM_EPSILON = 0.00064
DECAY_SCALE = 0.6065306597126334
F32 = jnp.float32
BF16 = jnp.bfloat16
I32 = jnp.int32
NT = (((1,), (1,)), ((), ()))
NN = (((1,), (0,)), ((), ()))


def call(kernel, outs, scalars=(), near=(), far=(), raw=(), held=(), scratch=(), vmem=16):
    reads = len(scalars) + len(near) + len(far) + len(raw)

    def body(*refs):
        kernel(*refs[:reads], *refs[reads + len(held) :])

    args = [*scalars]
    args += [*near]
    args += [pltpu.with_memory_space_constraint(x, pltpu.HBM) for x in (*far, *raw)]
    specs = [pl.BlockSpec(memory_space=pltpu.SMEM)] * len(scalars)
    specs += [pl.BlockSpec(memory_space=pltpu.VMEM)] * (len(near) + len(far))
    specs += [pl.BlockSpec(memory_space=pltpu.HBM)] * (len(raw) + len(held))
    return pl.pallas_call(
        body,
        out_shape=outs,
        in_specs=specs,
        out_specs=jax.tree.map(lambda _: pl.BlockSpec(memory_space=pltpu.VMEM), outs),
        scratch_shapes=list(scratch),
        compiler_params=pltpu.CompilerParams(vmem_limit_bytes=vmem * 1024 * 1024),
        cost_estimate=pl.CostEstimate(flops=1 << 20, bytes_accessed=1 << 20, transcendentals=0),
    )(*args, *held)


def dot(a, b, dims=NN):
    return lax.dot_general(a, b, dims, preferred_element_type=F32)


def split(x):
    high = x.astype(BF16)
    return high, (x - high.astype(F32)).astype(BF16)


def group_sum(x, width):
    rows, lanes = x.shape
    block = max(width, 128)
    ones = (
        lax.broadcasted_iota(I32, (block, block), 0) // width
        == lax.broadcasted_iota(I32, (block, block), 1) // width
    ).astype(BF16)
    high, low = split(x)
    parts = []
    for start in range(0, lanes, block):
        cut = slice(start, start + block)
        parts.append(dot(high[:, cut], ones) + dot(low[:, cut], ones))
    return jnp.concatenate(parts, axis=1)


def positions(seq_ref, count):
    lane = lax.broadcasted_iota(I32, (1, count), 1)

    def block(b, acc):
        for k in range(8):
            acc = jnp.where(lane == seq_ref[b * 8 + k], b * 8 + k, acc)
        return acc

    return lax.fori_loop(0, count // 8, block, jnp.zeros((1, count), I32))


def place_of_slot(table_ref, position, base, blocks, per_peer, requests, slot_dev):
    heads, halves, count = table_ref.shape
    slot = lax.broadcasted_iota(I32, (slot_dev, count), 0) + base
    named = jnp.zeros((slot_dev, count), F32)
    for h in range(heads):
        for c in range(halves):
            named = jnp.where(table_ref[h, c : c + 1, :] == slot, 1.0, named)
    other_of = jnp.broadcast_to(position // requests, (16, count)).astype(F32).astype(BF16)
    other = dot(other_of, named.astype(BF16), NT)[0:1, :].astype(I32)
    rows = max(16, blocks)
    mask = other == lax.broadcasted_iota(I32, (rows, slot_dev), 0)
    before = (
        lax.broadcasted_iota(I32, (slot_dev, slot_dev), 0)
        < lax.broadcasted_iota(I32, (slot_dev, slot_dev), 1)
    ).astype(F32).astype(BF16)
    ahead = dot(mask.astype(F32).astype(BF16), before)
    rank = jnp.sum(jnp.where(mask, ahead, 0.0), axis=0, keepdims=True).astype(I32)
    return other * per_peer + rank


def place_of_item(table_ref, lines_ref, position, first, requests):
    heads, halves, count = table_ref.shape
    per_item = heads * halves
    items = requests * per_item
    mine = (
        jnp.broadcast_to(position, (16, count)) - first == lax.broadcasted_iota(I32, (16, count), 0)
    ).astype(F32).astype(BF16)
    for h in range(heads):
        lines_ref[h * halves : (h + 1) * halves, :] = table_ref[h]
    lines = lines_ref[...]
    lane = lax.broadcasted_iota(I32, (16, items), 1)
    owner = lax.broadcasted_iota(I32, (16, items), 0) == lane // per_item
    of_item = (
        lax.broadcasted_iota(I32, (per_item, items), 0) == lax.broadcasted_iota(I32, (per_item, items), 1) % per_item
    ).astype(F32).astype(BF16)
    high = dot(dot(mine, (lines // 128).astype(F32).astype(BF16), NT).astype(BF16), of_item)
    low = dot(dot(mine, (lines % 128).astype(F32).astype(BF16), NT).astype(BF16), of_item)
    slots = high * 128.0 + low
    row = jnp.sum(jnp.where(owner, slots, 0.0), axis=0, keepdims=True)
    diagonal = lax.broadcasted_iota(I32, (items, items), 0) == lax.broadcasted_iota(I32, (items, items), 1)
    column = jnp.sum(jnp.where(diagonal, row, 0.0), axis=1, keepdims=True)
    return jnp.sum((column < row).astype(F32), axis=0, keepdims=True).astype(I32)


def send_kernel(
    blocks, requests, per_peer,
    seq_hbm, read_hbm, state_hbm, edge_hbm,
    out_ref,
    seq_ref, read_ref, state_ref, edge_ref, scratch, edge_scratch, sems,
):
    slot_dev = state_ref.shape[0]
    pack = out_ref.shape[1]
    me = lax.axis_index("blk")
    sources = (seq_hbm, read_hbm, state_hbm, edge_hbm)
    targets = (seq_ref, read_ref, state_ref, edge_ref)
    copies = [pltpu.make_async_copy(a, b, sems.at[i]) for i, (a, b) in enumerate(zip(sources, targets))]
    for copy in copies:
        copy.start()
    copies[0].wait()
    copies[1].wait()
    position = positions(seq_ref, read_ref.shape[2])
    place = place_of_slot(read_ref, position, me * slot_dev, blocks, per_peer, requests, slot_dev)
    pick = (place == lax.broadcasted_iota(I32, (slot_dev, slot_dev), 0)).astype(F32).astype(BF16)
    left = lax.broadcasted_iota(I32, (slot_dev, 128), 1) < 64
    copies[3].wait()
    edge_rows = edge_ref.shape[0]
    edges = jnp.concatenate([edge_ref[...], jnp.zeros((slot_dev - edge_rows, slot_dev), F32)], axis=0)
    edge_scratch[...] = dot(pick, edges.astype(BF16), NT)
    half = pack // 2
    copies[2].wait()
    for b in range(half):
        x = dot(pick, state_ref[:, b * 128 : (b + 1) * 128].astype(BF16))
        y = dot(pick, state_ref[:, (half + b) * 128 : (half + b + 1) * 128].astype(BF16))
        scratch[:, 2 * b, :] = jnp.where(left, x, pltpu.roll(y, 64, 1))
        scratch[:, 2 * b + 1, :] = jnp.where(left, pltpu.roll(x, 64, 1), y)
    for b in range(blocks):
        at = b * (per_peer + 1)
        out_ref[at : at + per_peer] = scratch[b * per_peer : (b + 1) * per_peer].astype(BF16)
        block = edge_scratch[b * per_peer : (b + 1) * per_peer, :]
        if per_peer < pack:
            block = jnp.concatenate([block, jnp.zeros((pack - per_peer, 128), F32)], axis=0)
        out_ref[at + per_peer] = block.astype(BF16)


def early_kernel(blocks, requests, per_peer, lines, *refs):
    scalars_hbm, refs = refs[:2], refs[2:]
    tables_hbm, refs = refs[:2], refs[2:]
    vectors_hbm, refs = refs[:lines], refs[lines:]
    arrays_hbm, refs = refs[:5], refs[5:]
    index_ref, partial_ref, first_ref, picked_ref, vector_ref = refs[:5]
    arrays, refs = refs[5:9], refs[9:]
    seq_ref, count_ref, read_ref, write_ref, layer_ref, line_scratch, lines_ref, sems, line_sem, array_sem = refs
    pairs = list(zip((*scalars_hbm, *tables_hbm, arrays_hbm[0]), (seq_ref, count_ref, read_ref, write_ref, layer_ref)))
    copies = [pltpu.make_async_copy(a, b, sems.at[i]) for i, (a, b) in enumerate(pairs)]
    line_copies = [
        pltpu.make_async_copy(a, vector_ref.at[pl.ds(i, 1)], line_sem.at[i]) for i, a in enumerate(vectors_hbm)
    ]
    array_copies = [
        pltpu.make_async_copy(a, b, array_sem.at[i]) for i, (a, b) in enumerate(zip(arrays_hbm[1:], arrays))
    ]
    for copy in (*copies, *line_copies, *array_copies):
        copy.start()
    for copy in copies[:4]:
        copy.wait()
    slot_dev = index_ref.shape[1]
    me = lax.axis_index("blk")
    first = me * requests
    position = positions(seq_ref, read_ref.shape[2])
    place_in = place_of_item(read_ref, lines_ref, position, first, requests)
    place_out = place_of_item(write_ref, lines_ref, position, first, requests)
    target = place_of_slot(write_ref, position, me * slot_dev, blocks, per_peer, requests, slot_dev)
    lane = lax.broadcasted_iota(I32, (1, slot_dev), 1)
    counts = jnp.zeros((1, slot_dev), I32)
    for p in range(requests):
        counts = jnp.where(lane == p, count_ref[seq_ref[first + p]], counts)
    index_ref[0:1, :] = place_in
    index_ref[1:2, :] = place_out
    index_ref[2:3, :] = place_in + place_in // per_peer
    index_ref[3:4, :] = counts
    index_ref[4:5, :] = place_out + place_out // per_peer
    index_ref[5:6, :] = target
    index_ref[6:7, :] = target + target // per_peer
    index_ref[7:8, :] = jnp.zeros((1, slot_dev), I32)
    copies[4].wait()
    for copy in (*line_copies, *array_copies):
        copy.wait()
    steps = layer_ref.shape[0] // requests
    line = layer_ref[...].astype(F32)
    line_scratch[...] = line
    delta = pltpu.roll(line, 1, 0) - line
    left_decay_ref, left_rate_ref = arrays[:2]
    rank = left_decay_ref.shape[0]
    mixed_decay = (line + delta * vector_ref[0:1, :]).astype(BF16)
    mixed_rate = (line + delta * vector_ref[1:2, :]).astype(BF16)
    partial_ref[:, :rank] = dot(mixed_decay, left_decay_ref[...], NT).astype(BF16)
    partial_ref[:, rank:] = dot(mixed_rate, left_rate_ref[...], NT).astype(BF16)
    for p in range(requests):
        first_ref[p : p + 1, :] = line_scratch[p * steps : p * steps + 1, :]
        n = count_ref[seq_ref[first + p]]
        picked_ref[p : p + 1, :] = line_scratch[pl.ds(p * steps + jnp.maximum(n - 1, 0), 1), :]


def first_kernel(
    requests, heads, halves, per_peer,
    index_ref, got_ref, first_ref, vector_ref, left_decay_ref, left_rate_ref,
    out_ref, edge_ref, pool_scratch,
):
    slot_dev = pool_scratch.shape[0]
    rows = first_ref.shape[1] // (heads * halves)
    for b in range(slot_dev // per_peer):
        block = got_ref[b * (per_peer + 1) + per_peer].astype(F32)
        pool_scratch[b * per_peer : (b + 1) * per_peer, :] = block[:per_peer, :]
    for p in range(requests):
        for k in range(heads * halves):
            place = index_ref[0, p * heads * halves + k]
            edge_ref[p : p + 1, k * rows : (k + 1) * rows] = pool_scratch[pl.ds(place, 1), :rows]
    line = first_ref[...]
    delta = edge_ref[...] - line
    rank = left_decay_ref.shape[0]
    mixed_decay = (line + delta * vector_ref[0:1, :]).astype(BF16)
    mixed_rate = (line + delta * vector_ref[1:2, :]).astype(BF16)
    out_ref[:, :rank] = dot(mixed_decay, left_decay_ref[...], NT)
    out_ref[:, rank:] = dot(mixed_rate, left_rate_ref[...], NT)


def expand(x, head_width):
    steps, lanes = x.shape
    heads = lanes // head_width
    per_block = 128 // head_width
    lane = lax.broadcasted_iota(I32, (steps, 128), 1) // head_width
    zero = jnp.zeros((steps, 128), x.dtype)
    lines = []
    for h in range(heads):
        own = h // per_block
        block = jnp.where(lane == h % per_block, x[:, own * 128 : (own + 1) * 128], zero)
        lines.append(jnp.concatenate([block if b == own else zero for b in range(lanes // 128)], axis=1))
    return jnp.concatenate(lines, axis=0)


def ident_of(head_width, width):
    return (
        lax.broadcasted_iota(I32, (head_width, width), 0)
        == lax.broadcasted_iota(I32, (head_width, width), 1) % head_width
    ).astype(F32).astype(BF16)


def head_rows(line, heads, head_width, shift):
    shape = (2 * heads, line.shape[1])
    own = lax.broadcasted_iota(I32, shape, 1) // head_width + shift
    return jnp.where(own == lax.broadcasted_iota(I32, shape, 0), jnp.broadcast_to(line, shape), 0.0)


def prepare_kernel(
    requests, heads,
    index_ref, parts_ref, vector_ref, right_decay_ref, right_rate_ref, key_ref, value_ref,
    a_ref, k_ref, b_ref, scale_ref, key_mod_ref, last_ref, value_t_ref, solve_ref,
    unit_first_ref, key_first_ref, value_first_ref, through_ref, added_ref,
    cross, compact, unit_scratch, cum_ref,
):
    rows, width = key_ref.shape
    steps = rows // requests
    head_width = width // heads
    rank = right_decay_ref.shape[0]
    total = parts_ref[0].astype(F32)
    for g in range(1, parts_ref.shape[0]):
        total = total + parts_ref[g].astype(F32)
    hidden = jnp.tanh(total[:, :rank]).astype(BF16)
    rate_hidden = total[:, rank:].astype(BF16)
    decay = vector_ref[2:3, :] + dot(hidden, right_decay_ref[...])
    step = lax.broadcasted_iota(I32, (rows, width), 0) % steps
    later = step > 0
    log_forget = jnp.where(later, -DECAY_SCALE * jax.nn.sigmoid(decay), 0.0)
    rate = jax.nn.sigmoid(vector_ref[3:4, :] + dot(rate_hidden, right_rate_ref[...]))
    key = key_ref[...].astype(F32)
    u = key * vector_ref[4:5, :]
    unit = u * lax.rsqrt(group_sum(u * u, head_width) + EPSILON)
    unit_scratch[...] = unit
    key_mod = key * (1.0 + (rate - 1.0) * vector_ref[5:6, :])
    key_mod_ref[...] = key_mod.astype(BF16)
    cum = log_forget
    shift = 1
    while shift < steps:
        cum = cum + jnp.where(step >= shift, pltpu.roll(cum, shift, 0), 0.0)
        shift *= 2
    grow = jnp.where(later, jnp.exp(-cum), 0.0)
    cum_ref[...] = cum
    scale_ref[...] = jnp.exp(cum).astype(BF16)
    a_ref[...] = jnp.where(later, unit * jnp.exp(cum - log_forget), 0.0).astype(BF16)
    k_ref[...] = (key_mod * grow).astype(BF16)
    b_ref[...] = (rate * unit * grow).astype(BF16)
    ident = ident_of(head_width, width)
    lanes = heads * steps
    for p in range(requests):
        cut = slice(p * steps, (p + 1) * steps)
        n = index_ref[3, p]
        at_n = cum_ref[pl.ds(p * steps + jnp.maximum(n - 1, 0), 1), :]
        last_ref[p : p + 1, :] = jnp.where(n > 0, jnp.exp(at_n), 1.0)
        unit_first_ref[p : p + 1, :] = unit_scratch[p * steps : p * steps + 1, :]
        key_first_ref[p : p + 1, :] = key_ref[cut, :].astype(F32)[0:1, :]
        value_first_ref[p : p + 1, :] = value_ref[cut, :].astype(F32)[0:1, :]
        right = jnp.concatenate([expand(k_ref[cut, :], head_width), expand(b_ref[cut, :], head_width)], axis=0)
        cross[p] = dot(a_ref[cut, :], right, NT)
        value_t_ref[p] = dot(ident, expand(value_ref[cut, :], head_width), NT).astype(BF16)
    lane = lax.broadcasted_iota(I32, (requests, lanes), 1)
    source = lane % steps
    group = lane - source
    solve, carry = [], []
    for t in range(steps):
        weights = jnp.where(source < t, cross[:, t, lanes:], 0.0)
        solve_t = jnp.where(source == t, 1.0, 0.0)
        carry_t = jnp.where(source < t, cross[:, t, :lanes], 0.0)
        for s in range(t):
            weight = jnp.take_along_axis(weights, group + s, axis=1)
            solve_t = solve_t - weight * solve[s]
            carry_t = carry_t - weight * carry[s]
        solve.append(solve_t)
        carry.append(carry_t)
        compact[0, :, t, :] = solve_t
        compact[1, :, t, :] = carry_t
        solve_ref[0, t] = solve_t
        solve_ref[1, t] = carry_t
    for p in range(requests):
        cut = slice(p * steps, (p + 1) * steps)
        n = index_ref[3, p]
        a_t = dot(ident, expand(a_ref[cut, :], head_width), NT).astype(BF16)
        value_t = value_t_ref[p]
        reach = dot(a_t, spread(compact[0, p].astype(BF16), steps), NT)
        removed = dot(value_t, spread(compact[1, p].astype(BF16), steps), NT)
        left = jnp.concatenate(
            [
                jnp.concatenate([-reach, jnp.zeros_like(reach)], axis=1),
                jnp.concatenate([-removed, value_t.astype(F32)], axis=1),
            ],
            axis=0,
        )
        at = lax.broadcasted_iota(I32, left.shape, 1) % steps
        left = jnp.where(at < n, left, 0.0).astype(BF16)
        right = jnp.concatenate([expand(b_ref[cut, :], head_width), expand(k_ref[cut, :], head_width)], axis=0)
        both = dot(left, right) * last_ref[p : p + 1, :]
        added_ref[p] = both[head_width:, :].astype(BF16)
        through_ref[p] = both[:head_width, :].astype(BF16)


def spread(x, steps):
    lanes = x.shape[1]
    group = lax.broadcasted_iota(I32, x.shape, 1) // steps
    zero = jnp.zeros_like(x)
    return jnp.concatenate([jnp.where(group == h, x, zero) for h in range(lanes // steps)], axis=0)


def layout_kernel(
    requests, heads, halves, per_peer,
    index_ref, got_ref, unit_first_ref, value_first_ref, edge_ref, picked_ref,
    state_ref, change_ref, edge_out_ref, edge_scratch,
):
    width = unit_first_ref.shape[1]
    head_width = width // heads
    pack = got_ref.shape[1]
    edge_rows = head_width // halves
    ident = ident_of(head_width, width)
    low = lax.broadcasted_iota(I32, (pack, 128), 1) < head_width
    for p in range(requests):
        for c in range(halves):
            for pair in range(heads // 2):
                at = (p * heads + 2 * pair) * halves + c
                even = got_ref[index_ref[2, at]].astype(F32)
                odd = got_ref[index_ref[2, at + halves]].astype(F32)
                top = jnp.where(low, even, pltpu.roll(odd, head_width, 1))
                bottom = jnp.where(low, pltpu.roll(even, head_width, 1), odd)
                lanes = slice(pair * 128, (pair + 1) * 128)
                state_ref[p, 2 * c * pack : (2 * c + 1) * pack, lanes] = top.astype(BF16)
                state_ref[p, (2 * c + 1) * pack : (2 * c + 2) * pack, lanes] = bottom.astype(BF16)
        unit = head_rows(unit_first_ref[p : p + 1, :], heads, head_width, 0).astype(BF16)
        value = head_rows(value_first_ref[p : p + 1, :], heads, head_width, heads).astype(BF16)
        change_ref[p] = (dot(ident, value, NT) - dot(state_ref[p], unit, NT)).astype(BF16)
        new_edge = jnp.where(index_ref[3, p] > 0, picked_ref[p : p + 1, :], edge_ref[p : p + 1, :])
        for k in range(heads * halves):
            lane = k * edge_rows
            line = new_edge[:, lane // 128 * 128 : lane // 128 * 128 + 128]
            if lane % 128:
                line = pltpu.roll(line, 128 - lane % 128, 1)
            edge_scratch[pl.ds(index_ref[1, p * heads * halves + k], 1), :] = line
    for b in range(edge_out_ref.shape[0]):
        block = edge_scratch[b * per_peer : (b + 1) * per_peer, :]
        if per_peer < pack:
            block = jnp.concatenate([block, jnp.zeros((pack - per_peer, 128), F32)], axis=0)
        edge_out_ref[b] = block.astype(BF16)


def state_kernel(
    requests, heads, halves, per_peer, groups,
    index_ref, *refs,
):
    parts_refs = refs[:groups]
    (
        state_ref, change_ref, edge_blocks_ref, unit_first_ref, key_first_ref, last_ref, through_ref, added_ref,
        vector_ref, right_decay_ref, right_rate_ref,
        send_ref, after_ref, key_mod_first_ref,
    ) = refs[groups:]
    width = unit_first_ref.shape[1]
    head_width = width // heads
    pack = send_ref.shape[1]
    rank = right_decay_ref.shape[0]
    total = parts_refs[0][...]
    for ref in parts_refs[1:]:
        total = total + ref[...]
    decay = vector_ref[2:3, :] + dot(jnp.tanh(total[:, :rank]).astype(BF16), right_decay_ref[...])
    forget = jnp.exp(-DECAY_SCALE * jax.nn.sigmoid(decay))
    rate = jax.nn.sigmoid(vector_ref[3:4, :] + dot(total[:, rank:].astype(BF16), right_rate_ref[...]))
    key_mod = key_first_ref[...] * (1.0 + (rate - 1.0) * vector_ref[5:6, :])
    key_mod_first_ref[...] = key_mod
    removal = rate * unit_first_ref[...]
    low = lax.broadcasted_iota(I32, (pack, 128), 1) < head_width
    own = lax.broadcasted_iota(I32, (head_width, 128), 1) < head_width
    for b in range(edge_blocks_ref.shape[0]):
        send_ref[b * (per_peer + 1) + per_peer] = edge_blocks_ref[b]
    for p in range(requests):
        n = index_ref[3, p]
        line = slice(p, p + 1)
        written = head_rows(removal[line, :], heads, head_width, 0) + head_rows(key_mod[line, :], heads, head_width, heads)
        start = state_ref[p].astype(F32)
        change = dot(change_ref[p], written.astype(BF16))
        after = start * forget[line, :] + change
        after_b = after.astype(BF16)
        after_ref[p] = after_b
        parts = []
        for pair in range(heads // 2):
            lanes = slice(pair * 128, (pair + 1) * 128)
            through = through_ref[p, :, lanes]
            zero = jnp.zeros_like(through)
            through = jnp.concatenate([jnp.where(own, through, zero), jnp.where(own, zero, through)], axis=0)
            parts.append(dot(after_b[:, lanes], through))
        kept = after * last_ref[line, :] + jnp.concatenate(parts, axis=1) + added_ref[p].astype(F32)
        kept = jnp.where(n > 0, kept, start)
        for c in range(halves):
            for pair in range(heads // 2):
                top = kept[(2 * c) * pack : (2 * c + 1) * pack, pair * 128 : (pair + 1) * 128]
                bottom = kept[(2 * c + 1) * pack : (2 * c + 2) * pack, pair * 128 : (pair + 1) * 128]
                at = (p * heads + 2 * pair) * halves + c
                even = jnp.where(low, top, pltpu.roll(bottom, head_width, 1))
                odd = jnp.where(low, pltpu.roll(top, head_width, 1), bottom)
                send_ref[index_ref[4, at]] = even.astype(BF16)
                send_ref[index_ref[4, at + halves]] = odd.astype(BF16)


def lines_kernel(gating_ref, *refs):
    *outs, scratch = refs
    requests, part = gating_ref.shape[:2]
    width = scratch.shape[1]
    me = lax.axis_index("head")
    for d, out in enumerate(outs):
        start = pl.multiple_of((me ^ d) * width, 128)
        for p in range(requests):
            scratch[p * part : (p + 1) * part, :] = gating_ref[p, :, pl.ds(start, width)].astype(F32)
        out[...] = scratch[...].astype(BF16)


def read_kernel(
    requests, heads, groups,
    *refs,
):
    return read_body(requests, heads, refs[:groups], *refs[groups:])


def read_body(
    requests, heads,
    recept_refs, scale_ref, key_mod_ref, key_mod_first_ref, a_ref, k_ref, b_ref, solve_ref, state_ref, value_t_ref,
    vector_ref, value_ref,
    result_ref, line_scratch, cross, compact, out_scratch,
):
    rows, width = value_ref.shape
    steps = rows // requests
    head_width = width // heads
    lanes = heads * steps
    part = steps // len(recept_refs)
    row = lax.broadcasted_iota(I32, (rows, rows), 0)
    source = (row % steps // part) ^ lax.axis_index("head")
    source_row = source * (requests * part) + row // steps * part + row % part
    order = (source_row == lax.broadcasted_iota(I32, (rows, rows), 1)).astype(F32).astype(BF16)
    recept = dot(order, jnp.concatenate([ref[...] for ref in recept_refs], axis=0))
    key_mod_first = jnp.broadcast_to(key_mod_first_ref[...][:, None, :], (requests, steps, width)).reshape(rows, width)
    first = lax.broadcasted_iota(I32, (rows, width), 0) % steps == 0
    key_mod = jnp.where(first, key_mod_first, key_mod_ref[...].astype(F32))
    bonus = group_sum(recept * key_mod * vector_ref[6:7, :], head_width)
    line_scratch[...] = (recept * scale_ref[...].astype(F32)).astype(BF16)
    for p in range(requests):
        cut = slice(p * steps, (p + 1) * steps)
        right = jnp.concatenate([expand(k_ref[cut, :], head_width), expand(b_ref[cut, :], head_width)], axis=0)
        cross[p] = dot(line_scratch[cut, :], right, NT)
    lane = lax.broadcasted_iota(I32, (requests, lanes), 1)
    source = lane % steps
    group = lane - source
    for t in range(steps):
        weights = jnp.where(source <= t, cross[:, t, lanes:], 0.0)
        from_a = jnp.zeros((requests, lanes), F32)
        from_v = jnp.where(source <= t, cross[:, t, :lanes], 0.0)
        for s in range(t + 1):
            weight = jnp.take_along_axis(weights, group + s, axis=1)
            from_a = from_a - weight * solve_ref[0, s]
            from_v = from_v - weight * solve_ref[1, s]
        compact[0, :, t, :] = from_a
        compact[1, :, t, :] = from_v
    out_low = lax.broadcasted_iota(I32, (steps, 128), 1) < head_width
    for p in range(requests):
        cut = slice(p * steps, (p + 1) * steps)
        read = jnp.concatenate(
            [spread(compact[0, p].astype(BF16), steps), spread(compact[1, p].astype(BF16), steps)], axis=1
        )
        state = state_ref[p]
        along = dot(state, expand(a_ref[cut, :], head_width), NT).astype(BF16)
        both = jnp.concatenate([along, value_t_ref[p]], axis=1)
        out = dot(read, jnp.concatenate([both, both], axis=0), NT)
        out = out + dot(expand(line_scratch[cut, :], head_width), jnp.concatenate([state, state], axis=0), NT)
        for pair in range(heads // 2):
            at = 2 * pair * steps
            out_scratch[cut, pair * 128 : (pair + 1) * 128] = jnp.where(
                out_low, out[at : at + steps, :], out[at + steps : at + 2 * steps, :]
            )
    out = out_scratch[...]
    centered = out - group_sum(out, head_width) * (1.0 / head_width)
    variance = group_sum(centered * centered, head_width) * (1.0 / head_width)
    line = centered * lax.rsqrt(variance + NORM_EPSILON) * vector_ref[7:8, :] + vector_ref[8:9, :]
    result_ref[...] = (line + bonus * value_ref[...].astype(F32)).astype(BF16)


def place_kernel(per_peer, index_ref, back_ref, out_ref, edge_ref, scratch, edge_scratch, edge_placed):
    slot_dev = out_ref.shape[0]
    pack = back_ref.shape[1]
    for b in range(slot_dev // per_peer):
        block = back_ref[b * (per_peer + 1) + per_peer].astype(F32)
        edge_scratch[b * per_peer : (b + 1) * per_peer, :] = block[:per_peer, :]
    for s in range(slot_dev):
        scratch[s] = back_ref[index_ref[6, s]].astype(F32)
        edge_placed[s : s + 1, :] = edge_scratch[pl.ds(index_ref[5, s], 1), :]
    left = lax.broadcasted_iota(I32, (slot_dev, 128), 1) < 64
    half = pack // 2
    for b in range(half):
        even = scratch[:, 2 * b, :]
        odd = scratch[:, 2 * b + 1, :]
        out_ref[:, b * 128 : (b + 1) * 128] = jnp.where(left, even, pltpu.roll(odd, 64, 1))
        out_ref[:, (half + b) * 128 : (half + b + 1) * 128] = jnp.where(left, pltpu.roll(even, 64, 1), odd)
    edge_ref[...] = jnp.transpose(edge_placed[...])[: edge_ref.shape[0], :]


def local(
    layer_entry_vectors,
    guessed_lookup_vectors,
    guessed_content_vectors,
    gating_query,
    lane_memory_store,
    prior_step_store,
    fading_blend_ratio,
    learning_speed_blend,
    fading_left_factor,
    fading_right_factor,
    fading_offset,
    learning_speed_left,
    learning_speed_right,
    learning_speed_offset,
    erasing_lookup_factor,
    written_lookup_factor,
    present_reward_factors,
    lane_standard_factor,
    lane_standard_offset,
    caller_memory_directory,
    kept_target_place,
    caller_sequence,
    approved_guesses,
):
    blocks = lax.axis_size("blk")
    groups = lax.axis_size("head")
    requests, steps, width = layer_entry_vectors.shape
    heads, halves = caller_memory_directory.shape[1:]
    slot_dev = lane_memory_store.shape[1]
    slot_width = lane_memory_store.shape[2]
    pack = slot_width // 128
    per_peer = slot_dev // blocks
    edge_rows = prior_step_store.shape[2]
    rows = requests * steps
    rank = fading_left_factor.shape[1]
    sds = jax.ShapeDtypeStruct

    def exchange(x, axis):
        return lax.all_to_all(x, axis, split_axis=0, concat_axis=0, tiled=True)

    read_table = caller_memory_directory.transpose(1, 2, 0)
    write_table = kept_target_place.transpose(1, 2, 0)
    sent = call(
        functools.partial(send_kernel, blocks, requests, per_peer),
        pltpu.HBM((blocks * (per_peer + 1), pack, 128), BF16),
        raw=(caller_sequence, read_table, lane_memory_store[0], prior_step_store[0].T),
        scratch=[
            pltpu.SMEM(caller_sequence.shape, I32),
            pltpu.VMEM(read_table.shape, I32),
            pltpu.VMEM((slot_dev, slot_width), F32),
            pltpu.VMEM((edge_rows, slot_dev), F32),
            pltpu.VMEM((slot_dev, pack, 128), F32),
            pltpu.VMEM((slot_dev, slot_dev), F32),
            pltpu.SemaphoreType.DMA((4,)),
        ],
    )
    got = exchange(sent.reshape(blocks, (per_peer + 1) * pack, 128), "blk")
    got = got.reshape(blocks * (per_peer + 1), pack, 128)
    layer = layer_entry_vectors.reshape(rows, width)
    key = guessed_lookup_vectors.reshape(rows, width)
    value = guessed_content_vectors.reshape(rows, width)
    vectors = (
        fading_blend_ratio, learning_speed_blend, fading_offset, learning_speed_offset, erasing_lookup_factor,
        written_lookup_factor, present_reward_factors, lane_standard_factor, lane_standard_offset,
    )
    arrays = (fading_left_factor.T, learning_speed_left.T, fading_right_factor, learning_speed_right)
    one = sds((requests, width), F32)
    wide = sds((rows, width), BF16)
    left = sds((rank, width), BF16)
    (
        index, partial_sums, first_lines, picked, vector,
        left_decay, left_rate, right_decay, right_rate,
    ) = call(
        functools.partial(early_kernel, blocks, requests, per_peer, len(vectors)),
        (
            sds((8, slot_dev), I32), sds((rows, 2 * rank), BF16), one, one,
            sds((16, width), F32), left, left, left, left,
        ),
        raw=(
            caller_sequence, approved_guesses, read_table, write_table,
            *(x.reshape(1, width) for x in vectors), layer, *arrays,
        ),
        scratch=[
            pltpu.SMEM(caller_sequence.shape, I32),
            pltpu.SMEM(approved_guesses.shape, I32),
            pltpu.VMEM(read_table.shape, I32),
            pltpu.VMEM(write_table.shape, I32),
            pltpu.VMEM((rows, width), BF16),
            pltpu.VMEM((rows, width), F32),
            pltpu.VMEM((heads * halves, write_table.shape[2]), I32),
            pltpu.SemaphoreType.DMA((5,)),
            pltpu.SemaphoreType.DMA((len(vectors),)),
            pltpu.SemaphoreType.DMA((len(arrays),)),
        ],
    )
    parts = lax.all_gather(partial_sums, "head", axis=0)

    head_width = width // heads
    (
        a_lines, k_lines, b_lines, scale, key_mod, last, value_t, solve,
        unit_first, key_first, value_first, through, added,
    ) = call(
        functools.partial(prepare_kernel, requests, heads),
        (
            wide, wide, wide, wide, wide, one,
            sds((requests, head_width, heads * steps), BF16),
            sds((2, steps, requests, heads * steps), F32),
            one, one, one,
            sds((requests, head_width, width), BF16),
            sds((requests, head_width, width), BF16),
        ),
        scalars=(index,),
        near=(parts, vector, right_decay, right_rate),
        far=(key, value),
        held=(first_lines, picked, left_decay, left_rate),
        scratch=[
            pltpu.VMEM((requests, steps, 2 * heads * steps), F32),
            pltpu.VMEM((2, requests, steps, heads * steps), F32),
            pltpu.VMEM((rows, width), F32),
            pltpu.VMEM((rows, width), F32),
        ],
    )
    read_later = (scale, key_mod, a_lines, k_lines, b_lines, solve, value_t)
    state_later = (vector, right_decay, right_rate, key_first, last, through, added)
    first_sums, edge = call(
        functools.partial(first_kernel, requests, heads, halves, per_peer),
        (sds((requests, 2 * rank), F32), one),
        scalars=(index,),
        near=(got, first_lines, vector, left_decay, left_rate),
        held=(unit_first, value_first, picked, *state_later[1:], *read_later),
        scratch=[pltpu.VMEM((slot_dev, 128), F32)],
    )
    first_parts = [first_sums] + [
        lax.ppermute(first_sums, "head", [(g, g ^ d) for g in range(groups)]) for d in range(1, groups)
    ]
    state, change, edge_blocks = call(
        functools.partial(layout_kernel, requests, heads, halves, per_peer),
        (
            sds((requests, head_width, width), BF16),
            sds((requests, head_width, 2 * heads), BF16),
            sds((blocks, pack, 128), BF16),
        ),
        scalars=(index,),
        near=(got, unit_first, value_first, edge, picked),
        held=(*state_later, *read_later),
        scratch=[pltpu.VMEM((slot_dev, 128), F32)],
    )
    back, after, key_mod_first = call(
        functools.partial(state_kernel, requests, heads, halves, per_peer, groups),
        (
            pltpu.HBM((blocks * (per_peer + 1), pack, 128), BF16),
            sds((requests, head_width, width), BF16),
            one,
        ),
        scalars=(index,),
        near=(
            *first_parts, state, change, edge_blocks, unit_first, key_first, last, through, added,
            vector, right_decay, right_rate,
        ),
        held=read_later,
    )
    back = exchange(back.reshape(blocks, (per_peer + 1) * pack, 128), "blk")
    back = back.reshape(blocks * (per_peer + 1), pack, 128)
    recept = call(
        lines_kernel,
        (sds((rows // groups, width), BF16),) * groups,
        far=(gating_query,),
        held=(index, vector, after, key_mod_first, *read_later),
        scratch=[pltpu.VMEM((rows // groups, width), F32)],
    )
    recept = [recept[0]] + [
        lax.ppermute(recept[d], "head", [(g, g ^ d) for g in range(groups)]) for d in range(1, groups)
    ]
    result = call(
        functools.partial(read_kernel, requests, heads, groups),
        pltpu.HBM((rows, width), BF16),
        near=(*recept, scale, key_mod, key_mod_first, a_lines, k_lines, b_lines, solve, after, value_t, vector),
        far=(value,),
        held=(index,),
        scratch=[
            pltpu.VMEM((rows, width), BF16),
            pltpu.VMEM((requests, steps, 2 * heads * steps), F32),
            pltpu.VMEM((2, requests, steps, heads * steps), F32),
            pltpu.VMEM((rows, width), F32),
        ],
    )
    new_states, new_edges = call(
        functools.partial(place_kernel, per_peer),
        (pltpu.HBM((slot_dev, slot_width), F32), pltpu.HBM((edge_rows, slot_dev), F32)),
        scalars=(index,),
        near=(back,),
        scratch=[
            pltpu.VMEM((slot_dev, pack, 128), F32),
            pltpu.VMEM((slot_dev, 128), F32),
            pltpu.VMEM((slot_dev, 128), F32),
        ],
    )
    return (result.reshape(requests, steps, width), new_states[None], new_edges.T[None])


def solution(mesh):
    return jax.shard_map(
        local,
        mesh=mesh,
        in_specs=(
            P("blk", None, "head"),
            P("blk", None, "head"),
            P("blk", None, "head"),
            P("blk", "head", None),
            P("head", "blk", None),
            P("head", "blk", None),
            P("head"),
            P("head"),
            P("head", None),
            P(None, "head"),
            P("head"),
            P("head", None),
            P(None, "head"),
            P("head"),
            P("head"),
            P("head"),
            P("head"),
            P("head"),
            P("head"),
            P(None, "head", None),
            P(None, "head", None),
            P(),
            P(),
        ),
        out_specs=(P("blk", None, "head"), P("head", "blk", None), P("head", "blk", None)),
        check_vma=False,
    )
```

```python
import functools

import jax
import jax.numpy as jnp
from jax import lax
from jax.experimental import pallas as pl
from jax.experimental.pallas import tpu as pltpu
from jax.sharding import PartitionSpec as P

EPSILON = 1e-05
NORM_EPSILON = 0.00064
DECAY_SCALE = 0.6065306597126334
F32 = jnp.float32
BF16 = jnp.bfloat16
I32 = jnp.int32
NT = (((1,), (1,)), ((), ()))
NN = (((1,), (0,)), ((), ()))


def call(kernel, outs, scalars=(), near=(), far=(), raw=(), held=(), scratch=(), raw_outs=(), vmem=16):
    reads = len(scalars) + len(near) + len(far) + len(raw)

    def body(*refs):
        kernel(*refs[:reads], *refs[reads + len(held) :])

    args = [*scalars]
    args += [*near]
    args += [pltpu.with_memory_space_constraint(x, pltpu.HBM) for x in (*far, *raw)]
    specs = [pl.BlockSpec(memory_space=pltpu.SMEM)] * len(scalars)
    specs += [pl.BlockSpec(memory_space=pltpu.VMEM)] * (len(near) + len(far))
    specs += [pl.BlockSpec(memory_space=pltpu.HBM)] * (len(raw) + len(held))
    return pl.pallas_call(
        body,
        out_shape=outs,
        in_specs=specs,
        out_specs=tuple(
            pl.BlockSpec(memory_space=pltpu.HBM if i in raw_outs else pltpu.VMEM) for i in range(len(outs))
        ),
        scratch_shapes=list(scratch),
        compiler_params=pltpu.CompilerParams(vmem_limit_bytes=vmem * 1024 * 1024),
        cost_estimate=pl.CostEstimate(flops=1 << 20, bytes_accessed=1 << 20, transcendentals=0),
    )(*args, *held)


def dot(a, b, dims=NN):
    return lax.dot_general(a, b, dims, preferred_element_type=F32)


def split(x):
    high = x.astype(BF16)
    return high, (x - high.astype(F32)).astype(BF16)


def group_sum(x, width):
    rows, lanes = x.shape
    block = max(width, 128)
    ones = (
        lax.broadcasted_iota(I32, (block, block), 0) // width
        == lax.broadcasted_iota(I32, (block, block), 1) // width
    ).astype(BF16)
    high, low = split(x)
    parts = []
    for start in range(0, lanes, block):
        cut = slice(start, start + block)
        parts.append(dot(high[:, cut], ones) + dot(low[:, cut], ones))
    return jnp.concatenate(parts, axis=1)


def order_of(blocks):
    return (2, 3, 1, 0, 4, 5, 7, 6) if blocks == 8 else tuple(range(blocks))


def seat_of(block, blocks):
    order = order_of(blocks)
    if order == tuple(range(blocks)):
        return block
    seat = jnp.zeros_like(block)
    for i, b in enumerate(order):
        seat = jnp.where(block == b, i, seat)
    return seat


def positions(seq_ref, count):
    lane = lax.broadcasted_iota(I32, (1, count), 1)

    def block(b, acc):
        for k in range(8):
            acc = jnp.where(lane == seq_ref[b * 8 + k], b * 8 + k, acc)
        return acc

    return lax.fori_loop(0, count // 8, block, jnp.zeros((1, count), I32))


def place_of_slot(table_ref, position, base, blocks, per_peer, requests, slot_dev):
    heads, halves, count = table_ref.shape
    slot = lax.broadcasted_iota(I32, (slot_dev, count), 0) + base
    named = jnp.zeros((slot_dev, count), F32)
    for h in range(heads):
        for c in range(halves):
            named = jnp.where(table_ref[h, c : c + 1, :] == slot, 1.0, named)
    other_of = jnp.broadcast_to(seat_of(position // requests, blocks), (16, count)).astype(F32).astype(BF16)
    other = dot(other_of, named.astype(BF16), NT)[0:1, :].astype(I32)
    rows = max(16, blocks)
    mask = other == lax.broadcasted_iota(I32, (rows, slot_dev), 0)
    before = (
        lax.broadcasted_iota(I32, (slot_dev, slot_dev), 0)
        < lax.broadcasted_iota(I32, (slot_dev, slot_dev), 1)
    ).astype(F32).astype(BF16)
    ahead = dot(mask.astype(F32).astype(BF16), before)
    rank = jnp.sum(jnp.where(mask, ahead, 0.0), axis=0, keepdims=True).astype(I32)
    return other * per_peer + rank


def place_of_item(table_ref, lines_ref, position, first, blocks, requests, slot_dev):
    heads, halves, count = table_ref.shape
    per_item = heads * halves
    items = requests * per_item
    mine = (
        jnp.broadcast_to(position, (16, count)) - first == lax.broadcasted_iota(I32, (16, count), 0)
    ).astype(F32).astype(BF16)
    for h in range(heads):
        lines_ref[h * halves : (h + 1) * halves, :] = table_ref[h]
    lines = lines_ref[...]
    lane = lax.broadcasted_iota(I32, (16, items), 1)
    owner = lax.broadcasted_iota(I32, (16, items), 0) == lane // per_item
    of_item = (
        lax.broadcasted_iota(I32, (per_item, items), 0) == lax.broadcasted_iota(I32, (per_item, items), 1) % per_item
    ).astype(F32).astype(BF16)
    seats = seat_of(lines // slot_dev, blocks)
    high = dot(dot(mine, seats.astype(F32).astype(BF16), NT).astype(BF16), of_item)
    low = dot(dot(mine, (lines % slot_dev).astype(F32).astype(BF16), NT).astype(BF16), of_item)
    slots = high * slot_dev + low
    row = jnp.sum(jnp.where(owner, slots, 0.0), axis=0, keepdims=True)
    diagonal = lax.broadcasted_iota(I32, (items, items), 0) == lax.broadcasted_iota(I32, (items, items), 1)
    column = jnp.sum(jnp.where(diagonal, row, 0.0), axis=1, keepdims=True)
    return jnp.sum((column < row).astype(F32), axis=0, keepdims=True).astype(I32)


def send_kernel(
    blocks, requests, per_peer, pieces,
    seq_hbm, read_hbm, state_hbm, edge_hbm,
    out_hbm,
    seq_ref, read_ref, state_ref, edge_ref, scratch, edge_scratch, out_ref, sems, state_sems, out_sems,
):
    slot_dev, slot_width = state_ref.shape
    pack = out_ref.shape[1]
    me = lax.axis_index("blk")
    sources = (seq_hbm, read_hbm, edge_hbm)
    targets = (seq_ref, read_ref, edge_ref)
    copies = [pltpu.make_async_copy(a, b, sems.at[i]) for i, (a, b) in enumerate(zip(sources, targets))]
    state_copies = []
    piece = slot_width // 2 // pieces
    for i in range(pieces):
        for start in (i * piece, slot_width // 2 + i * piece):
            cut = (slice(None), pl.ds(start, piece))
            state_copies.append(
                pltpu.make_async_copy(state_hbm.at[cut], state_ref.at[cut], state_sems.at[len(state_copies)])
            )
    for copy in (*copies[:2], *state_copies, copies[2]):
        copy.start()
    copies[0].wait()
    copies[1].wait()
    position = positions(seq_ref, read_ref.shape[2])
    place = place_of_slot(read_ref, position, me * slot_dev, blocks, per_peer, requests, slot_dev)
    pick = (place == lax.broadcasted_iota(I32, (slot_dev, slot_dev), 0)).astype(F32).astype(BF16)
    left = lax.broadcasted_iota(I32, (slot_dev, 128), 1) < 64
    half = pack // 2
    for b in range(half):
        if b % (half // pieces) == 0:
            state_copies[b // (half // pieces) * 2].wait()
            state_copies[b // (half // pieces) * 2 + 1].wait()
        x = dot(pick, state_ref[:, b * 128 : (b + 1) * 128].astype(BF16))
        y = dot(pick, state_ref[:, (half + b) * 128 : (half + b + 1) * 128].astype(BF16))
        scratch[:, 2 * b, :] = jnp.where(left, x, pltpu.roll(y, 64, 1))
        scratch[:, 2 * b + 1, :] = jnp.where(left, pltpu.roll(x, 64, 1), y)
    copies[2].wait()
    edge_rows = edge_ref.shape[0]
    edges = jnp.concatenate([edge_ref[...], jnp.zeros((slot_dev - edge_rows, slot_dev), F32)], axis=0)
    edge_scratch[...] = dot(pick, edges.astype(BF16), NT)
    out_copies = []
    for b in range(blocks):
        at = b * (per_peer + 1)
        out_ref[at : at + per_peer] = scratch[b * per_peer : (b + 1) * per_peer].astype(BF16)
        block = edge_scratch[b * per_peer : (b + 1) * per_peer, :]
        if per_peer < pack:
            block = jnp.concatenate([block, jnp.zeros((pack - per_peer, 128), F32)], axis=0)
        out_ref[at + per_peer] = block.astype(BF16)
        if (b + 1) % (blocks // 8) == 0:
            cut = pl.ds((b + 1 - blocks // 8) * (per_peer + 1), blocks // 8 * (per_peer + 1))
            out_copies.append(pltpu.make_async_copy(out_ref.at[cut], out_hbm.at[cut], out_sems.at[len(out_copies)]))
            out_copies[-1].start()
    for copy in out_copies:
        copy.wait()


def shift_kernel(requests, lines, *refs):
    scalars_hbm, refs = refs[:2], refs[2:]
    vectors_hbm, refs = refs[:lines], refs[lines:]
    arrays_hbm, refs = refs[:5], refs[5:]
    partial_ref, first_ref, picked_ref, vector_ref = refs[:4]
    arrays, refs = refs[4:8], refs[8:]
    seq_ref, count_ref, layer_ref, line_scratch, sems, line_sem, array_sem = refs
    pairs = zip((*scalars_hbm, arrays_hbm[0]), (seq_ref, count_ref, layer_ref))
    copies = [pltpu.make_async_copy(a, b, sems.at[i]) for i, (a, b) in enumerate(pairs)]
    line_copies = [
        pltpu.make_async_copy(a, vector_ref.at[pl.ds(i, 1)], line_sem.at[i]) for i, a in enumerate(vectors_hbm)
    ]
    array_copies = [
        pltpu.make_async_copy(a, b, array_sem.at[i]) for i, (a, b) in enumerate(zip(arrays_hbm[1:], arrays))
    ]
    for copy in (copies[2], *line_copies[:2], *array_copies, *copies[:2], *line_copies[2:]):
        copy.start()
    copies[2].wait()
    steps = layer_ref.shape[0] // requests
    line = layer_ref[...].astype(F32)
    line_scratch[...] = line
    delta = pltpu.roll(line, 1, 0) - line
    left_decay_ref, left_rate_ref = arrays[:2]
    rank = left_decay_ref.shape[0]
    for copy in (*line_copies, *array_copies, *copies[:2]):
        copy.wait()
    mixed_decay = (line + delta * vector_ref[0:1, :]).astype(BF16)
    mixed_rate = (line + delta * vector_ref[1:2, :]).astype(BF16)
    partial_ref[:, :rank] = dot(mixed_decay, left_decay_ref[...], NT).astype(BF16)
    partial_ref[:, rank:] = dot(mixed_rate, left_rate_ref[...], NT).astype(BF16)
    first = lax.axis_index("blk") * requests
    for p in range(requests):
        first_ref[p : p + 1, :] = line_scratch[p * steps : p * steps + 1, :]
        n = count_ref[seq_ref[first + p]]
        picked_ref[p : p + 1, :] = line_scratch[pl.ds(p * steps + jnp.maximum(n - 1, 0), 1), :]


def index_kernel(blocks, requests, per_peer, heads, vector_ref, *refs):
    hbm, refs = refs[:6], refs[6:]
    index_ref, key_ref, unit_ref, value_t_ref, unit_first_ref, key_first_ref, value_first_ref, *refs = refs
    seq_ref, count_ref, read_ref, write_ref, value_ref, lines_ref, sems = refs
    targets = (seq_ref, count_ref, read_ref, write_ref, key_ref, value_ref)
    copies = [pltpu.make_async_copy(a, b, sems.at[i]) for i, (a, b) in enumerate(zip(hbm, targets))]
    for copy in copies:
        copy.start()
    for copy in copies[:4]:
        copy.wait()
    slot_dev = index_ref.shape[1]
    me = lax.axis_index("blk")
    first = me * requests
    position = positions(seq_ref, read_ref.shape[2])
    place_in = place_of_item(read_ref, lines_ref, position, first, blocks, requests, slot_dev)
    place_out = place_of_item(write_ref, lines_ref, position, first, blocks, requests, slot_dev)
    target = place_of_slot(write_ref, position, me * slot_dev, blocks, per_peer, requests, slot_dev)
    lane = lax.broadcasted_iota(I32, (1, slot_dev), 1)
    counts = jnp.zeros((1, slot_dev), I32)
    for p in range(requests):
        counts = jnp.where(lane == p, count_ref[seq_ref[first + p]], counts)
    index_ref[0:1, :] = place_in
    index_ref[1:2, :] = place_out
    index_ref[2:3, :] = place_in + place_in // per_peer
    index_ref[3:4, :] = counts
    index_ref[4:5, :] = place_out + place_out // per_peer
    index_ref[5:6, :] = target
    index_ref[6:7, :] = target + target // per_peer
    index_ref[7:8, :] = jnp.zeros((1, slot_dev), I32)
    copies[4].wait()
    copies[5].wait()
    rows, width = key_ref.shape
    steps = rows // requests
    head_width = width // heads
    u = key_ref[...].astype(F32) * vector_ref[4:5, :]
    unit_ref[...] = u * lax.rsqrt(group_sum(u * u, head_width) + EPSILON)
    ident = ident_of(head_width, width)
    for p in range(requests):
        cut = slice(p * steps, (p + 1) * steps)
        line = slice(p, p + 1)
        unit_first_ref[line, :] = unit_ref[p * steps : p * steps + 1, :]
        key_first_ref[line, :] = key_ref[cut, :].astype(F32)[0:1, :]
        value_first_ref[line, :] = value_ref[cut, :].astype(F32)[0:1, :]
        value_t_ref[p] = dot(ident, expand(value_ref[cut, :], head_width), NT).astype(BF16)


def first_kernel(
    requests, heads, halves, per_peer,
    index_ref, got_ref, first_ref, vector_ref, left_decay_ref, left_rate_ref,
    out_ref, edge_ref, pool_scratch,
):
    slot_dev = pool_scratch.shape[0]
    rows = first_ref.shape[1] // (heads * halves)
    for b in range(slot_dev // per_peer):
        block = got_ref[b * (per_peer + 1) + per_peer].astype(F32)
        pool_scratch[b * per_peer : (b + 1) * per_peer, :] = block[:per_peer, :]
    for p in range(requests):
        for k in range(heads * halves):
            place = index_ref[0, p * heads * halves + k]
            edge_ref[p : p + 1, k * rows : (k + 1) * rows] = pool_scratch[pl.ds(place, 1), :rows]
    line = first_ref[...]
    delta = edge_ref[...] - line
    rank = left_decay_ref.shape[0]
    mixed_decay = (line + delta * vector_ref[0:1, :]).astype(BF16)
    mixed_rate = (line + delta * vector_ref[1:2, :]).astype(BF16)
    out_ref[:, :rank] = dot(mixed_decay, left_decay_ref[...], NT)
    out_ref[:, rank:] = dot(mixed_rate, left_rate_ref[...], NT)


def expand(x, head_width):
    steps, lanes = x.shape
    heads = lanes // head_width
    per_block = 128 // head_width
    lane = lax.broadcasted_iota(I32, (steps, 128), 1) // head_width
    zero = jnp.zeros((steps, 128), x.dtype)
    lines = []
    for h in range(heads):
        own = h // per_block
        block = jnp.where(lane == h % per_block, x[:, own * 128 : (own + 1) * 128], zero)
        lines.append(jnp.concatenate([block if b == own else zero for b in range(lanes // 128)], axis=1))
    return jnp.concatenate(lines, axis=0)


def ident_of(head_width, width):
    return (
        lax.broadcasted_iota(I32, (head_width, width), 0)
        == lax.broadcasted_iota(I32, (head_width, width), 1) % head_width
    ).astype(F32).astype(BF16)


def head_rows(line, heads, head_width, shift):
    shape = (2 * heads, line.shape[1])
    own = lax.broadcasted_iota(I32, shape, 1) // head_width + shift
    return jnp.where(own == lax.broadcasted_iota(I32, shape, 0), jnp.broadcast_to(line, shape), 0.0)


def prepare_kernel(
    requests, heads, groups,
    index_ref, *refs,
):
    parts_refs = refs[:groups]
    (
        vector_ref, right_decay_ref, right_rate_ref, key_ref, unit_ref, value_t_ref,
        a_ref, k_ref, b_ref, scale_ref, key_mod_ref, last_ref, solve_ref, through_ref, added_ref,
        cross, compact, cum_ref,
    ) = refs[groups:]
    rows, width = key_ref.shape
    steps = rows // requests
    head_width = width // heads
    rank = right_decay_ref.shape[0]
    total = parts_refs[0][...].astype(F32)
    for ref in parts_refs[1:]:
        total = total + ref[...].astype(F32)
    hidden = jnp.tanh(total[:, :rank]).astype(BF16)
    rate_hidden = total[:, rank:].astype(BF16)
    decay = vector_ref[2:3, :] + dot(hidden, right_decay_ref[...])
    step = lax.broadcasted_iota(I32, (rows, width), 0) % steps
    later = step > 0
    log_forget = jnp.where(later, -DECAY_SCALE * jax.nn.sigmoid(decay), 0.0)
    rate = jax.nn.sigmoid(vector_ref[3:4, :] + dot(rate_hidden, right_rate_ref[...]))
    key = key_ref[...].astype(F32)
    unit = unit_ref[...]
    key_mod = key * (1.0 + (rate - 1.0) * vector_ref[5:6, :])
    key_mod_ref[...] = key_mod.astype(BF16)
    cum = log_forget
    shift = 1
    while shift < steps:
        cum = cum + jnp.where(step >= shift, pltpu.roll(cum, shift, 0), 0.0)
        shift *= 2
    grow = jnp.where(later, jnp.exp(-cum), 0.0)
    cum_ref[...] = cum
    scale_ref[...] = jnp.exp(cum).astype(BF16)
    a_ref[...] = jnp.where(later, unit * jnp.exp(cum - log_forget), 0.0).astype(BF16)
    k_ref[...] = (key_mod * grow).astype(BF16)
    b_ref[...] = (rate * unit * grow).astype(BF16)
    ident = ident_of(head_width, width)
    lanes = heads * steps
    for p in range(requests):
        cut = slice(p * steps, (p + 1) * steps)
        n = index_ref[3, p]
        at_n = cum_ref[pl.ds(p * steps + jnp.maximum(n - 1, 0), 1), :]
        last_ref[p : p + 1, :] = jnp.where(n > 0, jnp.exp(at_n), 1.0)
        right = jnp.concatenate([expand(k_ref[cut, :], head_width), expand(b_ref[cut, :], head_width)], axis=0)
        cross[p] = dot(a_ref[cut, :], right, NT)
    lane = lax.broadcasted_iota(I32, (requests, lanes), 1)
    source = lane % steps
    group = lane - source
    solve, carry = [], []
    for t in range(steps):
        weights = jnp.where(source < t, cross[:, t, lanes:], 0.0)
        solve_t = jnp.where(source == t, 1.0, 0.0)
        carry_t = jnp.where(source < t, cross[:, t, :lanes], 0.0)
        for s in range(t):
            weight = jnp.take_along_axis(weights, group + s, axis=1)
            solve_t = solve_t - weight * solve[s]
            carry_t = carry_t - weight * carry[s]
        solve.append(solve_t)
        carry.append(carry_t)
        compact[0, :, t, :] = solve_t
        compact[1, :, t, :] = carry_t
        solve_ref[0, t] = solve_t
        solve_ref[1, t] = carry_t
    for p in range(requests):
        cut = slice(p * steps, (p + 1) * steps)
        n = index_ref[3, p]
        a_t = dot(ident, expand(a_ref[cut, :], head_width), NT).astype(BF16)
        value_t = value_t_ref[p]
        reach = dot(a_t, spread(compact[0, p].astype(BF16), steps), NT)
        removed = dot(value_t, spread(compact[1, p].astype(BF16), steps), NT)
        left = jnp.concatenate(
            [
                jnp.concatenate([-reach, jnp.zeros_like(reach)], axis=1),
                jnp.concatenate([-removed, value_t.astype(F32)], axis=1),
            ],
            axis=0,
        )
        at = lax.broadcasted_iota(I32, left.shape, 1) % steps
        left = jnp.where(at < n, left, 0.0).astype(BF16)
        right = jnp.concatenate([expand(b_ref[cut, :], head_width), expand(k_ref[cut, :], head_width)], axis=0)
        both = dot(left, right) * last_ref[p : p + 1, :]
        added_ref[p] = both[head_width:, :].astype(BF16)
        through_ref[p] = both[:head_width, :].astype(BF16)


def spread(x, steps):
    lanes = x.shape[1]
    group = lax.broadcasted_iota(I32, x.shape, 1) // steps
    zero = jnp.zeros_like(x)
    return jnp.concatenate([jnp.where(group == h, x, zero) for h in range(lanes // steps)], axis=0)


def layout_kernel(
    requests, heads, halves, per_peer,
    index_ref, got_ref, unit_first_ref, value_first_ref, edge_ref, picked_ref,
    state_ref, change_ref, edge_out_ref, edge_scratch,
):
    width = unit_first_ref.shape[1]
    head_width = width // heads
    pack = got_ref.shape[1]
    edge_rows = head_width // halves
    ident = ident_of(head_width, width)
    low = lax.broadcasted_iota(I32, (pack, 128), 1) < head_width
    for p in range(requests):
        for c in range(halves):
            for pair in range(heads // 2):
                at = (p * heads + 2 * pair) * halves + c
                even = got_ref[index_ref[2, at]].astype(F32)
                odd = got_ref[index_ref[2, at + halves]].astype(F32)
                top = jnp.where(low, even, pltpu.roll(odd, head_width, 1))
                bottom = jnp.where(low, pltpu.roll(even, head_width, 1), odd)
                lanes = slice(pair * 128, (pair + 1) * 128)
                state_ref[p, 2 * c * pack : (2 * c + 1) * pack, lanes] = top.astype(BF16)
                state_ref[p, (2 * c + 1) * pack : (2 * c + 2) * pack, lanes] = bottom.astype(BF16)
        unit = head_rows(unit_first_ref[p : p + 1, :], heads, head_width, 0).astype(BF16)
        value = head_rows(value_first_ref[p : p + 1, :], heads, head_width, heads).astype(BF16)
        change_ref[p] = (dot(ident, value, NT) - dot(state_ref[p], unit, NT)).astype(BF16)
        new_edge = jnp.where(index_ref[3, p] > 0, picked_ref[p : p + 1, :], edge_ref[p : p + 1, :])
        for k in range(heads * halves):
            lane = k * edge_rows
            line = new_edge[:, lane // 128 * 128 : lane // 128 * 128 + 128]
            if lane % 128:
                line = pltpu.roll(line, 128 - lane % 128, 1)
            edge_scratch[pl.ds(index_ref[1, p * heads * halves + k], 1), :] = line
    for b in range(edge_out_ref.shape[0]):
        block = edge_scratch[b * per_peer : (b + 1) * per_peer, :]
        if per_peer < pack:
            block = jnp.concatenate([block, jnp.zeros((pack - per_peer, 128), F32)], axis=0)
        edge_out_ref[b] = block.astype(BF16)


def state_kernel(
    requests, heads, halves, per_peer, groups,
    index_ref, *refs,
):
    parts_refs = refs[:groups]
    (
        state_ref, change_ref, edge_blocks_ref, unit_first_ref, key_first_ref, last_ref, through_ref, added_ref,
        vector_ref, right_decay_ref, right_rate_ref,
        send_ref, after_ref, key_mod_first_ref,
        kept_ref,
    ) = refs[groups:]
    width = unit_first_ref.shape[1]
    head_width = width // heads
    pack = send_ref.shape[1]
    rank = right_decay_ref.shape[0]
    total = parts_refs[0][...]
    for ref in parts_refs[1:]:
        total = total + ref[...]
    decay = vector_ref[2:3, :] + dot(jnp.tanh(total[:, :rank]).astype(BF16), right_decay_ref[...])
    forget = jnp.exp(-DECAY_SCALE * jax.nn.sigmoid(decay))
    rate = jax.nn.sigmoid(vector_ref[3:4, :] + dot(total[:, rank:].astype(BF16), right_rate_ref[...]))
    key_mod = key_first_ref[...] * (1.0 + (rate - 1.0) * vector_ref[5:6, :])
    key_mod_first_ref[...] = key_mod
    removal = rate * unit_first_ref[...]
    low = lax.broadcasted_iota(I32, (pack, 128), 1) < head_width
    own = lax.broadcasted_iota(I32, (head_width, 128), 1) < head_width
    for b in range(edge_blocks_ref.shape[0]):
        send_ref[b * (per_peer + 1) + per_peer] = edge_blocks_ref[b]
    for p in range(requests):
        line = slice(p, p + 1)
        written = head_rows(removal[line, :], heads, head_width, 0) + head_rows(key_mod[line, :], heads, head_width, heads)
        change = dot(change_ref[p], written.astype(BF16))
        after = state_ref[p].astype(F32) * forget[line, :] + change
        after_ref[p] = after.astype(BF16)
        kept_ref[p] = after * last_ref[line, :] + added_ref[p].astype(F32)
    for p in range(requests):
        parts = []
        for pair in range(heads // 2):
            lanes = slice(pair * 128, (pair + 1) * 128)
            through = through_ref[p, :, lanes]
            zero = jnp.zeros_like(through)
            through = jnp.concatenate([jnp.where(own, through, zero), jnp.where(own, zero, through)], axis=0)
            parts.append(dot(after_ref[p, :, lanes], through))
        kept = kept_ref[p] + jnp.concatenate(parts, axis=1)
        kept = jnp.where(index_ref[3, p] > 0, kept, state_ref[p].astype(F32))
        for c in range(halves):
            for pair in range(heads // 2):
                top = kept[(2 * c) * pack : (2 * c + 1) * pack, pair * 128 : (pair + 1) * 128]
                bottom = kept[(2 * c + 1) * pack : (2 * c + 2) * pack, pair * 128 : (pair + 1) * 128]
                at = (p * heads + 2 * pair) * halves + c
                even = jnp.where(low, top, pltpu.roll(bottom, head_width, 1))
                odd = jnp.where(low, pltpu.roll(top, head_width, 1), bottom)
                send_ref[index_ref[4, at]] = even.astype(BF16)
                send_ref[index_ref[4, at + halves]] = odd.astype(BF16)


def lines_kernel(gating_ref, *refs):
    *outs, scratch = refs
    requests, part = gating_ref.shape[:2]
    width = scratch.shape[1]
    me = lax.axis_index("head")
    for d, out in enumerate(outs):
        start = pl.multiple_of((me ^ d) * width, 128)
        for p in range(requests):
            scratch[p * part : (p + 1) * part, :] = gating_ref[p, :, pl.ds(start, width)].astype(F32)
        out[...] = scratch[...].astype(BF16)


def read_kernel(
    requests, heads, groups,
    *refs,
):
    return read_body(requests, heads, refs[:groups], *refs[groups:])


def read_body(
    requests, heads,
    recept_refs, scale_ref, key_mod_ref, key_mod_first_ref, a_ref, k_ref, b_ref, solve_ref, state_ref, value_t_ref,
    vector_ref, value_ref,
    result_ref, line_scratch, cross, compact, out_scratch,
):
    rows, width = value_ref.shape
    steps = rows // requests
    head_width = width // heads
    lanes = heads * steps
    part = steps // len(recept_refs)
    row = lax.broadcasted_iota(I32, (rows, rows), 0)
    source = (row % steps // part) ^ lax.axis_index("head")
    source_row = source * (requests * part) + row // steps * part + row % part
    order = (source_row == lax.broadcasted_iota(I32, (rows, rows), 1)).astype(F32).astype(BF16)
    recept = dot(order, jnp.concatenate([ref[...] for ref in recept_refs], axis=0))
    key_mod_first = jnp.broadcast_to(key_mod_first_ref[...][:, None, :], (requests, steps, width)).reshape(rows, width)
    first = lax.broadcasted_iota(I32, (rows, width), 0) % steps == 0
    key_mod = jnp.where(first, key_mod_first, key_mod_ref[...].astype(F32))
    bonus = group_sum(recept * key_mod * vector_ref[6:7, :], head_width)
    line_scratch[...] = (recept * scale_ref[...].astype(F32)).astype(BF16)
    for p in range(requests):
        cut = slice(p * steps, (p + 1) * steps)
        right = jnp.concatenate([expand(k_ref[cut, :], head_width), expand(b_ref[cut, :], head_width)], axis=0)
        cross[p] = dot(line_scratch[cut, :], right, NT)
    lane = lax.broadcasted_iota(I32, (requests, lanes), 1)
    source = lane % steps
    group = lane - source
    for t in range(steps):
        weights = jnp.where(source <= t, cross[:, t, lanes:], 0.0)
        from_a = jnp.zeros((requests, lanes), F32)
        from_v = jnp.where(source <= t, cross[:, t, :lanes], 0.0)
        for s in range(t + 1):
            weight = jnp.take_along_axis(weights, group + s, axis=1)
            from_a = from_a - weight * solve_ref[0, s]
            from_v = from_v - weight * solve_ref[1, s]
        compact[0, :, t, :] = from_a
        compact[1, :, t, :] = from_v
    out_low = lax.broadcasted_iota(I32, (steps, 128), 1) < head_width
    for p in range(requests):
        cut = slice(p * steps, (p + 1) * steps)
        read = jnp.concatenate(
            [spread(compact[0, p].astype(BF16), steps), spread(compact[1, p].astype(BF16), steps)], axis=1
        )
        state = state_ref[p]
        along = dot(state, expand(a_ref[cut, :], head_width), NT).astype(BF16)
        both = jnp.concatenate([along, value_t_ref[p]], axis=1)
        out = dot(read, jnp.concatenate([both, both], axis=0), NT)
        out = out + dot(expand(line_scratch[cut, :], head_width), jnp.concatenate([state, state], axis=0), NT)
        for pair in range(heads // 2):
            at = 2 * pair * steps
            out_scratch[cut, pair * 128 : (pair + 1) * 128] = jnp.where(
                out_low, out[at : at + steps, :], out[at + steps : at + 2 * steps, :]
            )
    out = out_scratch[...]
    centered = out - group_sum(out, head_width) * (1.0 / head_width)
    variance = group_sum(centered * centered, head_width) * (1.0 / head_width)
    line = centered * lax.rsqrt(variance + NORM_EPSILON) * vector_ref[7:8, :] + vector_ref[8:9, :]
    result_ref[...] = (line + bonus * value_ref[...].astype(F32)).astype(BF16)


def place_kernel(per_peer, index_ref, back_ref, out_ref, edge_ref, scratch, edge_scratch, edge_placed):
    slot_dev = out_ref.shape[0]
    pack = back_ref.shape[1]
    for s in range(slot_dev):
        scratch[s] = back_ref[index_ref[6, s]].astype(F32)
    left = lax.broadcasted_iota(I32, (slot_dev, 128), 1) < 64
    half = pack // 2
    for b in range(half):
        even = scratch[:, 2 * b, :]
        odd = scratch[:, 2 * b + 1, :]
        out_ref[:, b * 128 : (b + 1) * 128] = jnp.where(left, even, pltpu.roll(odd, 64, 1))
        out_ref[:, (half + b) * 128 : (half + b + 1) * 128] = jnp.where(left, pltpu.roll(even, 64, 1), odd)
    for b in range(slot_dev // per_peer):
        block = back_ref[b * (per_peer + 1) + per_peer].astype(F32)
        edge_scratch[b * per_peer : (b + 1) * per_peer, :] = block[:per_peer, :]
    for s in range(slot_dev):
        edge_placed[s : s + 1, :] = edge_scratch[pl.ds(index_ref[5, s], 1), :]
    edge_ref[...] = jnp.transpose(edge_placed[...])[: edge_ref.shape[0], :]


def local(
    layer_entry_vectors,
    guessed_lookup_vectors,
    guessed_content_vectors,
    gating_query,
    lane_memory_store,
    prior_step_store,
    fading_blend_ratio,
    learning_speed_blend,
    fading_left_factor,
    fading_right_factor,
    fading_offset,
    learning_speed_left,
    learning_speed_right,
    learning_speed_offset,
    erasing_lookup_factor,
    written_lookup_factor,
    present_reward_factors,
    lane_standard_factor,
    lane_standard_offset,
    caller_memory_directory,
    kept_target_place,
    caller_sequence,
    approved_guesses,
):
    blocks = lax.axis_size("blk")
    groups = lax.axis_size("head")
    requests, steps, width = layer_entry_vectors.shape
    heads, halves = caller_memory_directory.shape[1:]
    slot_dev = lane_memory_store.shape[1]
    slot_width = lane_memory_store.shape[2]
    pack = slot_width // 128
    per_peer = slot_dev // blocks
    edge_rows = prior_step_store.shape[2]
    rows = requests * steps
    rank = fading_left_factor.shape[1]
    sds = jax.ShapeDtypeStruct

    def exchange(x, axis):
        return lax.all_to_all(
            x, axis, split_axis=0, concat_axis=0, tiled=True, axis_index_groups=[list(order_of(blocks))]
        )

    read_table = caller_memory_directory.transpose(1, 2, 0)
    write_table = kept_target_place.transpose(1, 2, 0)
    pieces = 1
    (sent,) = call(
        functools.partial(send_kernel, blocks, requests, per_peer, pieces),
        (pltpu.HBM((blocks * (per_peer + 1), pack, 128), BF16),),
        raw=(caller_sequence, read_table, lane_memory_store[0], prior_step_store[0].T),
        raw_outs=(0,),
        scratch=[
            pltpu.SMEM(caller_sequence.shape, I32),
            pltpu.VMEM(read_table.shape, I32),
            pltpu.VMEM((slot_dev, slot_width), F32),
            pltpu.VMEM((edge_rows, slot_dev), F32),
            pltpu.VMEM((slot_dev, pack, 128), F32),
            pltpu.VMEM((slot_dev, slot_dev), F32),
            pltpu.VMEM((blocks * (per_peer + 1), pack, 128), BF16),
            pltpu.SemaphoreType.DMA((3,)),
            pltpu.SemaphoreType.DMA((2 * pieces,)),
            pltpu.SemaphoreType.DMA((8,)),
        ],
    )
    got = exchange(sent.reshape(blocks, (per_peer + 1) * pack, 128), "blk")
    got = got.reshape(blocks * (per_peer + 1), pack, 128)
    layer = layer_entry_vectors.reshape(rows, width)
    key = guessed_lookup_vectors.reshape(rows, width)
    value = guessed_content_vectors.reshape(rows, width)
    vectors = (
        fading_blend_ratio, learning_speed_blend, fading_offset, learning_speed_offset, erasing_lookup_factor,
        written_lookup_factor, present_reward_factors, lane_standard_factor, lane_standard_offset,
    )
    arrays = (fading_left_factor.T, learning_speed_left.T, fading_right_factor, learning_speed_right)
    one = sds((requests, width), F32)
    wide = sds((rows, width), BF16)
    left = sds((rank, width), BF16)
    (
        partial_sums, first_lines, picked, vector, left_decay, left_rate, right_decay, right_rate,
    ) = call(
        functools.partial(shift_kernel, requests, len(vectors)),
        (sds((rows, 2 * rank), BF16), one, one, sds((16, width), F32), left, left, left, left),
        raw=(caller_sequence, approved_guesses, *(x.reshape(1, width) for x in vectors), layer, *arrays),
        scratch=[
            pltpu.SMEM(caller_sequence.shape, I32),
            pltpu.SMEM(approved_guesses.shape, I32),
            pltpu.VMEM((rows, width), BF16),
            pltpu.VMEM((rows, width), F32),
            pltpu.SemaphoreType.DMA((3,)),
            pltpu.SemaphoreType.DMA((len(vectors),)),
            pltpu.SemaphoreType.DMA((len(arrays),)),
        ],
    )

    def from_group(x):
        return [x] + [lax.ppermute(x, "head", [(g, g ^ d) for g in range(groups)]) for d in range(1, groups)]

    parts = from_group(partial_sums)
    head_width = width // heads
    index, key_near, unit, value_t, unit_first, key_first, value_first = call(
        functools.partial(index_kernel, blocks, requests, per_peer, heads),
        (
            sds((8, slot_dev), I32), wide, sds((rows, width), F32),
            sds((requests, head_width, heads * steps), BF16),
            one, one, one,
        ),
        near=(vector,),
        raw=(caller_sequence, approved_guesses, read_table, write_table, key, value),
        held=(first_lines, picked, left_decay, left_rate, right_decay, right_rate),
        scratch=[
            pltpu.SMEM(caller_sequence.shape, I32),
            pltpu.SMEM(approved_guesses.shape, I32),
            pltpu.VMEM(read_table.shape, I32),
            pltpu.VMEM(write_table.shape, I32),
            pltpu.VMEM((rows, width), BF16),
            pltpu.VMEM((heads * halves, write_table.shape[2]), I32),
            pltpu.SemaphoreType.DMA((6,)),
        ],
    )
    a_lines, k_lines, b_lines, scale, key_mod, last, solve, through, added = call(
        functools.partial(prepare_kernel, requests, heads, groups),
        (
            wide, wide, wide, wide, wide, one,
            sds((2, steps, requests, heads * steps), F32),
            sds((requests, head_width, width), BF16),
            sds((requests, head_width, width), BF16),
        ),
        scalars=(index,),
        near=(*parts, vector, right_decay, right_rate, key_near, unit, value_t),
        held=(first_lines, picked, left_decay, left_rate, unit_first, key_first, value_first),
        scratch=[
            pltpu.VMEM((requests, steps, 2 * heads * steps), F32),
            pltpu.VMEM((2, requests, steps, heads * steps), F32),
            pltpu.VMEM((rows, width), F32),
        ],
    )
    read_later = (scale, key_mod, a_lines, k_lines, b_lines, solve, value_t)
    state_later = (vector, right_decay, right_rate, key_first, last, through, added)
    first_sums, edge = call(
        functools.partial(first_kernel, requests, heads, halves, per_peer),
        (sds((requests, 2 * rank), F32), one),
        scalars=(index,),
        near=(got, first_lines, vector, left_decay, left_rate),
        held=(unit_first, value_first, picked, *state_later[1:], *read_later),
        scratch=[pltpu.VMEM((slot_dev, 128), F32)],
    )
    first_parts = from_group(first_sums)
    state, change, edge_blocks = call(
        functools.partial(layout_kernel, requests, heads, halves, per_peer),
        (
            sds((requests, head_width, width), BF16),
            sds((requests, head_width, 2 * heads), BF16),
            sds((blocks, pack, 128), BF16),
        ),
        scalars=(index,),
        near=(got, unit_first, value_first, edge, picked),
        held=(*state_later, *read_later),
        scratch=[pltpu.VMEM((slot_dev, 128), F32)],
    )
    back, after, key_mod_first = call(
        functools.partial(state_kernel, requests, heads, halves, per_peer, groups),
        (
            pltpu.HBM((blocks * (per_peer + 1), pack, 128), BF16),
            sds((requests, head_width, width), BF16),
            one,
        ),
        scalars=(index,),
        near=(
            *first_parts, state, change, edge_blocks, unit_first, key_first, last, through, added,
            vector, right_decay, right_rate,
        ),
        held=read_later,
        scratch=[pltpu.VMEM((requests, head_width, width), F32)],
    )
    back = exchange(back.reshape(blocks, (per_peer + 1) * pack, 128), "blk")
    back = back.reshape(blocks * (per_peer + 1), pack, 128)
    recept = call(
        lines_kernel,
        (sds((rows // groups, width), BF16),) * groups,
        far=(gating_query,),
        held=(index, vector, after, key_mod_first, *read_later),
        scratch=[pltpu.VMEM((rows // groups, width), F32)],
    )
    recept = [recept[0]] + [
        lax.ppermute(recept[d], "head", [(g, g ^ d) for g in range(groups)]) for d in range(1, groups)
    ]
    (result,) = call(
        functools.partial(read_kernel, requests, heads, groups),
        (pltpu.HBM((rows, width), BF16),),
        near=(*recept, scale, key_mod, key_mod_first, a_lines, k_lines, b_lines, solve, after, value_t, vector),
        far=(value,),
        held=(index,),
        scratch=[
            pltpu.VMEM((rows, width), BF16),
            pltpu.VMEM((requests, steps, 2 * heads * steps), F32),
            pltpu.VMEM((2, requests, steps, heads * steps), F32),
            pltpu.VMEM((rows, width), F32),
        ],
    )
    new_states, new_edges = call(
        functools.partial(place_kernel, per_peer),
        (pltpu.HBM((slot_dev, slot_width), F32), pltpu.HBM((edge_rows, slot_dev), F32)),
        scalars=(index,),
        near=(back,),
        scratch=[
            pltpu.VMEM((slot_dev, pack, 128), F32),
            pltpu.VMEM((slot_dev, 128), F32),
            pltpu.VMEM((slot_dev, 128), F32),
        ],
    )
    return (result.reshape(requests, steps, width), new_states[None], new_edges.T[None])


def solution(mesh):
    return jax.shard_map(
        local,
        mesh=mesh,
        in_specs=(
            P("blk", None, "head"),
            P("blk", None, "head"),
            P("blk", None, "head"),
            P("blk", "head", None),
            P("head", "blk", None),
            P("head", "blk", None),
            P("head"),
            P("head"),
            P("head", None),
            P(None, "head"),
            P("head"),
            P("head", None),
            P(None, "head"),
            P("head"),
            P("head"),
            P("head"),
            P("head"),
            P("head"),
            P("head"),
            P(None, "head", None),
            P(None, "head", None),
            P(),
            P(),
        ),
        out_specs=(P("blk", None, "head"), P("head", "blk", None), P("head", "blk", None)),
        check_vma=False,
    )
```

```python
import functools

import jax
import jax.numpy as jnp
from jax import lax
from jax.experimental import pallas as pl
from jax.experimental.pallas import tpu as pltpu
from jax.sharding import PartitionSpec as P

EPSILON = 1e-05
NORM_EPSILON = 0.00064
DECAY_SCALE = 0.6065306597126334
F32 = jnp.float32
BF16 = jnp.bfloat16
I32 = jnp.int32
NT = (((1,), (1,)), ((), ()))
NN = (((1,), (0,)), ((), ()))


def call(kernel, outs, scalars=(), near=(), far=(), raw=(), loose=(), held=(), scratch=(), raw_outs=(), vmem=16):
    reads = len(scalars) + len(near) + len(far) + len(raw) + len(loose)

    def body(*refs):
        kernel(*refs[:reads], *refs[reads + len(held) :])

    args = [*scalars]
    args += [*near]
    args += [pltpu.with_memory_space_constraint(x, pltpu.HBM) for x in (*far, *raw)]
    specs = [pl.BlockSpec(memory_space=pltpu.SMEM)] * len(scalars)
    specs += [pl.BlockSpec(memory_space=pltpu.VMEM)] * (len(near) + len(far))
    specs += [pl.BlockSpec(memory_space=pltpu.HBM)] * (len(raw) + len(loose) + len(held))
    return pl.pallas_call(
        body,
        out_shape=outs,
        in_specs=specs,
        out_specs=tuple(
            pl.BlockSpec(memory_space=pltpu.HBM if i in raw_outs else pltpu.VMEM) for i in range(len(outs))
        ),
        scratch_shapes=list(scratch),
        compiler_params=pltpu.CompilerParams(vmem_limit_bytes=vmem * 1024 * 1024),
        cost_estimate=pl.CostEstimate(flops=1 << 20, bytes_accessed=1 << 20, transcendentals=0),
    )(*args, *loose, *held)


def dot(a, b, dims=NN):
    return lax.dot_general(a, b, dims, preferred_element_type=F32)


def split(x):
    high = x.astype(BF16)
    return high, (x - high.astype(F32)).astype(BF16)


def group_sum(x, width):
    rows, lanes = x.shape
    block = max(width, 128)
    ones = (
        lax.broadcasted_iota(I32, (block, block), 0) // width
        == lax.broadcasted_iota(I32, (block, block), 1) // width
    ).astype(BF16)
    high, low = split(x)
    parts = []
    for start in range(0, lanes, block):
        cut = slice(start, start + block)
        parts.append(dot(high[:, cut], ones) + dot(low[:, cut], ones))
    return jnp.concatenate(parts, axis=1)


def order_of(blocks):
    return (2, 3, 1, 0, 4, 5, 7, 6) if blocks == 8 else tuple(range(blocks))


def seat_of(block, blocks):
    order = order_of(blocks)
    if order == tuple(range(blocks)):
        return block
    seat = jnp.zeros_like(block)
    for i, b in enumerate(order):
        seat = jnp.where(block == b, i, seat)
    return seat


def positions(seq_ref, count):
    lane = lax.broadcasted_iota(I32, (1, count), 1)

    def block(b, acc):
        for k in range(8):
            acc = jnp.where(lane == seq_ref[b * 8 + k], b * 8 + k, acc)
        return acc

    return lax.fori_loop(0, count // 8, block, jnp.zeros((1, count), I32))


def place_of_slot(table_ref, position, base, blocks, per_peer, requests, slot_dev):
    heads, halves, count = table_ref.shape
    slot = lax.broadcasted_iota(I32, (slot_dev, count), 0) + base
    named = jnp.zeros((slot_dev, count), F32)
    for h in range(heads):
        for c in range(halves):
            named = jnp.where(table_ref[h, c : c + 1, :] == slot, 1.0, named)
    other_of = jnp.broadcast_to(seat_of(position // requests, blocks), (16, count)).astype(F32).astype(BF16)
    other = dot(other_of, named.astype(BF16), NT)[0:1, :].astype(I32)
    rows = max(16, blocks)
    mask = other == lax.broadcasted_iota(I32, (rows, slot_dev), 0)
    before = (
        lax.broadcasted_iota(I32, (slot_dev, slot_dev), 0)
        < lax.broadcasted_iota(I32, (slot_dev, slot_dev), 1)
    ).astype(F32).astype(BF16)
    ahead = dot(mask.astype(F32).astype(BF16), before)
    rank = jnp.sum(jnp.where(mask, ahead, 0.0), axis=0, keepdims=True).astype(I32)
    return other * per_peer + rank


def place_of_item(table_ref, lines_ref, position, first, blocks, requests, slot_dev):
    heads, halves, count = table_ref.shape
    per_item = heads * halves
    items = requests * per_item
    mine = (
        jnp.broadcast_to(position, (16, count)) - first == lax.broadcasted_iota(I32, (16, count), 0)
    ).astype(F32).astype(BF16)
    for h in range(heads):
        lines_ref[h * halves : (h + 1) * halves, :] = table_ref[h]
    lines = lines_ref[...]
    lane = lax.broadcasted_iota(I32, (16, items), 1)
    owner = lax.broadcasted_iota(I32, (16, items), 0) == lane // per_item
    of_item = (
        lax.broadcasted_iota(I32, (per_item, items), 0) == lax.broadcasted_iota(I32, (per_item, items), 1) % per_item
    ).astype(F32).astype(BF16)
    seats = seat_of(lines // slot_dev, blocks)
    high = dot(dot(mine, seats.astype(F32).astype(BF16), NT).astype(BF16), of_item)
    low = dot(dot(mine, (lines % slot_dev).astype(F32).astype(BF16), NT).astype(BF16), of_item)
    slots = high * slot_dev + low
    row = jnp.sum(jnp.where(owner, slots, 0.0), axis=0, keepdims=True)
    diagonal = lax.broadcasted_iota(I32, (items, items), 0) == lax.broadcasted_iota(I32, (items, items), 1)
    column = jnp.sum(jnp.where(diagonal, row, 0.0), axis=1, keepdims=True)
    return jnp.sum((column < row).astype(F32), axis=0, keepdims=True).astype(I32)


def send_kernel(
    blocks, requests, per_peer, pieces,
    seq_hbm, read_hbm, state_hbm, edge_hbm,
    out_hbm,
    seq_ref, read_ref, state_ref, edge_ref, flat, scratch, edge_scratch, out_ref, sems, state_sems, out_sems,
):
    slot_dev, slot_width = state_ref.shape
    pack = out_ref.shape[1]
    me = lax.axis_index("blk")
    sources = (seq_hbm, read_hbm, edge_hbm)
    targets = (seq_ref, read_ref, edge_ref)
    copies = [pltpu.make_async_copy(a, b, sems.at[i]) for i, (a, b) in enumerate(zip(sources, targets))]
    state_copies = []
    piece = slot_width // 2 // pieces
    for i in range(pieces):
        for start in (i * piece, slot_width // 2 + i * piece):
            cut = (slice(None), pl.ds(start, piece))
            state_copies.append(
                pltpu.make_async_copy(state_hbm.at[cut], state_ref.at[cut], state_sems.at[len(state_copies)])
            )
    for copy in (*copies[:2], *state_copies, copies[2]):
        copy.start()
    copies[0].wait()
    copies[1].wait()
    position = positions(seq_ref, read_ref.shape[2])
    place = place_of_slot(read_ref, position, me * slot_dev, blocks, per_peer, requests, slot_dev)
    pick = (place == lax.broadcasted_iota(I32, (slot_dev, slot_dev), 0)).astype(F32).astype(BF16)
    left = lax.broadcasted_iota(I32, (slot_dev, 128), 1) < 64
    half = pack // 2
    for b in range(half):
        if b % (half // pieces) == 0:
            state_copies[b // (half // pieces) * 2].wait()
            state_copies[b // (half // pieces) * 2 + 1].wait()
        x = dot(pick, state_ref[:, b * 128 : (b + 1) * 128].astype(BF16))
        y = dot(pick, state_ref[:, (half + b) * 128 : (half + b + 1) * 128].astype(BF16))
        flat[:, 2 * b * 128 : (2 * b + 1) * 128] = jnp.where(left, x, pltpu.roll(y, 64, 1))
        flat[:, (2 * b + 1) * 128 : (2 * b + 2) * 128] = jnp.where(left, pltpu.roll(x, 64, 1), y)
    for row in range(0, slot_dev, 8):
        for j in range(0, pack, 8):
            tiles = [flat[row : row + 8, i * 128 : (i + 1) * 128] for i in range(j, j + 8)]
            scratch[row : row + 8, j : j + 8, :] = jnp.swapaxes(jnp.stack(tiles), 0, 1)
    copies[2].wait()
    edge_rows = edge_ref.shape[0]
    edges = jnp.concatenate([edge_ref[...], jnp.zeros((slot_dev - edge_rows, slot_dev), F32)], axis=0)
    edge_scratch[...] = dot(pick, edges.astype(BF16), NT)
    out_copies = []
    for b in range(blocks):
        at = b * (per_peer + 1)
        out_ref[at : at + per_peer] = scratch[b * per_peer : (b + 1) * per_peer].astype(BF16)
        block = edge_scratch[b * per_peer : (b + 1) * per_peer, :]
        if per_peer < pack:
            block = jnp.concatenate([block, jnp.zeros((pack - per_peer, 128), F32)], axis=0)
        out_ref[at + per_peer] = block.astype(BF16)
        if (b + 1) % (blocks // 8) == 0:
            cut = pl.ds((b + 1 - blocks // 8) * (per_peer + 1), blocks // 8 * (per_peer + 1))
            out_copies.append(pltpu.make_async_copy(out_ref.at[cut], out_hbm.at[cut], out_sems.at[len(out_copies)]))
            out_copies[-1].start()
    for copy in out_copies:
        copy.wait()


def pick_of(place):
    count = place.shape[1]
    row = lax.broadcasted_iota(I32, (count, count), 0)
    lane = lax.broadcasted_iota(I32, (count, count), 1)
    column = jnp.sum(jnp.where(row == lane, place, 0).astype(F32), axis=1, keepdims=True).astype(I32)
    return (column == lane).astype(F32).astype(BF16)


def shift_kernel(requests, lines, *refs):
    scalars_hbm, refs = refs[:2], refs[2:]
    vectors_hbm, refs = refs[:lines], refs[lines:]
    arrays_hbm, refs = refs[:5], refs[5:]
    partial_ref, first_ref, picked_ref, vector_ref = refs[:4]
    arrays, refs = refs[4:8], refs[8:]
    seq_ref, count_ref, layer_ref, line_scratch, sems, line_sem, array_sem = refs
    pairs = zip((*scalars_hbm, arrays_hbm[0]), (seq_ref, count_ref, layer_ref))
    copies = [pltpu.make_async_copy(a, b, sems.at[i]) for i, (a, b) in enumerate(pairs)]
    line_copies = [
        pltpu.make_async_copy(a, vector_ref.at[pl.ds(i, 1)], line_sem.at[i]) for i, a in enumerate(vectors_hbm)
    ]
    array_copies = [
        pltpu.make_async_copy(a, b, array_sem.at[i]) for i, (a, b) in enumerate(zip(arrays_hbm[1:], arrays))
    ]
    for copy in (copies[2], *line_copies[:2], *array_copies, *copies[:2], *line_copies[2:]):
        copy.start()
    copies[2].wait()
    steps = layer_ref.shape[0] // requests
    line = layer_ref[...].astype(F32)
    line_scratch[...] = line
    delta = pltpu.roll(line, 1, 0) - line
    left_decay_ref, left_rate_ref = arrays[:2]
    rank = left_decay_ref.shape[0]
    for copy in (*line_copies, *array_copies, *copies[:2]):
        copy.wait()
    mixed_decay = (line + delta * vector_ref[0:1, :]).astype(BF16)
    mixed_rate = (line + delta * vector_ref[1:2, :]).astype(BF16)
    partial_ref[:, :rank] = dot(mixed_decay, left_decay_ref[...], NT).astype(BF16)
    partial_ref[:, rank:] = dot(mixed_rate, left_rate_ref[...], NT).astype(BF16)
    first = lax.axis_index("blk") * requests
    for p in range(requests):
        first_ref[p : p + 1, :] = line_scratch[p * steps : p * steps + 1, :]
        n = count_ref[seq_ref[first + p]]
        picked_ref[p : p + 1, :] = line_scratch[pl.ds(p * steps + jnp.maximum(n - 1, 0), 1), :]


def index_kernel(blocks, requests, per_peer, heads, vector_ref, *refs):
    hbm, refs = refs[:6], refs[6:]
    index_ref, pick_in_ref, pick_out_ref, key_ref, unit_ref, value_t_ref, *refs = refs
    unit_first_ref, key_first_ref, value_first_ref, *refs = refs
    seq_ref, count_ref, read_ref, write_ref, value_ref, lines_ref, sems = refs
    targets = (seq_ref, count_ref, read_ref, write_ref, key_ref, value_ref)
    copies = [pltpu.make_async_copy(a, b, sems.at[i]) for i, (a, b) in enumerate(zip(hbm, targets))]
    for copy in copies:
        copy.start()
    for copy in copies[:4]:
        copy.wait()
    slot_dev = index_ref.shape[1]
    me = lax.axis_index("blk")
    first = me * requests
    position = positions(seq_ref, read_ref.shape[2])
    place_in = place_of_item(read_ref, lines_ref, position, first, blocks, requests, slot_dev)
    place_out = place_of_item(write_ref, lines_ref, position, first, blocks, requests, slot_dev)
    target = place_of_slot(write_ref, position, me * slot_dev, blocks, per_peer, requests, slot_dev)
    lane = lax.broadcasted_iota(I32, (1, slot_dev), 1)
    counts = jnp.zeros((1, slot_dev), I32)
    for p in range(requests):
        counts = jnp.where(lane == p, count_ref[seq_ref[first + p]], counts)
    index_ref[0:1, :] = place_in
    index_ref[1:2, :] = place_out
    index_ref[2:3, :] = place_in + place_in // per_peer
    index_ref[3:4, :] = counts
    index_ref[4:5, :] = place_out + place_out // per_peer
    index_ref[5:8, :] = jnp.zeros((3, slot_dev), I32)
    pick_in_ref[...] = pick_of(place_in)
    pick_out_ref[...] = pick_of(target)
    copies[4].wait()
    copies[5].wait()
    rows, width = key_ref.shape
    steps = rows // requests
    head_width = width // heads
    u = key_ref[...].astype(F32) * vector_ref[4:5, :]
    unit_ref[...] = u * lax.rsqrt(group_sum(u * u, head_width) + EPSILON)
    ident = ident_of(head_width, width)
    for p in range(requests):
        cut = slice(p * steps, (p + 1) * steps)
        line = slice(p, p + 1)
        unit_first_ref[line, :] = unit_ref[p * steps : p * steps + 1, :]
        key_first_ref[line, :] = key_ref[cut, :].astype(F32)[0:1, :]
        value_first_ref[line, :] = value_ref[cut, :].astype(F32)[0:1, :]
        value_t_ref[p] = dot(ident, expand(value_ref[cut, :], head_width), NT).astype(BF16)


def first_kernel(
    requests, heads, halves, per_peer,
    pick_ref, got_ref, first_ref, vector_ref, left_decay_ref, left_rate_ref,
    out_ref, edge_ref, pool_scratch, item_scratch,
):
    slot_dev = pool_scratch.shape[0]
    per_item = heads * halves
    rows = first_ref.shape[1] // per_item
    for b in range(slot_dev // per_peer):
        block = got_ref[b * (per_peer + 1) + per_peer].astype(F32)
        pool_scratch[b * per_peer : (b + 1) * per_peer, :] = block[:per_peer, :]
    item_scratch[...] = dot(pick_ref[...], pool_scratch[...].astype(BF16))
    for k in range(per_item):
        edge_ref[:, k * rows : (k + 1) * rows] = item_scratch[pl.ds(k, requests, per_item), :rows]
    line = first_ref[...]
    delta = edge_ref[...] - line
    rank = left_decay_ref.shape[0]
    mixed_decay = (line + delta * vector_ref[0:1, :]).astype(BF16)
    mixed_rate = (line + delta * vector_ref[1:2, :]).astype(BF16)
    out_ref[:, :rank] = dot(mixed_decay, left_decay_ref[...], NT)
    out_ref[:, rank:] = dot(mixed_rate, left_rate_ref[...], NT)


def expand(x, head_width):
    steps, lanes = x.shape
    heads = lanes // head_width
    per_block = 128 // head_width
    lane = lax.broadcasted_iota(I32, (steps, 128), 1) // head_width
    zero = jnp.zeros((steps, 128), x.dtype)
    lines = []
    for h in range(heads):
        own = h // per_block
        block = jnp.where(lane == h % per_block, x[:, own * 128 : (own + 1) * 128], zero)
        lines.append(jnp.concatenate([block if b == own else zero for b in range(lanes // 128)], axis=1))
    return jnp.concatenate(lines, axis=0)


def ident_of(head_width, width):
    return (
        lax.broadcasted_iota(I32, (head_width, width), 0)
        == lax.broadcasted_iota(I32, (head_width, width), 1) % head_width
    ).astype(F32).astype(BF16)


def head_rows(line, heads, head_width, shift):
    shape = (2 * heads, line.shape[1])
    own = lax.broadcasted_iota(I32, shape, 1) // head_width + shift
    return jnp.where(own == lax.broadcasted_iota(I32, shape, 0), jnp.broadcast_to(line, shape), 0.0)


def prepare_kernel(
    requests, heads, groups,
    *refs,
):
    parts_refs = refs[:groups]
    (
        vector_ref, right_decay_ref, right_rate_ref, key_ref, unit_ref, value_t_ref, index_near_ref,
        a_ref, k_ref, b_ref, scale_ref, key_mod_ref, last_ref, solve_ref, through_ref, added_ref,
        cross, compact, cum_ref, k_low_ref, b_low_ref, index_ref, index_sem,
    ) = refs[groups:]
    index_copy = pltpu.make_async_copy(index_near_ref, index_ref, index_sem)
    index_copy.start()
    rows, width = key_ref.shape
    steps = rows // requests
    head_width = width // heads
    rank = right_decay_ref.shape[0]
    total = parts_refs[0][...].astype(F32)
    for ref in parts_refs[1:]:
        total = total + ref[...].astype(F32)
    hidden = jnp.tanh(total[:, :rank]).astype(BF16)
    rate_hidden = total[:, rank:].astype(BF16)
    decay = vector_ref[2:3, :] + dot(hidden, right_decay_ref[...])
    step = lax.broadcasted_iota(I32, (rows, width), 0) % steps
    later = step > 0
    log_forget = jnp.where(later, -DECAY_SCALE * jax.nn.sigmoid(decay), 0.0)
    rate = jax.nn.sigmoid(vector_ref[3:4, :] + dot(rate_hidden, right_rate_ref[...]))
    key = key_ref[...].astype(F32)
    unit = unit_ref[...]
    key_mod = key * (1.0 + (rate - 1.0) * vector_ref[5:6, :])
    key_mod_ref[...] = key_mod.astype(BF16)
    cum = log_forget
    shift = 1
    while shift < steps:
        cum = cum + jnp.where(step >= shift, pltpu.roll(cum, shift, 0), 0.0)
        shift *= 2
    grow = jnp.where(later, jnp.exp(-cum), 0.0)
    cum_ref[...] = cum
    scale_ref[...] = jnp.exp(cum).astype(BF16)
    a_ref[...] = jnp.where(later, unit * jnp.exp(cum - log_forget), 0.0).astype(BF16)
    k_ref[...], k_low_ref[...] = split(key_mod * grow)
    b_ref[...], b_low_ref[...] = split(rate * unit * grow)
    ident = ident_of(head_width, width)
    lanes = heads * steps
    index_copy.wait()
    for p in range(requests):
        cut = slice(p * steps, (p + 1) * steps)
        n = index_ref[3, p]
        at_n = cum_ref[pl.ds(p * steps + jnp.maximum(n - 1, 0), 1), :]
        last_ref[p : p + 1, :] = jnp.where(n > 0, jnp.exp(at_n), 1.0)
        right = jnp.concatenate([expand(k_ref[cut, :], head_width), expand(b_ref[cut, :], head_width)], axis=0)
        cross[p] = dot(a_ref[cut, :], right, NT)
    lane = lax.broadcasted_iota(I32, (requests, lanes), 1)
    source = lane % steps
    group = lane - source
    solve, carry = [], []
    for t in range(steps):
        weights = jnp.where(source < t, cross[:, t, lanes:], 0.0)
        solve_t = jnp.where(source == t, 1.0, 0.0)
        carry_t = jnp.where(source < t, cross[:, t, :lanes], 0.0)
        for s in range(t):
            weight = jnp.take_along_axis(weights, group + s, axis=1)
            solve_t = solve_t - weight * solve[s]
            carry_t = carry_t - weight * carry[s]
        solve.append(solve_t)
        carry.append(carry_t)
        compact[0, :, t, :] = solve_t
        compact[1, :, t, :] = carry_t
        solve_ref[0, t] = solve_t
        solve_ref[1, t] = carry_t
    for p in range(requests):
        cut = slice(p * steps, (p + 1) * steps)
        n = index_ref[3, p]
        a_t = dot(ident, expand(a_ref[cut, :], head_width), NT).astype(BF16)
        value_t = value_t_ref[p]
        reach = dot(a_t, spread(compact[0, p].astype(BF16), steps), NT)
        high, low = split(compact[1, p])
        removed = dot(value_t, spread(high, steps), NT) + dot(value_t, spread(low, steps), NT)
        left = jnp.concatenate(
            [
                jnp.concatenate([-reach, jnp.zeros_like(reach)], axis=1),
                jnp.concatenate([-removed, value_t.astype(F32)], axis=1),
            ],
            axis=0,
        )
        at = lax.broadcasted_iota(I32, left.shape, 1) % steps
        left, left_low = split(jnp.where(at < n, left, 0.0))
        right = jnp.concatenate([expand(b_ref[cut, :], head_width), expand(k_ref[cut, :], head_width)], axis=0)
        right_low = jnp.concatenate([expand(b_low_ref[cut, :], head_width), expand(k_low_ref[cut, :], head_width)], axis=0)
        both = (dot(left, right) + dot(left_low, right) + dot(left, right_low)) * last_ref[p : p + 1, :]
        added_ref[p] = both[head_width:, :].astype(BF16)
        through_ref[p] = both[:head_width, :].astype(BF16)


def spread(x, steps):
    lanes = x.shape[1]
    group = lax.broadcasted_iota(I32, x.shape, 1) // steps
    zero = jnp.zeros_like(x)
    return jnp.concatenate([jnp.where(group == h, x, zero) for h in range(lanes // steps)], axis=0)


def layout_kernel(
    requests, heads, halves, per_peer,
    index_ref, got_ref, unit_first_ref, value_first_ref, edge_ref, picked_ref,
    state_ref, change_ref, edge_out_ref, edge_scratch,
):
    width = unit_first_ref.shape[1]
    head_width = width // heads
    pack = got_ref.shape[1]
    edge_rows = head_width // halves
    ident = ident_of(head_width, width)
    low = lax.broadcasted_iota(I32, (pack, 128), 1) < head_width
    for p in range(requests):
        for c in range(halves):
            for pair in range(heads // 2):
                at = (p * heads + 2 * pair) * halves + c
                even = got_ref[index_ref[2, at]].astype(F32)
                odd = got_ref[index_ref[2, at + halves]].astype(F32)
                top = jnp.where(low, even, pltpu.roll(odd, head_width, 1))
                bottom = jnp.where(low, pltpu.roll(even, head_width, 1), odd)
                lanes = slice(pair * 128, (pair + 1) * 128)
                state_ref[p, 2 * c * pack : (2 * c + 1) * pack, lanes] = top.astype(BF16)
                state_ref[p, (2 * c + 1) * pack : (2 * c + 2) * pack, lanes] = bottom.astype(BF16)
        unit = head_rows(unit_first_ref[p : p + 1, :], heads, head_width, 0).astype(BF16)
        value = head_rows(value_first_ref[p : p + 1, :], heads, head_width, heads).astype(BF16)
        change_ref[p] = (dot(ident, value, NT) - dot(state_ref[p], unit, NT)).astype(BF16)
        new_edge = jnp.where(index_ref[3, p] > 0, picked_ref[p : p + 1, :], edge_ref[p : p + 1, :])
        for k in range(heads * halves):
            lane = k * edge_rows
            line = new_edge[:, lane // 128 * 128 : lane // 128 * 128 + 128]
            if lane % 128:
                line = pltpu.roll(line, 128 - lane % 128, 1)
            edge_scratch[pl.ds(index_ref[1, p * heads * halves + k], 1), :] = line
    for b in range(edge_out_ref.shape[0]):
        block = edge_scratch[b * per_peer : (b + 1) * per_peer, :]
        if per_peer < pack:
            block = jnp.concatenate([block, jnp.zeros((pack - per_peer, 128), F32)], axis=0)
        edge_out_ref[b] = block.astype(BF16)


def state_kernel(
    requests, heads, halves, per_peer, groups,
    *refs,
):
    parts_refs = refs[:groups]
    (
        state_ref, change_ref, edge_blocks_ref, unit_first_ref, key_first_ref, last_ref, through_ref, added_ref,
        vector_ref, right_decay_ref, right_rate_ref, index_near_ref,
        send_ref, after_ref, key_mod_first_ref,
        kept_ref, index_ref, index_sem,
    ) = refs[groups:]
    index_copy = pltpu.make_async_copy(index_near_ref, index_ref, index_sem)
    index_copy.start()
    width = unit_first_ref.shape[1]
    head_width = width // heads
    pack = send_ref.shape[1]
    rank = right_decay_ref.shape[0]
    total = parts_refs[0][...]
    for ref in parts_refs[1:]:
        total = total + ref[...]
    decay = vector_ref[2:3, :] + dot(jnp.tanh(total[:, :rank]).astype(BF16), right_decay_ref[...])
    forget = jnp.exp(-DECAY_SCALE * jax.nn.sigmoid(decay))
    rate = jax.nn.sigmoid(vector_ref[3:4, :] + dot(total[:, rank:].astype(BF16), right_rate_ref[...]))
    key_mod = key_first_ref[...] * (1.0 + (rate - 1.0) * vector_ref[5:6, :])
    key_mod_first_ref[...] = key_mod
    removal = rate * unit_first_ref[...]
    low = lax.broadcasted_iota(I32, (pack, 128), 1) < head_width
    own = lax.broadcasted_iota(I32, (head_width, 128), 1) < head_width
    for b in range(edge_blocks_ref.shape[0]):
        send_ref[b * (per_peer + 1) + per_peer] = edge_blocks_ref[b]
    for p in range(requests):
        line = slice(p, p + 1)
        written = head_rows(removal[line, :], heads, head_width, 0) + head_rows(key_mod[line, :], heads, head_width, heads)
        change = dot(change_ref[p], written.astype(BF16))
        after = state_ref[p].astype(F32) * forget[line, :] + change
        after_ref[p] = after.astype(BF16)
        kept_ref[p] = after * last_ref[line, :] + added_ref[p].astype(F32)
    index_copy.wait()
    for p in range(requests):
        parts = []
        for pair in range(heads // 2):
            lanes = slice(pair * 128, (pair + 1) * 128)
            through = through_ref[p, :, lanes]
            zero = jnp.zeros_like(through)
            through = jnp.concatenate([jnp.where(own, through, zero), jnp.where(own, zero, through)], axis=0)
            parts.append(dot(after_ref[p, :, lanes], through))
        kept = kept_ref[p] + jnp.concatenate(parts, axis=1)
        kept = jnp.where(index_ref[3, p] > 0, kept, state_ref[p].astype(F32))
        for c in range(halves):
            for pair in range(heads // 2):
                top = kept[(2 * c) * pack : (2 * c + 1) * pack, pair * 128 : (pair + 1) * 128]
                bottom = kept[(2 * c + 1) * pack : (2 * c + 2) * pack, pair * 128 : (pair + 1) * 128]
                at = (p * heads + 2 * pair) * halves + c
                even = jnp.where(low, top, pltpu.roll(bottom, head_width, 1))
                odd = jnp.where(low, pltpu.roll(top, head_width, 1), bottom)
                send_ref[index_ref[4, at]] = even.astype(BF16)
                send_ref[index_ref[4, at + halves]] = odd.astype(BF16)


def lines_kernel(gating_ref, *refs):
    *outs, scratch = refs
    requests, part = gating_ref.shape[:2]
    width = scratch.shape[1]
    me = lax.axis_index("head")
    for d, out in enumerate(outs):
        start = pl.multiple_of((me ^ d) * width, 128)
        for p in range(requests):
            scratch[p * part : (p + 1) * part, :] = gating_ref[p, :, pl.ds(start, width)].astype(F32)
        out[...] = scratch[...].astype(BF16)


def read_kernel(
    requests, heads, groups,
    *refs,
):
    return read_body(requests, heads, refs[:groups], *refs[groups:])


def read_body(
    requests, heads,
    recept_refs, scale_ref, key_mod_ref, key_mod_first_ref, a_ref, k_ref, b_ref, solve_ref, state_ref, value_t_ref,
    vector_ref, value_ref,
    result_ref, line_scratch, cross, compact, out_scratch,
):
    rows, width = value_ref.shape
    steps = rows // requests
    head_width = width // heads
    lanes = heads * steps
    part = steps // len(recept_refs)
    row = lax.broadcasted_iota(I32, (rows, rows), 0)
    source = (row % steps // part) ^ lax.axis_index("head")
    source_row = source * (requests * part) + row // steps * part + row % part
    order = (source_row == lax.broadcasted_iota(I32, (rows, rows), 1)).astype(F32).astype(BF16)
    recept = dot(order, jnp.concatenate([ref[...] for ref in recept_refs], axis=0))
    key_mod_first = jnp.broadcast_to(key_mod_first_ref[...][:, None, :], (requests, steps, width)).reshape(rows, width)
    first = lax.broadcasted_iota(I32, (rows, width), 0) % steps == 0
    key_mod = jnp.where(first, key_mod_first, key_mod_ref[...].astype(F32))
    bonus = group_sum(recept * key_mod * vector_ref[6:7, :], head_width)
    line_scratch[...] = (recept * scale_ref[...].astype(F32)).astype(BF16)
    for p in range(requests):
        cut = slice(p * steps, (p + 1) * steps)
        right = jnp.concatenate([expand(k_ref[cut, :], head_width), expand(b_ref[cut, :], head_width)], axis=0)
        cross[p] = dot(line_scratch[cut, :], right, NT)
    lane = lax.broadcasted_iota(I32, (requests, lanes), 1)
    source = lane % steps
    group = lane - source
    for t in range(steps):
        weights = jnp.where(source <= t, cross[:, t, lanes:], 0.0)
        from_a = jnp.zeros((requests, lanes), F32)
        from_v = jnp.where(source <= t, cross[:, t, :lanes], 0.0)
        for s in range(t + 1):
            weight = jnp.take_along_axis(weights, group + s, axis=1)
            from_a = from_a - weight * solve_ref[0, s]
            from_v = from_v - weight * solve_ref[1, s]
        compact[0, :, t, :] = from_a
        compact[1, :, t, :] = from_v
    out_low = lax.broadcasted_iota(I32, (steps, 128), 1) < head_width
    for p in range(requests):
        cut = slice(p * steps, (p + 1) * steps)
        read = jnp.concatenate(
            [spread(compact[0, p].astype(BF16), steps), spread(compact[1, p].astype(BF16), steps)], axis=1
        )
        state = state_ref[p]
        along = dot(state, expand(a_ref[cut, :], head_width), NT).astype(BF16)
        both = jnp.concatenate([along, value_t_ref[p]], axis=1)
        out = dot(read, jnp.concatenate([both, both], axis=0), NT)
        out = out + dot(expand(line_scratch[cut, :], head_width), jnp.concatenate([state, state], axis=0), NT)
        for pair in range(heads // 2):
            at = 2 * pair * steps
            out_scratch[cut, pair * 128 : (pair + 1) * 128] = jnp.where(
                out_low, out[at : at + steps, :], out[at + steps : at + 2 * steps, :]
            )
    out = out_scratch[...]
    centered = out - group_sum(out, head_width) * (1.0 / head_width)
    variance = group_sum(centered * centered, head_width) * (1.0 / head_width)
    line = centered * lax.rsqrt(variance + NORM_EPSILON) * vector_ref[7:8, :] + vector_ref[8:9, :]
    result_ref[...] = (line + bonus * value_ref[...].astype(F32)).astype(BF16)


def place_kernel(per_peer, pick_ref, back_ref, out_ref, edge_ref, scratch, flat, edge_scratch):
    slot_dev = out_ref.shape[0]
    pack = back_ref.shape[1]
    for b in range(slot_dev // per_peer):
        at = b * (per_peer + 1)
        scratch[b * per_peer : (b + 1) * per_peer] = back_ref[at : at + per_peer].astype(F32)
        edge_scratch[b * per_peer : (b + 1) * per_peer, :] = back_ref[at + per_peer].astype(F32)[:per_peer, :]
    left = lax.broadcasted_iota(I32, (8, 128), 1) < 64
    half = pack // 2
    for row in range(0, slot_dev, 8):
        for j in range(0, pack, 8):
            tiles = jnp.swapaxes(scratch[row : row + 8, j : j + 8, :], 0, 1)
            for i in range(4):
                even, odd = tiles[2 * i], tiles[2 * i + 1]
                b = j // 2 + i
                flat[row : row + 8, b * 128 : (b + 1) * 128] = jnp.where(left, even, pltpu.roll(odd, 64, 1))
                flat[row : row + 8, (half + b) * 128 : (half + b + 1) * 128] = jnp.where(left, pltpu.roll(even, 64, 1), odd)
    pick = pick_ref[...]
    for start in range(0, pack * 128, 256):
        out_ref[:, start : start + 256] = dot(pick, flat[:, start : start + 256].astype(BF16))
    edge_ref[...] = jnp.transpose(dot(pick, edge_scratch[...].astype(BF16)))[: edge_ref.shape[0], :]


def local(
    layer_entry_vectors,
    guessed_lookup_vectors,
    guessed_content_vectors,
    gating_query,
    lane_memory_store,
    prior_step_store,
    fading_blend_ratio,
    learning_speed_blend,
    fading_left_factor,
    fading_right_factor,
    fading_offset,
    learning_speed_left,
    learning_speed_right,
    learning_speed_offset,
    erasing_lookup_factor,
    written_lookup_factor,
    present_reward_factors,
    lane_standard_factor,
    lane_standard_offset,
    caller_memory_directory,
    kept_target_place,
    caller_sequence,
    approved_guesses,
):
    blocks = lax.axis_size("blk")
    groups = lax.axis_size("head")
    requests, steps, width = layer_entry_vectors.shape
    heads, halves = caller_memory_directory.shape[1:]
    slot_dev = lane_memory_store.shape[1]
    slot_width = lane_memory_store.shape[2]
    pack = slot_width // 128
    per_peer = slot_dev // blocks
    edge_rows = prior_step_store.shape[2]
    rows = requests * steps
    rank = fading_left_factor.shape[1]
    sds = jax.ShapeDtypeStruct

    def exchange(x, axis):
        return lax.all_to_all(
            x, axis, split_axis=0, concat_axis=0, tiled=True, axis_index_groups=[list(order_of(blocks))]
        )

    read_table = caller_memory_directory.transpose(1, 2, 0)
    write_table = kept_target_place.transpose(1, 2, 0)
    pieces = 1
    (sent,) = call(
        functools.partial(send_kernel, blocks, requests, per_peer, pieces),
        (pltpu.HBM((blocks * (per_peer + 1), pack, 128), BF16),),
        raw=(caller_sequence, read_table, lane_memory_store[0], prior_step_store[0].T),
        raw_outs=(0,),
        scratch=[
            pltpu.SMEM(caller_sequence.shape, I32),
            pltpu.VMEM(read_table.shape, I32),
            pltpu.VMEM((slot_dev, slot_width), F32),
            pltpu.VMEM((edge_rows, slot_dev), F32),
            pltpu.VMEM((slot_dev, slot_width), F32),
            pltpu.VMEM((slot_dev, pack, 128), F32),
            pltpu.VMEM((slot_dev, slot_dev), F32),
            pltpu.VMEM((blocks * (per_peer + 1), pack, 128), BF16),
            pltpu.SemaphoreType.DMA((3,)),
            pltpu.SemaphoreType.DMA((2 * pieces,)),
            pltpu.SemaphoreType.DMA((8,)),
        ],
    )
    got = exchange(sent.reshape(blocks, (per_peer + 1) * pack, 128), "blk")
    got = got.reshape(blocks * (per_peer + 1), pack, 128)
    layer = layer_entry_vectors.reshape(rows, width)
    key = guessed_lookup_vectors.reshape(rows, width)
    value = guessed_content_vectors.reshape(rows, width)
    vectors = (
        fading_blend_ratio, learning_speed_blend, fading_offset, learning_speed_offset, erasing_lookup_factor,
        written_lookup_factor, present_reward_factors, lane_standard_factor, lane_standard_offset,
    )
    arrays = (fading_left_factor.T, learning_speed_left.T, fading_right_factor, learning_speed_right)
    one = sds((requests, width), F32)
    wide = sds((rows, width), BF16)
    left = sds((rank, width), BF16)
    (
        partial_sums, first_lines, picked, vector, left_decay, left_rate, right_decay, right_rate,
    ) = call(
        functools.partial(shift_kernel, requests, len(vectors)),
        (sds((rows, 2 * rank), BF16), one, one, sds((16, width), F32), left, left, left, left),
        raw=(caller_sequence, approved_guesses, *(x.reshape(1, width) for x in vectors), layer, *arrays),
        scratch=[
            pltpu.SMEM(caller_sequence.shape, I32),
            pltpu.SMEM(approved_guesses.shape, I32),
            pltpu.VMEM((rows, width), BF16),
            pltpu.VMEM((rows, width), F32),
            pltpu.SemaphoreType.DMA((3,)),
            pltpu.SemaphoreType.DMA((len(vectors),)),
            pltpu.SemaphoreType.DMA((len(arrays),)),
        ],
    )

    def from_group(x):
        return [x] + [lax.ppermute(x, "head", [(g, g ^ d) for g in range(groups)]) for d in range(1, groups)]

    parts = from_group(partial_sums)
    head_width = width // heads
    square = sds((slot_dev, slot_dev), BF16)
    index, pick_in, pick_out, key_near, unit, value_t, unit_first, key_first, value_first = call(
        functools.partial(index_kernel, blocks, requests, per_peer, heads),
        (
            sds((8, slot_dev), I32), square, square, wide, sds((rows, width), F32),
            sds((requests, head_width, heads * steps), BF16),
            one, one, one,
        ),
        near=(vector,),
        raw=(caller_sequence, approved_guesses, read_table, write_table, key, value),
        held=(first_lines, picked, left_decay, left_rate, right_decay, right_rate),
        scratch=[
            pltpu.SMEM(caller_sequence.shape, I32),
            pltpu.SMEM(approved_guesses.shape, I32),
            pltpu.VMEM(read_table.shape, I32),
            pltpu.VMEM(write_table.shape, I32),
            pltpu.VMEM((rows, width), BF16),
            pltpu.VMEM((heads * halves, write_table.shape[2]), I32),
            pltpu.SemaphoreType.DMA((6,)),
        ],
    )
    a_lines, k_lines, b_lines, scale, key_mod, last, solve, through, added = call(
        functools.partial(prepare_kernel, requests, heads, groups),
        (
            wide, wide, wide, wide, wide, one,
            sds((2, steps, requests, heads * steps), F32),
            sds((requests, head_width, width), BF16),
            sds((requests, head_width, width), BF16),
        ),
        near=(*parts, vector, right_decay, right_rate, key_near, unit, value_t),
        loose=(index,),
        held=(pick_in, pick_out, first_lines, picked, left_decay, left_rate, unit_first, key_first, value_first),
        scratch=[
            pltpu.VMEM((requests, steps, 2 * heads * steps), F32),
            pltpu.VMEM((2, requests, steps, heads * steps), F32),
            pltpu.VMEM((rows, width), F32),
            pltpu.VMEM((rows, width), BF16),
            pltpu.VMEM((rows, width), BF16),
            pltpu.SMEM((8, slot_dev), I32),
            pltpu.SemaphoreType.DMA,
        ],
    )
    read_later = (scale, key_mod, a_lines, k_lines, b_lines, solve, value_t, pick_out)
    state_later = (vector, right_decay, right_rate, key_first, last, through, added)
    first_sums, edge = call(
        functools.partial(first_kernel, requests, heads, halves, per_peer),
        (sds((requests, 2 * rank), F32), one),
        near=(pick_in, got, first_lines, vector, left_decay, left_rate),
        held=(index, unit_first, value_first, picked, *state_later[1:], *read_later),
        scratch=[pltpu.VMEM((slot_dev, 128), F32), pltpu.VMEM((slot_dev, 128), F32)],
    )
    first_parts = from_group(first_sums)
    state, change, edge_blocks = call(
        functools.partial(layout_kernel, requests, heads, halves, per_peer),
        (
            sds((requests, head_width, width), BF16),
            sds((requests, head_width, 2 * heads), BF16),
            sds((blocks, pack, 128), BF16),
        ),
        scalars=(index,),
        near=(got, unit_first, value_first, edge, picked),
        held=(*state_later, *read_later),
        scratch=[pltpu.VMEM((slot_dev, 128), F32)],
    )
    back, after, key_mod_first = call(
        functools.partial(state_kernel, requests, heads, halves, per_peer, groups),
        (
            pltpu.HBM((blocks * (per_peer + 1), pack, 128), BF16),
            sds((requests, head_width, width), BF16),
            one,
        ),
        near=(
            *first_parts, state, change, edge_blocks, unit_first, key_first, last, through, added,
            vector, right_decay, right_rate,
        ),
        loose=(index,),
        held=read_later,
        scratch=[
            pltpu.VMEM((requests, head_width, width), F32),
            pltpu.SMEM((8, slot_dev), I32),
            pltpu.SemaphoreType.DMA,
        ],
    )
    back = exchange(back.reshape(blocks, (per_peer + 1) * pack, 128), "blk")
    back = back.reshape(blocks * (per_peer + 1), pack, 128)
    recept = call(
        lines_kernel,
        (sds((rows // groups, width), BF16),) * groups,
        far=(gating_query,),
        held=(vector, after, key_mod_first, *read_later),
        scratch=[pltpu.VMEM((rows // groups, width), F32)],
    )
    recept = [recept[0]] + [
        lax.ppermute(recept[d], "head", [(g, g ^ d) for g in range(groups)]) for d in range(1, groups)
    ]
    (result,) = call(
        functools.partial(read_kernel, requests, heads, groups),
        (pltpu.HBM((rows, width), BF16),),
        near=(*recept, scale, key_mod, key_mod_first, a_lines, k_lines, b_lines, solve, after, value_t, vector),
        far=(value,),
        held=(pick_out,),
        scratch=[
            pltpu.VMEM((rows, width), BF16),
            pltpu.VMEM((requests, steps, 2 * heads * steps), F32),
            pltpu.VMEM((2, requests, steps, heads * steps), F32),
            pltpu.VMEM((rows, width), F32),
        ],
    )
    new_states, new_edges = call(
        functools.partial(place_kernel, per_peer),
        (pltpu.HBM((slot_dev, slot_width), F32), pltpu.HBM((edge_rows, slot_dev), F32)),
        near=(pick_out, back),
        scratch=[
            pltpu.VMEM((slot_dev, pack, 128), F32),
            pltpu.VMEM((slot_dev, slot_width), F32),
            pltpu.VMEM((slot_dev, 128), F32),
        ],
    )
    return (result.reshape(requests, steps, width), new_states[None], new_edges.T[None])


def solution(mesh):
    return jax.shard_map(
        local,
        mesh=mesh,
        in_specs=(
            P("blk", None, "head"),
            P("blk", None, "head"),
            P("blk", None, "head"),
            P("blk", "head", None),
            P("head", "blk", None),
            P("head", "blk", None),
            P("head"),
            P("head"),
            P("head", None),
            P(None, "head"),
            P("head"),
            P("head", None),
            P(None, "head"),
            P("head"),
            P("head"),
            P("head"),
            P("head"),
            P("head"),
            P("head"),
            P(None, "head", None),
            P(None, "head", None),
            P(),
            P(),
        ),
        out_specs=(P("blk", None, "head"), P("head", "blk", None), P("head", "blk", None)),
        check_vma=False,
    )
```

```python
import functools

import jax
import jax.numpy as jnp
from jax import lax
from jax.experimental import pallas as pl
from jax.experimental.pallas import tpu as pltpu
from jax.sharding import PartitionSpec as P

EPSILON = 1e-05
NORM_EPSILON = 0.00064
DECAY_SCALE = 0.6065306597126334
F32 = jnp.float32
BF16 = jnp.bfloat16
I32 = jnp.int32
NT = (((1,), (1,)), ((), ()))
NN = (((1,), (0,)), ((), ()))


def call(kernel, outs, scalars=(), near=(), far=(), raw=(), loose=(), held=(), scratch=(), raw_outs=(), vmem=16):
    reads = len(scalars) + len(near) + len(far) + len(raw) + len(loose)

    def body(*refs):
        kernel(*refs[:reads], *refs[reads + len(held) :])

    args = [*scalars]
    args += [*near]
    args += [pltpu.with_memory_space_constraint(x, pltpu.HBM) for x in (*far, *raw)]
    specs = [pl.BlockSpec(memory_space=pltpu.SMEM)] * len(scalars)
    specs += [pl.BlockSpec(memory_space=pltpu.VMEM)] * (len(near) + len(far))
    specs += [pl.BlockSpec(memory_space=pltpu.HBM)] * (len(raw) + len(loose) + len(held))
    return pl.pallas_call(
        body,
        out_shape=outs,
        in_specs=specs,
        out_specs=tuple(
            pl.BlockSpec(memory_space=pltpu.HBM if i in raw_outs else pltpu.VMEM) for i in range(len(outs))
        ),
        scratch_shapes=list(scratch),
        compiler_params=pltpu.CompilerParams(vmem_limit_bytes=vmem * 1024 * 1024),
        cost_estimate=pl.CostEstimate(flops=1 << 20, bytes_accessed=1 << 20, transcendentals=0),
    )(*args, *loose, *held)


def dot(a, b, dims=NN):
    return lax.dot_general(a, b, dims, preferred_element_type=F32)


def split(x):
    high = x.astype(BF16)
    return high, (x - high.astype(F32)).astype(BF16)


def group_sum(x, width):
    rows, lanes = x.shape
    block = max(width, 128)
    ones = (
        lax.broadcasted_iota(I32, (block, block), 0) // width
        == lax.broadcasted_iota(I32, (block, block), 1) // width
    ).astype(BF16)
    high, low = split(x)
    parts = []
    for start in range(0, lanes, block):
        cut = slice(start, start + block)
        parts.append(dot(high[:, cut], ones) + dot(low[:, cut], ones))
    return jnp.concatenate(parts, axis=1)


def order_of(blocks):
    return (4, 5, 7, 6, 2, 3, 1, 0) if blocks == 8 else tuple(range(blocks))


def seat_of(block, blocks):
    order = order_of(blocks)
    if order == tuple(range(blocks)):
        return block
    seat = jnp.zeros_like(block)
    for i, b in enumerate(order):
        seat = jnp.where(block == b, i, seat)
    return seat


def positions(seq_ref, count):
    lane = lax.broadcasted_iota(I32, (1, count), 1)

    def block(b, acc):
        for k in range(8):
            acc = jnp.where(lane == seq_ref[b * 8 + k], b * 8 + k, acc)
        return acc

    return lax.fori_loop(0, count // 8, block, jnp.zeros((1, count), I32))


def place_of_slot(table_ref, position, base, blocks, per_peer, requests, slot_dev):
    heads, halves, count = table_ref.shape
    slot = lax.broadcasted_iota(I32, (slot_dev, count), 0) + base
    named = jnp.zeros((slot_dev, count), F32)
    for h in range(heads):
        for c in range(halves):
            named = jnp.where(table_ref[h, c : c + 1, :] == slot, 1.0, named)
    other_of = jnp.broadcast_to(seat_of(position // requests, blocks), (16, count)).astype(F32).astype(BF16)
    other = dot(other_of, named.astype(BF16), NT)[0:1, :].astype(I32)
    rows = max(16, blocks)
    mask = other == lax.broadcasted_iota(I32, (rows, slot_dev), 0)
    before = (
        lax.broadcasted_iota(I32, (slot_dev, slot_dev), 0)
        < lax.broadcasted_iota(I32, (slot_dev, slot_dev), 1)
    ).astype(F32).astype(BF16)
    ahead = dot(mask.astype(F32).astype(BF16), before)
    rank = jnp.sum(jnp.where(mask, ahead, 0.0), axis=0, keepdims=True).astype(I32)
    return other * per_peer + rank


def place_of_item(table_ref, lines_ref, position, first, blocks, requests, slot_dev):
    heads, halves, count = table_ref.shape
    per_item = heads * halves
    items = requests * per_item
    mine = (
        jnp.broadcast_to(position, (16, count)) - first == lax.broadcasted_iota(I32, (16, count), 0)
    ).astype(F32).astype(BF16)
    for h in range(heads):
        lines_ref[h * halves : (h + 1) * halves, :] = table_ref[h]
    lines = lines_ref[...]
    lane = lax.broadcasted_iota(I32, (16, items), 1)
    owner = lax.broadcasted_iota(I32, (16, items), 0) == lane // per_item
    of_item = (
        lax.broadcasted_iota(I32, (per_item, items), 0) == lax.broadcasted_iota(I32, (per_item, items), 1) % per_item
    ).astype(F32).astype(BF16)
    seats = seat_of(lines // slot_dev, blocks)
    high = dot(dot(mine, seats.astype(F32).astype(BF16), NT).astype(BF16), of_item)
    low = dot(dot(mine, (lines % slot_dev).astype(F32).astype(BF16), NT).astype(BF16), of_item)
    slots = high * slot_dev + low
    row = jnp.sum(jnp.where(owner, slots, 0.0), axis=0, keepdims=True)
    diagonal = lax.broadcasted_iota(I32, (items, items), 0) == lax.broadcasted_iota(I32, (items, items), 1)
    column = jnp.sum(jnp.where(diagonal, row, 0.0), axis=1, keepdims=True)
    return jnp.sum((column < row).astype(F32), axis=0, keepdims=True).astype(I32)


def send_kernel(
    blocks, requests, per_peer, pieces,
    seq_hbm, read_hbm, state_hbm, edge_hbm,
    out_hbm,
    seq_ref, read_ref, state_ref, edge_ref, flat, scratch, edge_scratch, out_ref, sems, state_sems, out_sems,
):
    slot_dev, slot_width = state_ref.shape
    pack = out_ref.shape[1]
    me = lax.axis_index("blk")
    sources = (seq_hbm, read_hbm, edge_hbm)
    targets = (seq_ref, read_ref, edge_ref)
    copies = [pltpu.make_async_copy(a, b, sems.at[i]) for i, (a, b) in enumerate(zip(sources, targets))]
    state_copies = []
    piece = slot_width // 2 // pieces
    for i in range(pieces):
        for start in (i * piece, slot_width // 2 + i * piece):
            cut = (slice(None), pl.ds(start, piece))
            state_copies.append(
                pltpu.make_async_copy(state_hbm.at[cut], state_ref.at[cut], state_sems.at[len(state_copies)])
            )
    for copy in (*copies[:2], *state_copies, copies[2]):
        copy.start()
    copies[0].wait()
    copies[1].wait()
    position = positions(seq_ref, read_ref.shape[2])
    place = place_of_slot(read_ref, position, me * slot_dev, blocks, per_peer, requests, slot_dev)
    pick = (place == lax.broadcasted_iota(I32, (slot_dev, slot_dev), 0)).astype(F32).astype(BF16)
    left = lax.broadcasted_iota(I32, (slot_dev, 128), 1) < 64
    half = pack // 2
    for b in range(half):
        if b % (half // pieces) == 0:
            state_copies[b // (half // pieces) * 2].wait()
            state_copies[b // (half // pieces) * 2 + 1].wait()
        x = dot(pick, state_ref[:, b * 128 : (b + 1) * 128].astype(BF16))
        y = dot(pick, state_ref[:, (half + b) * 128 : (half + b + 1) * 128].astype(BF16))
        flat[:, 2 * b * 128 : (2 * b + 1) * 128] = jnp.where(left, x, pltpu.roll(y, 64, 1))
        flat[:, (2 * b + 1) * 128 : (2 * b + 2) * 128] = jnp.where(left, pltpu.roll(x, 64, 1), y)
    for row in range(0, slot_dev, 8):
        for j in range(0, pack, 8):
            tiles = [flat[row : row + 8, i * 128 : (i + 1) * 128] for i in range(j, j + 8)]
            scratch[row : row + 8, j : j + 8, :] = jnp.swapaxes(jnp.stack(tiles), 0, 1)
    copies[2].wait()
    edge_rows = edge_ref.shape[0]
    edges = jnp.concatenate([edge_ref[...], jnp.zeros((slot_dev - edge_rows, slot_dev), F32)], axis=0)
    edge_scratch[...] = dot(pick, edges.astype(BF16), NT)
    out_copies = []
    for b in range(blocks):
        at = b * (per_peer + 1)
        out_ref[at : at + per_peer] = scratch[b * per_peer : (b + 1) * per_peer].astype(BF16)
        block = edge_scratch[b * per_peer : (b + 1) * per_peer, :]
        if per_peer < pack:
            block = jnp.concatenate([block, jnp.zeros((pack - per_peer, 128), F32)], axis=0)
        out_ref[at + per_peer] = block.astype(BF16)
        if (b + 1) % (blocks // 8) == 0:
            cut = pl.ds((b + 1 - blocks // 8) * (per_peer + 1), blocks // 8 * (per_peer + 1))
            out_copies.append(pltpu.make_async_copy(out_ref.at[cut], out_hbm.at[cut], out_sems.at[len(out_copies)]))
            out_copies[-1].start()
    for copy in out_copies:
        copy.wait()


def pick_of(place):
    count = place.shape[1]
    row = lax.broadcasted_iota(I32, (count, count), 0)
    lane = lax.broadcasted_iota(I32, (count, count), 1)
    column = jnp.sum(jnp.where(row == lane, place, 0).astype(F32), axis=1, keepdims=True).astype(I32)
    return (column == lane).astype(F32).astype(BF16)


def shift_kernel(requests, lines, *refs):
    scalars_hbm, refs = refs[:2], refs[2:]
    vectors_hbm, refs = refs[:lines], refs[lines:]
    arrays_hbm, refs = refs[:5], refs[5:]
    partial_ref, first_ref, picked_ref, vector_ref = refs[:4]
    arrays, refs = refs[4:8], refs[8:]
    seq_ref, count_ref, layer_ref, line_scratch, sems, line_sem, array_sem = refs
    pairs = zip((*scalars_hbm, arrays_hbm[0]), (seq_ref, count_ref, layer_ref))
    copies = [pltpu.make_async_copy(a, b, sems.at[i]) for i, (a, b) in enumerate(pairs)]
    line_copies = [
        pltpu.make_async_copy(a, vector_ref.at[pl.ds(i, 1)], line_sem.at[i]) for i, a in enumerate(vectors_hbm)
    ]
    array_copies = [
        pltpu.make_async_copy(a, b, array_sem.at[i]) for i, (a, b) in enumerate(zip(arrays_hbm[1:], arrays))
    ]
    for copy in (copies[2], *line_copies[:2], *array_copies, *copies[:2], *line_copies[2:]):
        copy.start()
    copies[2].wait()
    steps = layer_ref.shape[0] // requests
    line = layer_ref[...].astype(F32)
    line_scratch[...] = line
    delta = pltpu.roll(line, 1, 0) - line
    left_decay_ref, left_rate_ref = arrays[:2]
    rank = left_decay_ref.shape[0]
    for copy in (*line_copies, *array_copies, *copies[:2]):
        copy.wait()
    mixed_decay = (line + delta * vector_ref[0:1, :]).astype(BF16)
    mixed_rate = (line + delta * vector_ref[1:2, :]).astype(BF16)
    partial_ref[:, :rank] = dot(mixed_decay, left_decay_ref[...], NT).astype(BF16)
    partial_ref[:, rank:] = dot(mixed_rate, left_rate_ref[...], NT).astype(BF16)
    first = lax.axis_index("blk") * requests
    for p in range(requests):
        first_ref[p : p + 1, :] = line_scratch[p * steps : p * steps + 1, :]
        n = count_ref[seq_ref[first + p]]
        picked_ref[p : p + 1, :] = line_scratch[pl.ds(p * steps + jnp.maximum(n - 1, 0), 1), :]


def index_kernel(blocks, requests, per_peer, heads, vector_ref, *refs):
    hbm, refs = refs[:6], refs[6:]
    index_ref, pick_in_ref, pick_out_ref, key_ref, unit_ref, value_t_ref, *refs = refs
    unit_first_ref, key_first_ref, value_first_ref, *refs = refs
    seq_ref, count_ref, read_ref, write_ref, value_ref, lines_ref, sems = refs
    targets = (seq_ref, count_ref, read_ref, write_ref, key_ref, value_ref)
    copies = [pltpu.make_async_copy(a, b, sems.at[i]) for i, (a, b) in enumerate(zip(hbm, targets))]
    for copy in copies:
        copy.start()
    for copy in copies[:4]:
        copy.wait()
    slot_dev = index_ref.shape[1]
    me = lax.axis_index("blk")
    first = me * requests
    position = positions(seq_ref, read_ref.shape[2])
    place_in = place_of_item(read_ref, lines_ref, position, first, blocks, requests, slot_dev)
    place_out = place_of_item(write_ref, lines_ref, position, first, blocks, requests, slot_dev)
    target = place_of_slot(write_ref, position, me * slot_dev, blocks, per_peer, requests, slot_dev)
    lane = lax.broadcasted_iota(I32, (1, slot_dev), 1)
    counts = jnp.zeros((1, slot_dev), I32)
    for p in range(requests):
        counts = jnp.where(lane == p, count_ref[seq_ref[first + p]], counts)
    index_ref[0:1, :] = place_in
    index_ref[1:2, :] = place_out
    index_ref[2:3, :] = place_in + place_in // per_peer
    index_ref[3:4, :] = counts
    index_ref[4:5, :] = place_out + place_out // per_peer
    index_ref[5:8, :] = jnp.zeros((3, slot_dev), I32)
    pick_in_ref[...] = pick_of(place_in)
    pick_out_ref[...] = pick_of(target)
    copies[4].wait()
    copies[5].wait()
    rows, width = key_ref.shape
    steps = rows // requests
    head_width = width // heads
    u = key_ref[...].astype(F32) * vector_ref[4:5, :]
    unit_ref[...] = u * lax.rsqrt(group_sum(u * u, head_width) + EPSILON)
    ident = ident_of(head_width, width)
    for p in range(requests):
        cut = slice(p * steps, (p + 1) * steps)
        line = slice(p, p + 1)
        unit_first_ref[line, :] = unit_ref[p * steps : p * steps + 1, :]
        key_first_ref[line, :] = key_ref[cut, :].astype(F32)[0:1, :]
        value_first_ref[line, :] = value_ref[cut, :].astype(F32)[0:1, :]
        value_t_ref[p] = dot(ident, expand(value_ref[cut, :], head_width), NT).astype(BF16)


def first_kernel(
    requests, heads, halves, per_peer,
    pick_ref, got_ref, first_ref, vector_ref, left_decay_ref, left_rate_ref,
    out_ref, edge_ref, pool_scratch, item_scratch,
):
    slot_dev = pool_scratch.shape[0]
    per_item = heads * halves
    rows = first_ref.shape[1] // per_item
    for b in range(slot_dev // per_peer):
        block = got_ref[b * (per_peer + 1) + per_peer].astype(F32)
        pool_scratch[b * per_peer : (b + 1) * per_peer, :] = block[:per_peer, :]
    item_scratch[...] = dot(pick_ref[...], pool_scratch[...].astype(BF16))
    for k in range(per_item):
        edge_ref[:, k * rows : (k + 1) * rows] = item_scratch[pl.ds(k, requests, per_item), :rows]
    line = first_ref[...]
    delta = edge_ref[...] - line
    rank = left_decay_ref.shape[0]
    mixed_decay = (line + delta * vector_ref[0:1, :]).astype(BF16)
    mixed_rate = (line + delta * vector_ref[1:2, :]).astype(BF16)
    out_ref[:, :rank] = dot(mixed_decay, left_decay_ref[...], NT)
    out_ref[:, rank:] = dot(mixed_rate, left_rate_ref[...], NT)


def expand(x, head_width):
    steps, lanes = x.shape
    heads = lanes // head_width
    per_block = 128 // head_width
    lane = lax.broadcasted_iota(I32, (steps, 128), 1) // head_width
    zero = jnp.zeros((steps, 128), x.dtype)
    lines = []
    for h in range(heads):
        own = h // per_block
        block = jnp.where(lane == h % per_block, x[:, own * 128 : (own + 1) * 128], zero)
        lines.append(jnp.concatenate([block if b == own else zero for b in range(lanes // 128)], axis=1))
    return jnp.concatenate(lines, axis=0)


def ident_of(head_width, width):
    return (
        lax.broadcasted_iota(I32, (head_width, width), 0)
        == lax.broadcasted_iota(I32, (head_width, width), 1) % head_width
    ).astype(F32).astype(BF16)


def head_rows(line, heads, head_width, shift):
    shape = (2 * heads, line.shape[1])
    own = lax.broadcasted_iota(I32, shape, 1) // head_width + shift
    return jnp.where(own == lax.broadcasted_iota(I32, shape, 0), jnp.broadcast_to(line, shape), 0.0)


def prepare_kernel(
    requests, heads, groups,
    *refs,
):
    parts_refs = refs[:groups]
    (
        vector_ref, right_decay_ref, right_rate_ref, key_ref, unit_ref, value_t_ref, index_near_ref,
        a_ref, k_ref, b_ref, scale_ref, key_mod_ref, last_ref, solve_ref, through_ref, added_ref,
        cross, compact, cum_ref, k_low_ref, b_low_ref, a_t_ref, left_ref, left_low_ref, index_ref, index_sem,
    ) = refs[groups:]
    index_copy = pltpu.make_async_copy(index_near_ref, index_ref, index_sem)
    index_copy.start()
    rows, width = key_ref.shape
    steps = rows // requests
    head_width = width // heads
    rank = right_decay_ref.shape[0]
    total = parts_refs[0][...].astype(F32)
    for ref in parts_refs[1:]:
        total = total + ref[...].astype(F32)
    hidden = jnp.tanh(total[:, :rank]).astype(BF16)
    rate_hidden = total[:, rank:].astype(BF16)
    decay = vector_ref[2:3, :] + dot(hidden, right_decay_ref[...])
    step = lax.broadcasted_iota(I32, (rows, width), 0) % steps
    later = step > 0
    log_forget = jnp.where(later, -DECAY_SCALE * jax.nn.sigmoid(decay), 0.0)
    rate = jax.nn.sigmoid(vector_ref[3:4, :] + dot(rate_hidden, right_rate_ref[...]))
    key = key_ref[...].astype(F32)
    unit = unit_ref[...]
    key_mod = key * (1.0 + (rate - 1.0) * vector_ref[5:6, :])
    key_mod_ref[...] = key_mod.astype(BF16)
    cum = log_forget
    shift = 1
    while shift < steps:
        cum = cum + jnp.where(step >= shift, pltpu.roll(cum, shift, 0), 0.0)
        shift *= 2
    grow = jnp.where(later, jnp.exp(-cum), 0.0)
    cum_ref[...] = cum
    scale = jnp.exp(cum)
    scale_ref[...] = scale.astype(BF16)
    a_ref[...] = jnp.where(later, unit * pltpu.roll(scale, 1, 0), 0.0).astype(BF16)
    k_ref[...], k_low_ref[...] = split(key_mod * grow)
    b_ref[...], b_low_ref[...] = split(rate * unit * grow)
    ident = ident_of(head_width, width)
    lanes = heads * steps
    index_copy.wait()
    for p in range(requests):
        cut = slice(p * steps, (p + 1) * steps)
        n = index_ref[3, p]
        at_n = cum_ref[pl.ds(p * steps + jnp.maximum(n - 1, 0), 1), :]
        last_ref[p : p + 1, :] = jnp.where(n > 0, jnp.exp(at_n), 1.0)
        right = jnp.concatenate([expand(k_ref[cut, :], head_width), expand(b_ref[cut, :], head_width)], axis=0)
        cross[p] = dot(a_ref[cut, :], right, NT)
        a_t_ref[p] = dot(ident, expand(a_ref[cut, :], head_width), NT).astype(BF16)
    lane = lax.broadcasted_iota(I32, (requests, lanes), 1)
    source = lane % steps
    group = lane - source
    solve, carry = [], []
    for t in range(steps):
        weights = jnp.where(source < t, cross[:, t, lanes:], 0.0)
        solve_t = jnp.where(source == t, 1.0, 0.0)
        carry_t = jnp.where(source < t, cross[:, t, :lanes], 0.0)
        for s in range(t):
            weight = jnp.take_along_axis(weights, group + s, axis=1)
            solve_t = solve_t - weight * solve[s]
            carry_t = carry_t - weight * carry[s]
        solve.append(solve_t)
        carry.append(carry_t)
        compact[0, :, t, :] = solve_t
        compact[1, :, t, :] = carry_t
        solve_ref[0, t] = solve_t
        solve_ref[1, t] = carry_t
    for p in range(requests):
        n = index_ref[3, p]
        value_t = value_t_ref[p]
        reach = dot(a_t_ref[p], spread(compact[0, p].astype(BF16), steps), NT)
        high, low = split(compact[1, p])
        removed = dot(value_t, spread(high, steps), NT) + dot(value_t, spread(low, steps), NT)
        left = jnp.concatenate(
            [
                jnp.concatenate([-reach, jnp.zeros_like(reach)], axis=1),
                jnp.concatenate([-removed, value_t.astype(F32)], axis=1),
            ],
            axis=0,
        )
        at = lax.broadcasted_iota(I32, left.shape, 1) % steps
        left_ref[p], left_low_ref[p] = split(jnp.where(at < n, left, 0.0))
    for p in range(requests):
        cut = slice(p * steps, (p + 1) * steps)
        left, left_low = left_ref[p], left_low_ref[p]
        right = jnp.concatenate([expand(b_ref[cut, :], head_width), expand(k_ref[cut, :], head_width)], axis=0)
        right_low = jnp.concatenate([expand(b_low_ref[cut, :], head_width), expand(k_low_ref[cut, :], head_width)], axis=0)
        both = (dot(left, right) + dot(left_low, right) + dot(left, right_low)) * last_ref[p : p + 1, :]
        added_ref[p] = both[head_width:, :].astype(BF16)
        through_ref[p] = both[:head_width, :].astype(BF16)


def spread(x, steps):
    lanes = x.shape[1]
    group = lax.broadcasted_iota(I32, x.shape, 1) // steps
    zero = jnp.zeros_like(x)
    return jnp.concatenate([jnp.where(group == h, x, zero) for h in range(lanes // steps)], axis=0)


def layout_kernel(
    requests, heads, halves, per_peer,
    index_ref, got_ref, unit_first_ref, value_first_ref, edge_ref, picked_ref,
    state_ref, change_ref, edge_out_ref, edge_scratch,
):
    width = unit_first_ref.shape[1]
    head_width = width // heads
    pack = got_ref.shape[1]
    edge_rows = head_width // halves
    ident = ident_of(head_width, width)
    low = lax.broadcasted_iota(I32, (pack, 128), 1) < head_width
    for p in range(requests):
        for c in range(halves):
            for pair in range(heads // 2):
                at = (p * heads + 2 * pair) * halves + c
                even = got_ref[index_ref[2, at]].astype(F32)
                odd = got_ref[index_ref[2, at + halves]].astype(F32)
                top = jnp.where(low, even, pltpu.roll(odd, head_width, 1))
                bottom = jnp.where(low, pltpu.roll(even, head_width, 1), odd)
                lanes = slice(pair * 128, (pair + 1) * 128)
                state_ref[p, 2 * c * pack : (2 * c + 1) * pack, lanes] = top.astype(BF16)
                state_ref[p, (2 * c + 1) * pack : (2 * c + 2) * pack, lanes] = bottom.astype(BF16)
        unit = head_rows(unit_first_ref[p : p + 1, :], heads, head_width, 0).astype(BF16)
        value = head_rows(value_first_ref[p : p + 1, :], heads, head_width, heads).astype(BF16)
        change_ref[p] = (dot(ident, value, NT) - dot(state_ref[p], unit, NT)).astype(BF16)
        new_edge = jnp.where(index_ref[3, p] > 0, picked_ref[p : p + 1, :], edge_ref[p : p + 1, :])
        for k in range(heads * halves):
            lane = k * edge_rows
            line = new_edge[:, lane // 128 * 128 : lane // 128 * 128 + 128]
            if lane % 128:
                line = pltpu.roll(line, 128 - lane % 128, 1)
            edge_scratch[pl.ds(index_ref[1, p * heads * halves + k], 1), :] = line
    for b in range(edge_out_ref.shape[0]):
        block = edge_scratch[b * per_peer : (b + 1) * per_peer, :]
        if per_peer < pack:
            block = jnp.concatenate([block, jnp.zeros((pack - per_peer, 128), F32)], axis=0)
        edge_out_ref[b] = block.astype(BF16)


def state_kernel(
    requests, heads, halves, per_peer, groups,
    *refs,
):
    parts_refs = refs[:groups]
    (
        state_ref, change_ref, edge_blocks_ref, unit_first_ref, key_first_ref, last_ref, through_ref, added_ref,
        vector_ref, right_decay_ref, right_rate_ref, index_near_ref,
        send_ref, after_ref, key_mod_first_ref,
        kept_ref, index_ref, index_sem,
    ) = refs[groups:]
    index_copy = pltpu.make_async_copy(index_near_ref, index_ref, index_sem)
    index_copy.start()
    width = unit_first_ref.shape[1]
    head_width = width // heads
    pack = send_ref.shape[1]
    rank = right_decay_ref.shape[0]
    total = parts_refs[0][...]
    for ref in parts_refs[1:]:
        total = total + ref[...]
    decay = vector_ref[2:3, :] + dot(jnp.tanh(total[:, :rank]).astype(BF16), right_decay_ref[...])
    forget = jnp.exp(-DECAY_SCALE * jax.nn.sigmoid(decay))
    rate = jax.nn.sigmoid(vector_ref[3:4, :] + dot(total[:, rank:].astype(BF16), right_rate_ref[...]))
    key_mod = key_first_ref[...] * (1.0 + (rate - 1.0) * vector_ref[5:6, :])
    key_mod_first_ref[...] = key_mod
    removal = rate * unit_first_ref[...]
    low = lax.broadcasted_iota(I32, (pack, 128), 1) < head_width
    own = lax.broadcasted_iota(I32, (head_width, 128), 1) < head_width
    for b in range(edge_blocks_ref.shape[0]):
        send_ref[b * (per_peer + 1) + per_peer] = edge_blocks_ref[b]
    for p in range(requests):
        line = slice(p, p + 1)
        written = head_rows(removal[line, :], heads, head_width, 0) + head_rows(key_mod[line, :], heads, head_width, heads)
        change = dot(change_ref[p], written.astype(BF16))
        after = state_ref[p].astype(F32) * forget[line, :] + change
        after_ref[p] = after.astype(BF16)
        kept_ref[p] = after * last_ref[line, :] + added_ref[p].astype(F32)
    index_copy.wait()
    for p in range(requests):
        parts = []
        for pair in range(heads // 2):
            lanes = slice(pair * 128, (pair + 1) * 128)
            through = through_ref[p, :, lanes]
            zero = jnp.zeros_like(through)
            through = jnp.concatenate([jnp.where(own, through, zero), jnp.where(own, zero, through)], axis=0)
            parts.append(dot(after_ref[p, :, lanes], through))
        kept = kept_ref[p] + jnp.concatenate(parts, axis=1)
        kept = jnp.where(index_ref[3, p] > 0, kept, state_ref[p].astype(F32))
        for c in range(halves):
            for pair in range(heads // 2):
                top = kept[(2 * c) * pack : (2 * c + 1) * pack, pair * 128 : (pair + 1) * 128]
                bottom = kept[(2 * c + 1) * pack : (2 * c + 2) * pack, pair * 128 : (pair + 1) * 128]
                at = (p * heads + 2 * pair) * halves + c
                even = jnp.where(low, top, pltpu.roll(bottom, head_width, 1))
                odd = jnp.where(low, pltpu.roll(top, head_width, 1), bottom)
                send_ref[index_ref[4, at]] = even.astype(BF16)
                send_ref[index_ref[4, at + halves]] = odd.astype(BF16)


def lines_kernel(gating_ref, *refs):
    *outs, scratch = refs
    requests, part = gating_ref.shape[:2]
    width = scratch.shape[1]
    me = lax.axis_index("head")
    for d, out in enumerate(outs):
        start = pl.multiple_of((me ^ d) * width, 128)
        for p in range(requests):
            scratch[p * part : (p + 1) * part, :] = gating_ref[p, :, pl.ds(start, width)].astype(F32)
        out[...] = scratch[...].astype(BF16)


def read_kernel(
    requests, heads, groups,
    *refs,
):
    return read_body(requests, heads, refs[:groups], *refs[groups:])


def read_body(
    requests, heads,
    recept_refs, scale_ref, key_mod_ref, key_mod_first_ref, a_ref, k_ref, b_ref, solve_ref, state_ref, value_t_ref,
    vector_ref, value_ref,
    result_ref, line_scratch, cross, compact, out_scratch,
):
    rows, width = value_ref.shape
    steps = rows // requests
    head_width = width // heads
    lanes = heads * steps
    part = steps // len(recept_refs)
    row = lax.broadcasted_iota(I32, (rows, rows), 0)
    source = (row % steps // part) ^ lax.axis_index("head")
    source_row = source * (requests * part) + row // steps * part + row % part
    order = (source_row == lax.broadcasted_iota(I32, (rows, rows), 1)).astype(F32).astype(BF16)
    recept = dot(order, jnp.concatenate([ref[...] for ref in recept_refs], axis=0))
    key_mod_first = jnp.broadcast_to(key_mod_first_ref[...][:, None, :], (requests, steps, width)).reshape(rows, width)
    first = lax.broadcasted_iota(I32, (rows, width), 0) % steps == 0
    key_mod = jnp.where(first, key_mod_first, key_mod_ref[...].astype(F32))
    bonus = group_sum(recept * key_mod * vector_ref[6:7, :], head_width)
    line_scratch[...] = (recept * scale_ref[...].astype(F32)).astype(BF16)
    for p in range(requests):
        cut = slice(p * steps, (p + 1) * steps)
        right = jnp.concatenate([expand(k_ref[cut, :], head_width), expand(b_ref[cut, :], head_width)], axis=0)
        cross[p] = dot(line_scratch[cut, :], right, NT)
    lane = lax.broadcasted_iota(I32, (requests, lanes), 1)
    source = lane % steps
    group = lane - source
    for t in range(steps):
        weights = jnp.where(source <= t, cross[:, t, lanes:], 0.0)
        from_a = jnp.zeros((requests, lanes), F32)
        from_v = jnp.where(source <= t, cross[:, t, :lanes], 0.0)
        for s in range(t + 1):
            weight = jnp.take_along_axis(weights, group + s, axis=1)
            from_a = from_a - weight * solve_ref[0, s]
            from_v = from_v - weight * solve_ref[1, s]
        compact[0, :, t, :] = from_a
        compact[1, :, t, :] = from_v
    out_low = lax.broadcasted_iota(I32, (steps, 128), 1) < head_width
    for p in range(requests):
        cut = slice(p * steps, (p + 1) * steps)
        read = jnp.concatenate(
            [spread(compact[0, p].astype(BF16), steps), spread(compact[1, p].astype(BF16), steps)], axis=1
        )
        state = state_ref[p]
        along = dot(state, expand(a_ref[cut, :], head_width), NT).astype(BF16)
        both = jnp.concatenate([along, value_t_ref[p]], axis=1)
        out = dot(read, jnp.concatenate([both, both], axis=0), NT)
        out = out + dot(expand(line_scratch[cut, :], head_width), jnp.concatenate([state, state], axis=0), NT)
        for pair in range(heads // 2):
            at = 2 * pair * steps
            out_scratch[cut, pair * 128 : (pair + 1) * 128] = jnp.where(
                out_low, out[at : at + steps, :], out[at + steps : at + 2 * steps, :]
            )
    out = out_scratch[...]
    centered = out - group_sum(out, head_width) * (1.0 / head_width)
    variance = group_sum(centered * centered, head_width) * (1.0 / head_width)
    line = centered * lax.rsqrt(variance + NORM_EPSILON) * vector_ref[7:8, :] + vector_ref[8:9, :]
    result_ref[...] = (line + bonus * value_ref[...].astype(F32)).astype(BF16)


def place_kernel(per_peer, pick_ref, back_ref, out_ref, edge_ref, scratch, flat, edge_scratch):
    slot_dev = out_ref.shape[0]
    pack = back_ref.shape[1]
    for b in range(slot_dev // per_peer):
        at = b * (per_peer + 1)
        scratch[b * per_peer : (b + 1) * per_peer] = back_ref[at : at + per_peer].astype(F32)
        edge_scratch[b * per_peer : (b + 1) * per_peer, :] = back_ref[at + per_peer].astype(F32)[:per_peer, :]
    left = lax.broadcasted_iota(I32, (8, 128), 1) < 64
    half = pack // 2
    for row in range(0, slot_dev, 8):
        for j in range(0, pack, 8):
            tiles = jnp.swapaxes(scratch[row : row + 8, j : j + 8, :], 0, 1)
            for i in range(4):
                even, odd = tiles[2 * i], tiles[2 * i + 1]
                b = j // 2 + i
                flat[row : row + 8, b * 128 : (b + 1) * 128] = jnp.where(left, even, pltpu.roll(odd, 64, 1))
                flat[row : row + 8, (half + b) * 128 : (half + b + 1) * 128] = jnp.where(left, pltpu.roll(even, 64, 1), odd)
    pick = pick_ref[...]
    for start in range(0, pack * 128, 256):
        out_ref[:, start : start + 256] = dot(pick, flat[:, start : start + 256].astype(BF16))
    edge_ref[...] = jnp.transpose(dot(pick, edge_scratch[...].astype(BF16)))[: edge_ref.shape[0], :]


def local(
    layer_entry_vectors,
    guessed_lookup_vectors,
    guessed_content_vectors,
    gating_query,
    lane_memory_store,
    prior_step_store,
    fading_blend_ratio,
    learning_speed_blend,
    fading_left_factor,
    fading_right_factor,
    fading_offset,
    learning_speed_left,
    learning_speed_right,
    learning_speed_offset,
    erasing_lookup_factor,
    written_lookup_factor,
    present_reward_factors,
    lane_standard_factor,
    lane_standard_offset,
    caller_memory_directory,
    kept_target_place,
    caller_sequence,
    approved_guesses,
):
    blocks = lax.axis_size("blk")
    groups = lax.axis_size("head")
    requests, steps, width = layer_entry_vectors.shape
    heads, halves = caller_memory_directory.shape[1:]
    slot_dev = lane_memory_store.shape[1]
    slot_width = lane_memory_store.shape[2]
    pack = slot_width // 128
    per_peer = slot_dev // blocks
    edge_rows = prior_step_store.shape[2]
    rows = requests * steps
    rank = fading_left_factor.shape[1]
    sds = jax.ShapeDtypeStruct

    def exchange(x, axis):
        return lax.all_to_all(
            x, axis, split_axis=0, concat_axis=0, tiled=True, axis_index_groups=[list(order_of(blocks))]
        )

    read_table = caller_memory_directory.transpose(1, 2, 0)
    write_table = kept_target_place.transpose(1, 2, 0)
    pieces = 1
    (sent,) = call(
        functools.partial(send_kernel, blocks, requests, per_peer, pieces),
        (pltpu.HBM((blocks * (per_peer + 1), pack, 128), BF16),),
        raw=(caller_sequence, read_table, lane_memory_store[0], prior_step_store[0].T),
        raw_outs=(0,),
        scratch=[
            pltpu.SMEM(caller_sequence.shape, I32),
            pltpu.VMEM(read_table.shape, I32),
            pltpu.VMEM((slot_dev, slot_width), F32),
            pltpu.VMEM((edge_rows, slot_dev), F32),
            pltpu.VMEM((slot_dev, slot_width), F32),
            pltpu.VMEM((slot_dev, pack, 128), F32),
            pltpu.VMEM((slot_dev, slot_dev), F32),
            pltpu.VMEM((blocks * (per_peer + 1), pack, 128), BF16),
            pltpu.SemaphoreType.DMA((3,)),
            pltpu.SemaphoreType.DMA((2 * pieces,)),
            pltpu.SemaphoreType.DMA((8,)),
        ],
    )
    got = exchange(sent.reshape(blocks, (per_peer + 1) * pack, 128), "blk")
    got = got.reshape(blocks * (per_peer + 1), pack, 128)
    layer = layer_entry_vectors.reshape(rows, width)
    key = guessed_lookup_vectors.reshape(rows, width)
    value = guessed_content_vectors.reshape(rows, width)
    vectors = (
        fading_blend_ratio, learning_speed_blend, fading_offset, learning_speed_offset, erasing_lookup_factor,
        written_lookup_factor, present_reward_factors, lane_standard_factor, lane_standard_offset,
    )
    arrays = (fading_left_factor.T, learning_speed_left.T, fading_right_factor, learning_speed_right)
    one = sds((requests, width), F32)
    wide = sds((rows, width), BF16)
    left = sds((rank, width), BF16)
    (
        partial_sums, first_lines, picked, vector, left_decay, left_rate, right_decay, right_rate,
    ) = call(
        functools.partial(shift_kernel, requests, len(vectors)),
        (sds((rows, 2 * rank), BF16), one, one, sds((16, width), F32), left, left, left, left),
        raw=(caller_sequence, approved_guesses, *(x.reshape(1, width) for x in vectors), layer, *arrays),
        scratch=[
            pltpu.SMEM(caller_sequence.shape, I32),
            pltpu.SMEM(approved_guesses.shape, I32),
            pltpu.VMEM((rows, width), BF16),
            pltpu.VMEM((rows, width), F32),
            pltpu.SemaphoreType.DMA((3,)),
            pltpu.SemaphoreType.DMA((len(vectors),)),
            pltpu.SemaphoreType.DMA((len(arrays),)),
        ],
    )

    def from_group(x):
        return [x] + [lax.ppermute(x, "head", [(g, g ^ d) for g in range(groups)]) for d in range(1, groups)]

    parts = from_group(partial_sums)
    head_width = width // heads
    square = sds((slot_dev, slot_dev), BF16)
    index, pick_in, pick_out, key_near, unit, value_t, unit_first, key_first, value_first = call(
        functools.partial(index_kernel, blocks, requests, per_peer, heads),
        (
            sds((8, slot_dev), I32), square, square, wide, sds((rows, width), F32),
            sds((requests, head_width, heads * steps), BF16),
            one, one, one,
        ),
        near=(vector,),
        raw=(caller_sequence, approved_guesses, read_table, write_table, key, value),
        held=(first_lines, picked, left_decay, left_rate, right_decay, right_rate),
        scratch=[
            pltpu.SMEM(caller_sequence.shape, I32),
            pltpu.SMEM(approved_guesses.shape, I32),
            pltpu.VMEM(read_table.shape, I32),
            pltpu.VMEM(write_table.shape, I32),
            pltpu.VMEM((rows, width), BF16),
            pltpu.VMEM((heads * halves, write_table.shape[2]), I32),
            pltpu.SemaphoreType.DMA((6,)),
        ],
    )
    a_lines, k_lines, b_lines, scale, key_mod, last, solve, through, added = call(
        functools.partial(prepare_kernel, requests, heads, groups),
        (
            wide, wide, wide, wide, wide, one,
            sds((2, steps, requests, heads * steps), F32),
            sds((requests, head_width, width), BF16),
            sds((requests, head_width, width), BF16),
        ),
        near=(*parts, vector, right_decay, right_rate, key_near, unit, value_t),
        loose=(index,),
        held=(pick_in, pick_out, first_lines, picked, left_decay, left_rate, unit_first, key_first, value_first),
        scratch=[
            pltpu.VMEM((requests, steps, 2 * heads * steps), F32),
            pltpu.VMEM((2, requests, steps, heads * steps), F32),
            pltpu.VMEM((rows, width), F32),
            pltpu.VMEM((rows, width), BF16),
            pltpu.VMEM((rows, width), BF16),
            pltpu.VMEM((requests, head_width, heads * steps), BF16),
            pltpu.VMEM((requests, 2 * head_width, 2 * heads * steps), BF16),
            pltpu.VMEM((requests, 2 * head_width, 2 * heads * steps), BF16),
            pltpu.SMEM((8, slot_dev), I32),
            pltpu.SemaphoreType.DMA,
        ],
    )
    read_later = (scale, key_mod, a_lines, k_lines, b_lines, solve, value_t, pick_out)
    state_later = (vector, right_decay, right_rate, key_first, last, through, added)
    first_sums, edge = call(
        functools.partial(first_kernel, requests, heads, halves, per_peer),
        (sds((requests, 2 * rank), F32), one),
        near=(pick_in, got, first_lines, vector, left_decay, left_rate),
        held=(index, unit_first, value_first, picked, *state_later[1:], *read_later),
        scratch=[pltpu.VMEM((slot_dev, 128), F32), pltpu.VMEM((slot_dev, 128), F32)],
    )
    first_parts = from_group(first_sums)
    state, change, edge_blocks = call(
        functools.partial(layout_kernel, requests, heads, halves, per_peer),
        (
            sds((requests, head_width, width), BF16),
            sds((requests, head_width, 2 * heads), BF16),
            sds((blocks, pack, 128), BF16),
        ),
        scalars=(index,),
        near=(got, unit_first, value_first, edge, picked),
        held=(*state_later, *read_later),
        scratch=[pltpu.VMEM((slot_dev, 128), F32)],
    )
    back, after, key_mod_first = call(
        functools.partial(state_kernel, requests, heads, halves, per_peer, groups),
        (
            pltpu.HBM((blocks * (per_peer + 1), pack, 128), BF16),
            sds((requests, head_width, width), BF16),
            one,
        ),
        near=(
            *first_parts, state, change, edge_blocks, unit_first, key_first, last, through, added,
            vector, right_decay, right_rate,
        ),
        loose=(index,),
        held=read_later,
        scratch=[
            pltpu.VMEM((requests, head_width, width), F32),
            pltpu.SMEM((8, slot_dev), I32),
            pltpu.SemaphoreType.DMA,
        ],
    )
    back = exchange(back.reshape(blocks, (per_peer + 1) * pack, 128), "blk")
    back = back.reshape(blocks * (per_peer + 1), pack, 128)
    recept = call(
        lines_kernel,
        (sds((rows // groups, width), BF16),) * groups,
        far=(gating_query,),
        held=(vector, after, key_mod_first, *read_later),
        scratch=[pltpu.VMEM((rows // groups, width), F32)],
    )
    recept = [recept[0]] + [
        lax.ppermute(recept[d], "head", [(g, g ^ d) for g in range(groups)]) for d in range(1, groups)
    ]
    (result,) = call(
        functools.partial(read_kernel, requests, heads, groups),
        (pltpu.HBM((rows, width), BF16),),
        near=(*recept, scale, key_mod, key_mod_first, a_lines, k_lines, b_lines, solve, after, value_t, vector),
        far=(value,),
        held=(pick_out,),
        scratch=[
            pltpu.VMEM((rows, width), BF16),
            pltpu.VMEM((requests, steps, 2 * heads * steps), F32),
            pltpu.VMEM((2, requests, steps, heads * steps), F32),
            pltpu.VMEM((rows, width), F32),
        ],
    )
    new_states, new_edges = call(
        functools.partial(place_kernel, per_peer),
        (pltpu.HBM((slot_dev, slot_width), F32), pltpu.HBM((edge_rows, slot_dev), F32)),
        near=(pick_out, back),
        scratch=[
            pltpu.VMEM((slot_dev, pack, 128), F32),
            pltpu.VMEM((slot_dev, slot_width), F32),
            pltpu.VMEM((slot_dev, 128), F32),
        ],
    )
    return (result.reshape(requests, steps, width), new_states[None], new_edges.T[None])


def solution(mesh):
    return jax.shard_map(
        local,
        mesh=mesh,
        in_specs=(
            P("blk", None, "head"),
            P("blk", None, "head"),
            P("blk", None, "head"),
            P("blk", "head", None),
            P("head", "blk", None),
            P("head", "blk", None),
            P("head"),
            P("head"),
            P("head", None),
            P(None, "head"),
            P("head"),
            P("head", None),
            P(None, "head"),
            P("head"),
            P("head"),
            P("head"),
            P("head"),
            P("head"),
            P("head"),
            P(None, "head", None),
            P(None, "head", None),
            P(),
            P(),
        ),
        out_specs=(P("blk", None, "head"), P("head", "blk", None), P("head", "blk", None)),
        check_vma=False,
    )
```

```python
import functools

import jax
import jax.numpy as jnp
from jax import lax
from jax.experimental import pallas as pl
from jax.experimental.pallas import tpu as pltpu
from jax.sharding import PartitionSpec as P

EPSILON = 1e-05
NORM_EPSILON = 0.00064
DECAY_SCALE = 0.6065306597126334
F32 = jnp.float32
BF16 = jnp.bfloat16
I32 = jnp.int32
NT = (((1,), (1,)), ((), ()))
NN = (((1,), (0,)), ((), ()))


def call(kernel, outs, scalars=(), near=(), far=(), raw=(), loose=(), held=(), scratch=(), raw_outs=(), vmem=16):
    reads = len(scalars) + len(near) + len(far) + len(raw) + len(loose)

    def body(*refs):
        kernel(*refs[:reads], *refs[reads + len(held) :])

    args = [*scalars]
    args += [*near]
    args += [pltpu.with_memory_space_constraint(x, pltpu.HBM) for x in (*far, *raw)]
    specs = [pl.BlockSpec(memory_space=pltpu.SMEM)] * len(scalars)
    specs += [pl.BlockSpec(memory_space=pltpu.VMEM)] * (len(near) + len(far))
    specs += [pl.BlockSpec(memory_space=pltpu.HBM)] * (len(raw) + len(loose) + len(held))
    return pl.pallas_call(
        body,
        out_shape=outs,
        in_specs=specs,
        out_specs=tuple(
            pl.BlockSpec(memory_space=pltpu.HBM if i in raw_outs else pltpu.VMEM) for i in range(len(outs))
        ),
        scratch_shapes=list(scratch),
        compiler_params=pltpu.CompilerParams(vmem_limit_bytes=vmem * 1024 * 1024),
        cost_estimate=pl.CostEstimate(flops=1 << 20, bytes_accessed=1 << 20, transcendentals=0),
    )(*args, *loose, *held)


def dot(a, b, dims=NN):
    return lax.dot_general(a, b, dims, preferred_element_type=F32)


def split(x):
    high = x.astype(BF16)
    return high, (x - high.astype(F32)).astype(BF16)


def group_sum(x, width):
    rows, lanes = x.shape
    block = max(width, 128)
    ones = (
        lax.broadcasted_iota(I32, (block, block), 0) // width
        == lax.broadcasted_iota(I32, (block, block), 1) // width
    ).astype(BF16)
    high, low = split(x)
    parts = []
    for start in range(0, lanes, block):
        cut = slice(start, start + block)
        parts.append(dot(high[:, cut], ones) + dot(low[:, cut], ones))
    return jnp.concatenate(parts, axis=1)


def order_of(blocks):
    return (4, 5, 7, 6, 2, 3, 1, 0) if blocks == 8 else tuple(range(blocks))


def seat_of(block, blocks):
    order = order_of(blocks)
    if order == tuple(range(blocks)):
        return block
    seat = jnp.zeros_like(block)
    for i, b in enumerate(order):
        seat = jnp.where(block == b, i, seat)
    return seat


def positions(seq_ref, count):
    lane = lax.broadcasted_iota(I32, (1, count), 1)

    def block(b, acc):
        for k in range(8):
            acc = jnp.where(lane == seq_ref[b * 8 + k], b * 8 + k, acc)
        return acc

    return lax.fori_loop(0, count // 8, block, jnp.zeros((1, count), I32))


def place_of_slot(table_ref, position, base, blocks, per_peer, requests, slot_dev):
    heads, halves, count = table_ref.shape
    slot = lax.broadcasted_iota(I32, (slot_dev, count), 0) + base
    named = jnp.zeros((slot_dev, count), F32)
    for h in range(heads):
        for c in range(halves):
            named = jnp.where(table_ref[h, c : c + 1, :] == slot, 1.0, named)
    other_of = jnp.broadcast_to(seat_of(position // requests, blocks), (16, count)).astype(F32).astype(BF16)
    other = dot(other_of, named.astype(BF16), NT)[0:1, :].astype(I32)
    rows = max(16, blocks)
    mask = other == lax.broadcasted_iota(I32, (rows, slot_dev), 0)
    before = (
        lax.broadcasted_iota(I32, (slot_dev, slot_dev), 0)
        < lax.broadcasted_iota(I32, (slot_dev, slot_dev), 1)
    ).astype(F32).astype(BF16)
    ahead = dot(mask.astype(F32).astype(BF16), before)
    rank = jnp.sum(jnp.where(mask, ahead, 0.0), axis=0, keepdims=True).astype(I32)
    return other * per_peer + rank


def place_of_item(table_ref, lines_ref, position, first, blocks, requests, slot_dev):
    heads, halves, count = table_ref.shape
    per_item = heads * halves
    items = requests * per_item
    mine = (
        jnp.broadcast_to(position, (16, count)) - first == lax.broadcasted_iota(I32, (16, count), 0)
    ).astype(F32).astype(BF16)
    for h in range(heads):
        lines_ref[h * halves : (h + 1) * halves, :] = table_ref[h]
    lines = lines_ref[...]
    lane = lax.broadcasted_iota(I32, (16, items), 1)
    owner = lax.broadcasted_iota(I32, (16, items), 0) == lane // per_item
    of_item = (
        lax.broadcasted_iota(I32, (per_item, items), 0) == lax.broadcasted_iota(I32, (per_item, items), 1) % per_item
    ).astype(F32).astype(BF16)
    seats = seat_of(lines // slot_dev, blocks)
    high = dot(dot(mine, seats.astype(F32).astype(BF16), NT).astype(BF16), of_item)
    low = dot(dot(mine, (lines % slot_dev).astype(F32).astype(BF16), NT).astype(BF16), of_item)
    slots = high * slot_dev + low
    row = jnp.sum(jnp.where(owner, slots, 0.0), axis=0, keepdims=True)
    diagonal = lax.broadcasted_iota(I32, (items, items), 0) == lax.broadcasted_iota(I32, (items, items), 1)
    column = jnp.sum(jnp.where(diagonal, row, 0.0), axis=1, keepdims=True)
    return jnp.sum((column < row).astype(F32), axis=0, keepdims=True).astype(I32)


def send_kernel(
    blocks, requests, per_peer, pieces,
    seq_hbm, read_hbm, state_hbm, edge_hbm,
    out_hbm,
    seq_ref, read_ref, state_ref, edge_ref, flat, edge_scratch, out_ref, sems, state_sems, out_sems,
):
    slot_dev, slot_width = state_ref.shape
    pack = out_ref.shape[1]
    me = lax.axis_index("blk")
    sources = (seq_hbm, read_hbm, edge_hbm)
    targets = (seq_ref, read_ref, edge_ref)
    copies = [pltpu.make_async_copy(a, b, sems.at[i]) for i, (a, b) in enumerate(zip(sources, targets))]
    state_copies = []
    piece = slot_width // 2 // pieces
    for i in range(pieces):
        for start in (i * piece, slot_width // 2 + i * piece):
            cut = (slice(None), pl.ds(start, piece))
            state_copies.append(
                pltpu.make_async_copy(state_hbm.at[cut], state_ref.at[cut], state_sems.at[len(state_copies)])
            )
    for copy in (*copies[:2], *state_copies, copies[2]):
        copy.start()
    copies[0].wait()
    copies[1].wait()
    position = positions(seq_ref, read_ref.shape[2])
    place = place_of_slot(read_ref, position, me * slot_dev, blocks, per_peer, requests, slot_dev)
    pick = (place == lax.broadcasted_iota(I32, (slot_dev, slot_dev), 0)).astype(F32).astype(BF16)
    left = lax.broadcasted_iota(I32, (slot_dev, 128), 1) < 64
    half = pack // 2
    for b in range(half):
        if b % (half // pieces) == 0:
            state_copies[b // (half // pieces) * 2].wait()
            state_copies[b // (half // pieces) * 2 + 1].wait()
        x = dot(pick, state_ref[:, b * 128 : (b + 1) * 128].astype(BF16))
        y = dot(pick, state_ref[:, (half + b) * 128 : (half + b + 1) * 128].astype(BF16))
        flat[:, 2 * b * 128 : (2 * b + 1) * 128] = jnp.where(left, x, pltpu.roll(y, 64, 1))
        flat[:, (2 * b + 1) * 128 : (2 * b + 2) * 128] = jnp.where(left, pltpu.roll(x, 64, 1), y)
    copies[2].wait()
    edge_rows = edge_ref.shape[0]
    edges = jnp.concatenate([edge_ref[...], jnp.zeros((slot_dev - edge_rows, slot_dev), F32)], axis=0)
    edge_scratch[...] = dot(pick, edges.astype(BF16), NT)
    out_copies = []
    for row in range(0, slot_dev, 8):
        parts = []
        for j in range(0, pack, 8):
            tiles = [flat[row : row + 8, i * 128 : (i + 1) * 128] for i in range(j, j + 8)]
            parts.append(jnp.swapaxes(jnp.stack(tiles), 0, 1))
        for i in range(8):
            place = row + i
            block = jnp.concatenate([part[i] for part in parts], axis=0)
            out_ref[place + place // per_peer] = block.astype(BF16)
        if (row + 8) % (slot_dev // 8) == 0:
            first, last = (row + 8) * 8 // slot_dev * (blocks // 8) - blocks // 8, (row + 8) * 8 // slot_dev * (blocks // 8)
            for b in range(first, last):
                block = edge_scratch[b * per_peer : (b + 1) * per_peer, :]
                if per_peer < pack:
                    block = jnp.concatenate([block, jnp.zeros((pack - per_peer, 128), F32)], axis=0)
                out_ref[b * (per_peer + 1) + per_peer] = block.astype(BF16)
            cut = pl.ds(first * (per_peer + 1), (last - first) * (per_peer + 1))
            out_copies.append(pltpu.make_async_copy(out_ref.at[cut], out_hbm.at[cut], out_sems.at[len(out_copies)]))
            out_copies[-1].start()
    for copy in out_copies:
        copy.wait()


def pick_of(place):
    count = place.shape[1]
    row = lax.broadcasted_iota(I32, (count, count), 0)
    lane = lax.broadcasted_iota(I32, (count, count), 1)
    column = jnp.sum(jnp.where(row == lane, place, 0).astype(F32), axis=1, keepdims=True).astype(I32)
    return (column == lane).astype(F32).astype(BF16)


def shift_kernel(requests, lines, *refs):
    scalars_hbm, refs = refs[:2], refs[2:]
    vectors_hbm, refs = refs[:lines], refs[lines:]
    arrays_hbm, refs = refs[:5], refs[5:]
    partial_ref, first_ref, picked_ref, vector_ref = refs[:4]
    arrays, refs = refs[4:8], refs[8:]
    seq_ref, count_ref, layer_ref, line_scratch, sems, line_sem, array_sem = refs
    pairs = zip((*scalars_hbm, arrays_hbm[0]), (seq_ref, count_ref, layer_ref))
    copies = [pltpu.make_async_copy(a, b, sems.at[i]) for i, (a, b) in enumerate(pairs)]
    line_copies = [
        pltpu.make_async_copy(a, vector_ref.at[pl.ds(i, 1)], line_sem.at[i]) for i, a in enumerate(vectors_hbm)
    ]
    array_copies = [
        pltpu.make_async_copy(a, b, array_sem.at[i]) for i, (a, b) in enumerate(zip(arrays_hbm[1:], arrays))
    ]
    for copy in (copies[2], *line_copies[:2], *array_copies, *copies[:2], *line_copies[2:]):
        copy.start()
    copies[2].wait()
    steps = layer_ref.shape[0] // requests
    line = layer_ref[...].astype(F32)
    line_scratch[...] = line
    delta = pltpu.roll(line, 1, 0) - line
    left_decay_ref, left_rate_ref = arrays[:2]
    rank = left_decay_ref.shape[0]
    for copy in (*line_copies, *array_copies, *copies[:2]):
        copy.wait()
    mixed_decay = (line + delta * vector_ref[0:1, :]).astype(BF16)
    mixed_rate = (line + delta * vector_ref[1:2, :]).astype(BF16)
    partial_ref[:, :rank] = dot(mixed_decay, left_decay_ref[...], NT).astype(BF16)
    partial_ref[:, rank:] = dot(mixed_rate, left_rate_ref[...], NT).astype(BF16)
    first = lax.axis_index("blk") * requests
    for p in range(requests):
        first_ref[p : p + 1, :] = line_scratch[p * steps : p * steps + 1, :]
        n = count_ref[seq_ref[first + p]]
        picked_ref[p : p + 1, :] = line_scratch[pl.ds(p * steps + jnp.maximum(n - 1, 0), 1), :]


def index_kernel(blocks, requests, per_peer, heads, vector_ref, *refs):
    hbm, refs = refs[:6], refs[6:]
    index_ref, pick_in_ref, pick_out_ref, key_ref, unit_ref, value_t_ref, *refs = refs
    unit_first_ref, key_first_ref, value_first_ref, *refs = refs
    seq_ref, count_ref, read_ref, write_ref, value_ref, lines_ref, sems = refs
    targets = (seq_ref, count_ref, read_ref, write_ref, key_ref, value_ref)
    copies = [pltpu.make_async_copy(a, b, sems.at[i]) for i, (a, b) in enumerate(zip(hbm, targets))]
    for copy in copies:
        copy.start()
    for copy in copies[:4]:
        copy.wait()
    slot_dev = index_ref.shape[1]
    me = lax.axis_index("blk")
    first = me * requests
    position = positions(seq_ref, read_ref.shape[2])
    place_in = place_of_item(read_ref, lines_ref, position, first, blocks, requests, slot_dev)
    place_out = place_of_item(write_ref, lines_ref, position, first, blocks, requests, slot_dev)
    target = place_of_slot(write_ref, position, me * slot_dev, blocks, per_peer, requests, slot_dev)
    lane = lax.broadcasted_iota(I32, (1, slot_dev), 1)
    counts = jnp.zeros((1, slot_dev), I32)
    for p in range(requests):
        counts = jnp.where(lane == p, count_ref[seq_ref[first + p]], counts)
    index_ref[0:1, :] = place_in
    index_ref[1:2, :] = place_out
    index_ref[2:3, :] = place_in + place_in // per_peer
    index_ref[3:4, :] = counts
    index_ref[4:5, :] = place_out + place_out // per_peer
    index_ref[5:8, :] = jnp.zeros((3, slot_dev), I32)
    pick_in_ref[...] = pick_of(place_in)
    pick_out_ref[...] = pick_of(target)
    copies[4].wait()
    copies[5].wait()
    rows, width = key_ref.shape
    steps = rows // requests
    head_width = width // heads
    u = key_ref[...].astype(F32) * vector_ref[4:5, :]
    unit_ref[...] = u * lax.rsqrt(group_sum(u * u, head_width) + EPSILON)
    ident = ident_of(head_width, width)
    for p in range(requests):
        cut = slice(p * steps, (p + 1) * steps)
        line = slice(p, p + 1)
        unit_first_ref[line, :] = unit_ref[p * steps : p * steps + 1, :]
        key_first_ref[line, :] = key_ref[cut, :].astype(F32)[0:1, :]
        value_first_ref[line, :] = value_ref[cut, :].astype(F32)[0:1, :]
        value_t_ref[p] = dot(ident, expand(value_ref[cut, :], head_width), NT).astype(BF16)


def first_kernel(
    requests, heads, halves, per_peer,
    pick_ref, got_ref, first_ref, vector_ref, left_decay_ref, left_rate_ref,
    out_ref, edge_ref, pool_scratch, item_scratch,
):
    slot_dev = pool_scratch.shape[0]
    per_item = heads * halves
    rows = first_ref.shape[1] // per_item
    for b in range(slot_dev // per_peer):
        block = got_ref[b * (per_peer + 1) + per_peer].astype(F32)
        pool_scratch[b * per_peer : (b + 1) * per_peer, :] = block[:per_peer, :]
    item_scratch[...] = dot(pick_ref[...], pool_scratch[...].astype(BF16))
    for k in range(per_item):
        edge_ref[:, k * rows : (k + 1) * rows] = item_scratch[pl.ds(k, requests, per_item), :rows]
    line = first_ref[...]
    delta = edge_ref[...] - line
    rank = left_decay_ref.shape[0]
    mixed_decay = (line + delta * vector_ref[0:1, :]).astype(BF16)
    mixed_rate = (line + delta * vector_ref[1:2, :]).astype(BF16)
    out_ref[:, :rank] = dot(mixed_decay, left_decay_ref[...], NT)
    out_ref[:, rank:] = dot(mixed_rate, left_rate_ref[...], NT)


def expand(x, head_width):
    steps, lanes = x.shape
    heads = lanes // head_width
    per_block = 128 // head_width
    lane = lax.broadcasted_iota(I32, (steps, 128), 1) // head_width
    zero = jnp.zeros((steps, 128), x.dtype)
    lines = []
    for h in range(heads):
        own = h // per_block
        block = jnp.where(lane == h % per_block, x[:, own * 128 : (own + 1) * 128], zero)
        lines.append(jnp.concatenate([block if b == own else zero for b in range(lanes // 128)], axis=1))
    return jnp.concatenate(lines, axis=0)


def ident_of(head_width, width):
    return (
        lax.broadcasted_iota(I32, (head_width, width), 0)
        == lax.broadcasted_iota(I32, (head_width, width), 1) % head_width
    ).astype(F32).astype(BF16)


def head_rows(line, heads, head_width, shift):
    shape = (2 * heads, line.shape[1])
    own = lax.broadcasted_iota(I32, shape, 1) // head_width + shift
    return jnp.where(own == lax.broadcasted_iota(I32, shape, 0), jnp.broadcast_to(line, shape), 0.0)


def prepare_kernel(
    requests, heads, groups,
    *refs,
):
    parts_refs = refs[:groups]
    (
        vector_ref, right_decay_ref, right_rate_ref, key_ref, unit_ref, value_t_ref, index_near_ref,
        a_ref, k_ref, b_ref, scale_ref, key_mod_ref, last_ref, solve_ref, through_ref, added_ref,
        cross, compact, cum_ref, k_low_ref, b_low_ref, a_t_ref, left_ref, left_low_ref, index_ref, index_sem,
    ) = refs[groups:]
    index_copy = pltpu.make_async_copy(index_near_ref, index_ref, index_sem)
    index_copy.start()
    rows, width = key_ref.shape
    steps = rows // requests
    head_width = width // heads
    rank = right_decay_ref.shape[0]
    total = parts_refs[0][...].astype(F32)
    for ref in parts_refs[1:]:
        total = total + ref[...].astype(F32)
    hidden = jnp.tanh(total[:, :rank]).astype(BF16)
    rate_hidden = total[:, rank:].astype(BF16)
    decay = vector_ref[2:3, :] + dot(hidden, right_decay_ref[...])
    step = lax.broadcasted_iota(I32, (rows, width), 0) % steps
    later = step > 0
    log_forget = jnp.where(later, -DECAY_SCALE * jax.nn.sigmoid(decay), 0.0)
    rate = jax.nn.sigmoid(vector_ref[3:4, :] + dot(rate_hidden, right_rate_ref[...]))
    key = key_ref[...].astype(F32)
    unit = unit_ref[...]
    key_mod = key * (1.0 + (rate - 1.0) * vector_ref[5:6, :])
    key_mod_ref[...] = key_mod.astype(BF16)
    cum = log_forget
    shift = 1
    while shift < steps:
        cum = cum + jnp.where(step >= shift, pltpu.roll(cum, shift, 0), 0.0)
        shift *= 2
    grow = jnp.where(later, jnp.exp(-cum), 0.0)
    cum_ref[...] = cum
    scale = jnp.exp(cum)
    scale_ref[...] = scale
    a_ref[...] = jnp.where(later, unit * pltpu.roll(scale, 1, 0), 0.0).astype(BF16)
    k_ref[...], k_low_ref[...] = split(key_mod * grow)
    b_ref[...], b_low_ref[...] = split(rate * unit * grow)
    ident = ident_of(head_width, width)
    lanes = heads * steps
    index_copy.wait()
    for p in range(requests):
        cut = slice(p * steps, (p + 1) * steps)
        n = index_ref[3, p]
        at_n = cum_ref[pl.ds(p * steps + jnp.maximum(n - 1, 0), 1), :]
        last_ref[p : p + 1, :] = jnp.where(n > 0, jnp.exp(at_n), 1.0)
        right = jnp.concatenate([expand(k_ref[cut, :], head_width), expand(b_ref[cut, :], head_width)], axis=0)
        cross[p] = dot(a_ref[cut, :], right, NT)
        a_t_ref[p] = dot(ident, expand(a_ref[cut, :], head_width), NT).astype(BF16)
    lane = lax.broadcasted_iota(I32, (requests, lanes), 1)
    source = lane % steps
    group = lane - source
    solve, carry = [], []
    for t in range(steps):
        weights = jnp.where(source < t, cross[:, t, lanes:], 0.0)
        solve_t = jnp.where(source == t, 1.0, 0.0)
        carry_t = jnp.where(source < t, cross[:, t, :lanes], 0.0)
        for s in range(t):
            weight = jnp.take_along_axis(weights, group + s, axis=1)
            solve_t = solve_t - weight * solve[s]
            carry_t = carry_t - weight * carry[s]
        solve.append(solve_t)
        carry.append(carry_t)
        compact[0, :, t, :] = solve_t
        compact[1, :, t, :] = carry_t
        solve_ref[0, t] = solve_t
        solve_ref[1, t] = carry_t
    for p in range(requests):
        n = index_ref[3, p]
        value_t = value_t_ref[p]
        reach = dot(a_t_ref[p], spread(compact[0, p].astype(BF16), steps), NT)
        high, low = split(compact[1, p])
        removed = dot(value_t, spread(high, steps), NT) + dot(value_t, spread(low, steps), NT)
        left = jnp.concatenate(
            [
                jnp.concatenate([-reach, jnp.zeros_like(reach)], axis=1),
                jnp.concatenate([-removed, value_t.astype(F32)], axis=1),
            ],
            axis=0,
        )
        at = lax.broadcasted_iota(I32, left.shape, 1) % steps
        left_ref[p], left_low_ref[p] = split(jnp.where(at < n, left, 0.0))
    for p in range(requests):
        cut = slice(p * steps, (p + 1) * steps)
        left, left_low = left_ref[p], left_low_ref[p]
        right = jnp.concatenate([expand(b_ref[cut, :], head_width), expand(k_ref[cut, :], head_width)], axis=0)
        right_low = jnp.concatenate([expand(b_low_ref[cut, :], head_width), expand(k_low_ref[cut, :], head_width)], axis=0)
        both = (dot(left, right) + dot(left_low, right) + dot(left, right_low)) * last_ref[p : p + 1, :]
        added_ref[p] = both[head_width:, :].astype(BF16)
        through_ref[p] = both[:head_width, :].astype(BF16)


def spread(x, steps):
    lanes = x.shape[1]
    group = lax.broadcasted_iota(I32, x.shape, 1) // steps
    zero = jnp.zeros_like(x)
    return jnp.concatenate([jnp.where(group == h, x, zero) for h in range(lanes // steps)], axis=0)


def layout_kernel(
    requests, heads, halves, per_peer,
    got_ref, unit_first_ref, value_first_ref, edge_ref, picked_ref, index_near_ref,
    state_ref, change_ref, edge_out_ref, edge_scratch, value_scratch, index_ref, index_sem,
):
    index_copy = pltpu.make_async_copy(index_near_ref, index_ref, index_sem)
    index_copy.start()
    width = unit_first_ref.shape[1]
    head_width = width // heads
    pack = got_ref.shape[1]
    edge_rows = head_width // halves
    ident = ident_of(head_width, width)
    low = lax.broadcasted_iota(I32, (pack, 128), 1) < head_width
    for p in range(requests):
        value = head_rows(value_first_ref[p : p + 1, :], heads, head_width, heads).astype(BF16)
        value_scratch[p] = dot(ident, value, NT)
    index_copy.wait()
    for p in range(requests):
        for c in range(halves):
            for pair in range(heads // 2):
                at = (p * heads + 2 * pair) * halves + c
                even = got_ref[index_ref[2, at]].astype(F32)
                odd = got_ref[index_ref[2, at + halves]].astype(F32)
                top = jnp.where(low, even, pltpu.roll(odd, head_width, 1))
                bottom = jnp.where(low, pltpu.roll(even, head_width, 1), odd)
                lanes = slice(pair * 128, (pair + 1) * 128)
                state_ref[p, 2 * c * pack : (2 * c + 1) * pack, lanes] = top.astype(BF16)
                state_ref[p, (2 * c + 1) * pack : (2 * c + 2) * pack, lanes] = bottom.astype(BF16)
        unit = head_rows(unit_first_ref[p : p + 1, :], heads, head_width, 0).astype(BF16)
        change_ref[p] = (value_scratch[p] - dot(state_ref[p], unit, NT)).astype(BF16)
        new_edge = jnp.where(index_ref[3, p] > 0, picked_ref[p : p + 1, :], edge_ref[p : p + 1, :])
        for k in range(heads * halves):
            lane = k * edge_rows
            line = new_edge[:, lane // 128 * 128 : lane // 128 * 128 + 128]
            if lane % 128:
                line = pltpu.roll(line, 128 - lane % 128, 1)
            edge_scratch[pl.ds(index_ref[1, p * heads * halves + k], 1), :] = line
    for b in range(edge_out_ref.shape[0]):
        block = edge_scratch[b * per_peer : (b + 1) * per_peer, :]
        if per_peer < pack:
            block = jnp.concatenate([block, jnp.zeros((pack - per_peer, 128), F32)], axis=0)
        edge_out_ref[b] = block.astype(BF16)


def state_kernel(
    requests, heads, halves, per_peer, groups,
    *refs,
):
    parts_refs = refs[:groups]
    (
        state_ref, change_ref, edge_blocks_ref, unit_first_ref, key_first_ref, last_ref, through_ref, added_ref,
        vector_ref, right_decay_ref, right_rate_ref, index_near_ref,
        send_ref, after_ref, key_mod_first_ref,
        kept_ref, index_ref, index_sem,
    ) = refs[groups:]
    index_copy = pltpu.make_async_copy(index_near_ref, index_ref, index_sem)
    index_copy.start()
    width = unit_first_ref.shape[1]
    head_width = width // heads
    pack = send_ref.shape[1]
    rank = right_decay_ref.shape[0]
    total = parts_refs[0][...]
    for ref in parts_refs[1:]:
        total = total + ref[...]
    decay = vector_ref[2:3, :] + dot(jnp.tanh(total[:, :rank]).astype(BF16), right_decay_ref[...])
    forget = jnp.exp(-DECAY_SCALE * jax.nn.sigmoid(decay))
    rate = jax.nn.sigmoid(vector_ref[3:4, :] + dot(total[:, rank:].astype(BF16), right_rate_ref[...]))
    key_mod = key_first_ref[...] * (1.0 + (rate - 1.0) * vector_ref[5:6, :])
    key_mod_first_ref[...] = key_mod
    removal = rate * unit_first_ref[...]
    low = lax.broadcasted_iota(I32, (pack, 128), 1) < head_width
    own = lax.broadcasted_iota(I32, (head_width, 128), 1) < head_width
    for b in range(edge_blocks_ref.shape[0]):
        send_ref[b * (per_peer + 1) + per_peer] = edge_blocks_ref[b]
    for p in range(requests):
        line = slice(p, p + 1)
        written = head_rows(removal[line, :], heads, head_width, 0) + head_rows(key_mod[line, :], heads, head_width, heads)
        change = dot(change_ref[p], written.astype(BF16))
        after = state_ref[p].astype(F32) * forget[line, :] + change
        after_ref[p] = after.astype(BF16)
        kept_ref[p] = after * last_ref[line, :] + added_ref[p].astype(F32)
    index_copy.wait()
    for p in range(requests):
        parts = []
        for pair in range(heads // 2):
            lanes = slice(pair * 128, (pair + 1) * 128)
            through = through_ref[p, :, lanes]
            zero = jnp.zeros_like(through)
            through = jnp.concatenate([jnp.where(own, through, zero), jnp.where(own, zero, through)], axis=0)
            parts.append(dot(after_ref[p, :, lanes], through))
        kept = kept_ref[p] + jnp.concatenate(parts, axis=1)
        kept = jnp.where(index_ref[3, p] > 0, kept, state_ref[p].astype(F32))
        for c in range(halves):
            for pair in range(heads // 2):
                top = kept[(2 * c) * pack : (2 * c + 1) * pack, pair * 128 : (pair + 1) * 128]
                bottom = kept[(2 * c + 1) * pack : (2 * c + 2) * pack, pair * 128 : (pair + 1) * 128]
                at = (p * heads + 2 * pair) * halves + c
                even = jnp.where(low, top, pltpu.roll(bottom, head_width, 1))
                odd = jnp.where(low, pltpu.roll(top, head_width, 1), bottom)
                send_ref[index_ref[4, at]] = even.astype(BF16)
                send_ref[index_ref[4, at + halves]] = odd.astype(BF16)


def lines_kernel(gating_ref, *refs):
    *outs, scratch = refs
    requests, part = gating_ref.shape[:2]
    width = scratch.shape[1]
    me = lax.axis_index("head")
    for d, out in enumerate(outs):
        start = pl.multiple_of((me ^ d) * width, 128)
        for p in range(requests):
            scratch[p * part : (p + 1) * part, :] = gating_ref[p, :, pl.ds(start, width)].astype(F32)
        out[...] = scratch[...].astype(BF16)


def read_kernel(
    requests, heads, groups,
    *refs,
):
    return read_body(requests, heads, refs[:groups], *refs[groups:])


def read_body(
    requests, heads,
    recept_refs, scale_ref, key_mod_ref, key_mod_first_ref, a_ref, k_ref, b_ref, solve_ref, state_ref, value_t_ref,
    vector_ref, value_ref,
    result_ref, line_scratch, low_scratch, cross, compact, out_scratch,
):
    rows, width = value_ref.shape
    steps = rows // requests
    head_width = width // heads
    lanes = heads * steps
    part = steps // len(recept_refs)
    row = lax.broadcasted_iota(I32, (rows, rows), 0)
    source = (row % steps // part) ^ lax.axis_index("head")
    source_row = source * (requests * part) + row // steps * part + row % part
    order = (source_row == lax.broadcasted_iota(I32, (rows, rows), 1)).astype(F32).astype(BF16)
    recept = dot(order, jnp.concatenate([ref[...] for ref in recept_refs], axis=0))
    key_mod_first = jnp.broadcast_to(key_mod_first_ref[...][:, None, :], (requests, steps, width)).reshape(rows, width)
    first = lax.broadcasted_iota(I32, (rows, width), 0) % steps == 0
    key_mod = jnp.where(first, key_mod_first, key_mod_ref[...].astype(F32))
    bonus = group_sum(recept * key_mod * vector_ref[6:7, :], head_width)
    line_scratch[...], line_low = split(recept * scale_ref[...])
    low_scratch[...] = line_low
    for p in range(requests):
        cut = slice(p * steps, (p + 1) * steps)
        right = jnp.concatenate([expand(k_ref[cut, :], head_width), expand(b_ref[cut, :], head_width)], axis=0)
        both_parts = dot(jnp.concatenate([line_scratch[cut, :], low_scratch[cut, :]], axis=0), right, NT)
        cross[p] = both_parts[:steps, :] + both_parts[steps:, :]
    lane = lax.broadcasted_iota(I32, (requests, lanes), 1)
    source = lane % steps
    group = lane - source
    for t in range(steps):
        weights = jnp.where(source <= t, cross[:, t, lanes:], 0.0)
        from_a = jnp.zeros((requests, lanes), F32)
        from_v = jnp.where(source <= t, cross[:, t, :lanes], 0.0)
        for s in range(t + 1):
            weight = jnp.take_along_axis(weights, group + s, axis=1)
            from_a = from_a - weight * solve_ref[0, s]
            from_v = from_v - weight * solve_ref[1, s]
        compact[0, :, t, :] = from_a
        compact[1, :, t, :] = from_v
    out_low = lax.broadcasted_iota(I32, (steps, 128), 1) < head_width
    for p in range(requests):
        cut = slice(p * steps, (p + 1) * steps)
        read = jnp.concatenate(
            [spread(compact[0, p].astype(BF16), steps), spread(compact[1, p].astype(BF16), steps)], axis=1
        )
        state = state_ref[p]
        along = dot(state, expand(a_ref[cut, :], head_width), NT).astype(BF16)
        both = jnp.concatenate([along, value_t_ref[p]], axis=1)
        out = dot(read, jnp.concatenate([both, both], axis=0), NT)
        out = out + dot(expand(line_scratch[cut, :], head_width), jnp.concatenate([state, state], axis=0), NT)
        out = out + dot(expand(low_scratch[cut, :], head_width), jnp.concatenate([state, state], axis=0), NT)
        for pair in range(heads // 2):
            at = 2 * pair * steps
            out_scratch[cut, pair * 128 : (pair + 1) * 128] = jnp.where(
                out_low, out[at : at + steps, :], out[at + steps : at + 2 * steps, :]
            )
    out = out_scratch[...]
    centered = out - group_sum(out, head_width) * (1.0 / head_width)
    variance = group_sum(centered * centered, head_width) * (1.0 / head_width)
    line = centered * lax.rsqrt(variance + NORM_EPSILON) * vector_ref[7:8, :] + vector_ref[8:9, :]
    result_ref[...] = (line + bonus * value_ref[...].astype(F32)).astype(BF16)


def place_kernel(per_peer, pick_ref, back_ref, out_ref, edge_ref, scratch, flat, edge_scratch):
    slot_dev = out_ref.shape[0]
    pack = back_ref.shape[1]
    for b in range(slot_dev // per_peer):
        at = b * (per_peer + 1)
        scratch[b * per_peer : (b + 1) * per_peer] = back_ref[at : at + per_peer].astype(F32)
        edge_scratch[b * per_peer : (b + 1) * per_peer, :] = back_ref[at + per_peer].astype(F32)[:per_peer, :]
    left = lax.broadcasted_iota(I32, (8, 128), 1) < 64
    half = pack // 2
    for row in range(0, slot_dev, 8):
        for j in range(0, pack, 8):
            tiles = jnp.swapaxes(scratch[row : row + 8, j : j + 8, :], 0, 1)
            for i in range(4):
                even, odd = tiles[2 * i], tiles[2 * i + 1]
                b = j // 2 + i
                flat[row : row + 8, b * 128 : (b + 1) * 128] = jnp.where(left, even, pltpu.roll(odd, 64, 1))
                flat[row : row + 8, (half + b) * 128 : (half + b + 1) * 128] = jnp.where(left, pltpu.roll(even, 64, 1), odd)
    pick = pick_ref[...]
    for start in range(0, pack * 128, 256):
        out_ref[:, start : start + 256] = dot(pick, flat[:, start : start + 256].astype(BF16))
    edge_ref[...] = jnp.transpose(dot(pick, edge_scratch[...].astype(BF16)))[: edge_ref.shape[0], :]


def local(
    layer_entry_vectors,
    guessed_lookup_vectors,
    guessed_content_vectors,
    gating_query,
    lane_memory_store,
    prior_step_store,
    fading_blend_ratio,
    learning_speed_blend,
    fading_left_factor,
    fading_right_factor,
    fading_offset,
    learning_speed_left,
    learning_speed_right,
    learning_speed_offset,
    erasing_lookup_factor,
    written_lookup_factor,
    present_reward_factors,
    lane_standard_factor,
    lane_standard_offset,
    caller_memory_directory,
    kept_target_place,
    caller_sequence,
    approved_guesses,
):
    blocks = lax.axis_size("blk")
    groups = lax.axis_size("head")
    requests, steps, width = layer_entry_vectors.shape
    heads, halves = caller_memory_directory.shape[1:]
    slot_dev = lane_memory_store.shape[1]
    slot_width = lane_memory_store.shape[2]
    pack = slot_width // 128
    per_peer = slot_dev // blocks
    edge_rows = prior_step_store.shape[2]
    rows = requests * steps
    rank = fading_left_factor.shape[1]
    sds = jax.ShapeDtypeStruct

    def exchange(x, axis):
        return lax.all_to_all(
            x, axis, split_axis=0, concat_axis=0, tiled=True, axis_index_groups=[list(order_of(blocks))]
        )

    read_table = caller_memory_directory.transpose(1, 2, 0)
    write_table = kept_target_place.transpose(1, 2, 0)
    pieces = 1
    (sent,) = call(
        functools.partial(send_kernel, blocks, requests, per_peer, pieces),
        (pltpu.HBM((blocks * (per_peer + 1), pack, 128), BF16),),
        raw=(caller_sequence, read_table, lane_memory_store[0], prior_step_store[0].T),
        raw_outs=(0,),
        scratch=[
            pltpu.SMEM(caller_sequence.shape, I32),
            pltpu.VMEM(read_table.shape, I32),
            pltpu.VMEM((slot_dev, slot_width), F32),
            pltpu.VMEM((edge_rows, slot_dev), F32),
            pltpu.VMEM((slot_dev, slot_width), F32),
            pltpu.VMEM((slot_dev, slot_dev), F32),
            pltpu.VMEM((blocks * (per_peer + 1), pack, 128), BF16),
            pltpu.SemaphoreType.DMA((3,)),
            pltpu.SemaphoreType.DMA((2 * pieces,)),
            pltpu.SemaphoreType.DMA((8,)),
        ],
    )
    got = exchange(sent.reshape(blocks, (per_peer + 1) * pack, 128), "blk")
    got = got.reshape(blocks * (per_peer + 1), pack, 128)
    layer = layer_entry_vectors.reshape(rows, width)
    key = guessed_lookup_vectors.reshape(rows, width)
    value = guessed_content_vectors.reshape(rows, width)
    vectors = (
        fading_blend_ratio, learning_speed_blend, fading_offset, learning_speed_offset, erasing_lookup_factor,
        written_lookup_factor, present_reward_factors, lane_standard_factor, lane_standard_offset,
    )
    arrays = (fading_left_factor.T, learning_speed_left.T, fading_right_factor, learning_speed_right)
    one = sds((requests, width), F32)
    wide = sds((rows, width), BF16)
    left = sds((rank, width), BF16)
    (
        partial_sums, first_lines, picked, vector, left_decay, left_rate, right_decay, right_rate,
    ) = call(
        functools.partial(shift_kernel, requests, len(vectors)),
        (sds((rows, 2 * rank), BF16), one, one, sds((16, width), F32), left, left, left, left),
        raw=(caller_sequence, approved_guesses, *(x.reshape(1, width) for x in vectors), layer, *arrays),
        scratch=[
            pltpu.SMEM(caller_sequence.shape, I32),
            pltpu.SMEM(approved_guesses.shape, I32),
            pltpu.VMEM((rows, width), BF16),
            pltpu.VMEM((rows, width), F32),
            pltpu.SemaphoreType.DMA((3,)),
            pltpu.SemaphoreType.DMA((len(vectors),)),
            pltpu.SemaphoreType.DMA((len(arrays),)),
        ],
    )

    def from_group(x):
        return [x] + [lax.ppermute(x, "head", [(g, g ^ d) for g in range(groups)]) for d in range(1, groups)]

    parts = from_group(partial_sums)
    head_width = width // heads
    square = sds((slot_dev, slot_dev), BF16)
    index, pick_in, pick_out, key_near, unit, value_t, unit_first, key_first, value_first = call(
        functools.partial(index_kernel, blocks, requests, per_peer, heads),
        (
            sds((8, slot_dev), I32), square, square, wide, sds((rows, width), F32),
            sds((requests, head_width, heads * steps), BF16),
            one, one, one,
        ),
        near=(vector,),
        raw=(caller_sequence, approved_guesses, read_table, write_table, key, value),
        held=(first_lines, picked, left_decay, left_rate, right_decay, right_rate),
        scratch=[
            pltpu.SMEM(caller_sequence.shape, I32),
            pltpu.SMEM(approved_guesses.shape, I32),
            pltpu.VMEM(read_table.shape, I32),
            pltpu.VMEM(write_table.shape, I32),
            pltpu.VMEM((rows, width), BF16),
            pltpu.VMEM((heads * halves, write_table.shape[2]), I32),
            pltpu.SemaphoreType.DMA((6,)),
        ],
    )
    a_lines, k_lines, b_lines, scale, key_mod, last, solve, through, added = call(
        functools.partial(prepare_kernel, requests, heads, groups),
        (
            wide, wide, wide, sds((rows, width), F32), wide, one,
            sds((2, steps, requests, heads * steps), F32),
            sds((requests, head_width, width), BF16),
            sds((requests, head_width, width), BF16),
        ),
        near=(*parts, vector, right_decay, right_rate, key_near, unit, value_t),
        loose=(index,),
        held=(pick_in, pick_out, first_lines, picked, left_decay, left_rate, unit_first, key_first, value_first),
        scratch=[
            pltpu.VMEM((requests, steps, 2 * heads * steps), F32),
            pltpu.VMEM((2, requests, steps, heads * steps), F32),
            pltpu.VMEM((rows, width), F32),
            pltpu.VMEM((rows, width), BF16),
            pltpu.VMEM((rows, width), BF16),
            pltpu.VMEM((requests, head_width, heads * steps), BF16),
            pltpu.VMEM((requests, 2 * head_width, 2 * heads * steps), BF16),
            pltpu.VMEM((requests, 2 * head_width, 2 * heads * steps), BF16),
            pltpu.SMEM((8, slot_dev), I32),
            pltpu.SemaphoreType.DMA,
        ],
    )
    read_later = (scale, key_mod, a_lines, k_lines, b_lines, solve, value_t, pick_out)
    state_later = (vector, right_decay, right_rate, key_first, last, through, added)
    first_sums, edge = call(
        functools.partial(first_kernel, requests, heads, halves, per_peer),
        (sds((requests, 2 * rank), F32), one),
        near=(pick_in, got, first_lines, vector, left_decay, left_rate),
        held=(index, unit_first, value_first, picked, *state_later[1:], *read_later),
        scratch=[pltpu.VMEM((slot_dev, 128), F32), pltpu.VMEM((slot_dev, 128), F32)],
    )
    first_parts = from_group(first_sums)
    state, change, edge_blocks = call(
        functools.partial(layout_kernel, requests, heads, halves, per_peer),
        (
            sds((requests, head_width, width), BF16),
            sds((requests, head_width, 2 * heads), BF16),
            sds((blocks, pack, 128), BF16),
        ),
        near=(got, unit_first, value_first, edge, picked),
        loose=(index,),
        held=(*state_later, *read_later),
        scratch=[
            pltpu.VMEM((slot_dev, 128), F32),
            pltpu.VMEM((requests, head_width, 2 * heads), F32),
            pltpu.SMEM((8, slot_dev), I32),
            pltpu.SemaphoreType.DMA,
        ],
    )
    back, after, key_mod_first = call(
        functools.partial(state_kernel, requests, heads, halves, per_peer, groups),
        (
            pltpu.HBM((blocks * (per_peer + 1), pack, 128), BF16),
            sds((requests, head_width, width), BF16),
            one,
        ),
        near=(
            *first_parts, state, change, edge_blocks, unit_first, key_first, last, through, added,
            vector, right_decay, right_rate,
        ),
        loose=(index,),
        held=read_later,
        scratch=[
            pltpu.VMEM((requests, head_width, width), F32),
            pltpu.SMEM((8, slot_dev), I32),
            pltpu.SemaphoreType.DMA,
        ],
    )
    back = exchange(back.reshape(blocks, (per_peer + 1) * pack, 128), "blk")
    back = back.reshape(blocks * (per_peer + 1), pack, 128)
    recept = call(
        lines_kernel,
        (sds((rows // groups, width), BF16),) * groups,
        far=(gating_query,),
        held=(vector, after, key_mod_first, *read_later),
        scratch=[pltpu.VMEM((rows // groups, width), F32)],
    )
    recept = [recept[0]] + [
        lax.ppermute(recept[d], "head", [(g, g ^ d) for g in range(groups)]) for d in range(1, groups)
    ]
    (result,) = call(
        functools.partial(read_kernel, requests, heads, groups),
        (pltpu.HBM((rows, width), BF16),),
        near=(*recept, scale, key_mod, key_mod_first, a_lines, k_lines, b_lines, solve, after, value_t, vector),
        far=(value,),
        held=(pick_out,),
        scratch=[
            pltpu.VMEM((rows, width), BF16),
            pltpu.VMEM((rows, width), BF16),
            pltpu.VMEM((requests, steps, 2 * heads * steps), F32),
            pltpu.VMEM((2, requests, steps, heads * steps), F32),
            pltpu.VMEM((rows, width), F32),
        ],
    )
    new_states, new_edges = call(
        functools.partial(place_kernel, per_peer),
        (pltpu.HBM((slot_dev, slot_width), F32), pltpu.HBM((edge_rows, slot_dev), F32)),
        near=(pick_out, back),
        scratch=[
            pltpu.VMEM((slot_dev, pack, 128), F32),
            pltpu.VMEM((slot_dev, slot_width), F32),
            pltpu.VMEM((slot_dev, 128), F32),
        ],
    )
    return (result.reshape(requests, steps, width), new_states[None], new_edges.T[None])


def solution(mesh):
    return jax.shard_map(
        local,
        mesh=mesh,
        in_specs=(
            P("blk", None, "head"),
            P("blk", None, "head"),
            P("blk", None, "head"),
            P("blk", "head", None),
            P("head", "blk", None),
            P("head", "blk", None),
            P("head"),
            P("head"),
            P("head", None),
            P(None, "head"),
            P("head"),
            P("head", None),
            P(None, "head"),
            P("head"),
            P("head"),
            P("head"),
            P("head"),
            P("head"),
            P("head"),
            P(None, "head", None),
            P(None, "head", None),
            P(),
            P(),
        ),
        out_specs=(P("blk", None, "head"), P("head", "blk", None), P("head", "blk", None)),
        check_vma=False,
    )
```
